32 devices in a mesh: view: 2 (over y), dp: 16 (over z, x, core).
Axes of the slice: x: 2, y: 2, z: 4, core: 2. Of those that a mesh axis runs over, the one named last changes fastest.
Arguments:
- inputs: bfloat16 [2, 64, 14, 14, 1024], P('view', 'dp'), may hold values from -6 to 6
- resolution: int32 [2, 64], P('view', 'dp'), may hold values from 160 to 224, as said below
- reduce_a: bfloat16 [1024, 256], replicated, may hold values from -0.1875 to 0.1875
- spatial_a: bfloat16 [3, 3, 256, 256], replicated, may hold values from -0.125 to 0.125
- expand_a: bfloat16 [256, 1024], replicated, may hold values from -0.375 to 0.375
- reduce_b: bfloat16 [1024, 512], replicated, may hold values from -0.1875 to 0.1875
- spatial_b: bfloat16 [3, 3, 512, 512], replicated, may hold values from -0.09375 to 0.09375
- expand_b: bfloat16 [512, 2048], replicated, may hold values from -0.25 to 0.25
- shortcut_b: bfloat16 [1024, 2048], replicated, may hold values from -0.1875 to 0.1875
- scale_reduce_a: float32 [256], replicated, may hold values from 0.5 to 1.5
- shift_reduce_a: float32 [256], replicated, may hold values from -3 to 3
- scale_spatial_a: float32 [256], replicated, may hold values from 0.5 to 1.5
- shift_spatial_a: float32 [256], replicated, may hold values from -3 to 3
- scale_expand_a: float32 [1024], replicated, may hold values from 0.5 to 1.5
- shift_expand_a: float32 [1024], replicated, may hold values from -3 to 3
- scale_reduce_b: float32 [512], replicated, may hold values from 0.5 to 1.5
- shift_reduce_b: float32 [512], replicated, may hold values from -3 to 3
- scale_spatial_b: float32 [512], replicated, may hold values from 0.5 to 1.5
- shift_spatial_b: float32 [512], replicated, may hold values from -3 to 3
- scale_expand_b: float32 [2048], replicated, may hold values from 0.5 to 1.5
- shift_expand_b: float32 [2048], replicated, may hold values from -3 to 3
- scale_shortcut: float32 [2048], replicated, may hold values from 0.5 to 1.5
- shift_shortcut: float32 [2048], replicated, may hold values from -3 to 3
Outputs:
- loss: float32 [2, 64], P('view', 'dp')
- block_a: bfloat16 [2, 64, 14, 14, 1024], P('view', 'dp')
- block_b: bfloat16 [2, 64, 7, 7, 2048], P('view', 'dp')
- input_grad: bfloat16 [2, 64, 14, 14, 1024], P('view', 'dp')
- grads_a: float32 [1117184], P(('view', 'dp'))
- grads_b: float32 [6039552], P(('view', 'dp'))
The draws below stay inside these ranges and needn't reach their ends.
Inputs may be any that keep to these rules, and one draw needn't show every extreme that they name: Each view of each image has resolution 160 or 224; both values occur in every draw.
All inputs are finite; a program needn't handle non-finite values.
Results may differ from the reference program's by a relative error of at most 0.018.
Values sent between devices are 32-bit elements; how exact they have to be, the bound alone decides.
No kernel may reach another device: no remote copies, remote signals or barrier semaphores. Data moves between devices by JAX's collectives and lax.ppermute only.
A program may use at most 192 MiB of HBM per device.

```python
import jax
import jax.numpy as jnp
from jax import lax

C3 = 1024
M3 = 256
M4 = 512
C4 = 2048
H3 = 14
H4 = 7
IMAGES = 64


def draw_resolution(key, part):
    key = jax.random.fold_in(key, 7)
    coin_key, place_key = jax.random.split(key)
    coins = jax.random.randint(coin_key, (2, IMAGES), 0, 2)
    place = jax.random.randint(place_key, (), 0, IMAGES)
    coins = coins.at[:, place].set(1)
    coins = coins.at[:, (place + 1) % IMAGES].set(0)
    return (160 + 64 * coins).astype(jnp.int32)


def levels(own_key, extent, pieces, smallest, top_value):
    def one(dim, blocks):
        steps = jax.random.uniform(jax.random.fold_in(jax.random.fold_in(own_key, 6), dim), (blocks,), jnp.float32, smallest / len(pieces), top_value / len(pieces))
        return jnp.repeat(jnp.exp(steps), extent[dim] // blocks).reshape((-1,) + (1,) * (len(extent) - dim - 1))

    factor_of = one(*pieces[0])
    for cut in pieces[1:]:
        factor_of = factor_of * one(*cut)
    return factor_of


def normal_values(key, extent, deviation, limit, pieces=(), kind=jnp.bfloat16):
    loudness = levels(key, extent, pieces, -0.22, 0.18) if pieces else 1.0
    entries = jax.random.normal(key, extent, jnp.float32) * deviation * loudness
    return jnp.minimum(jnp.maximum(entries, -limit), limit).astype(kind)


def setup_inputs(seed: int = 0) -> dict:
    streams_of = jax.random.split(jax.random.key(seed), 24)
    return {
        "inputs": normal_values(streams_of[0], (2, IMAGES, H3, H3, C3), 1.0, 6.0, ((0, 2), (1, 16))),
        "resolution": draw_resolution(jax.random.fold_in(streams_of[23], 71), 0),
        "reduce_a": normal_values(streams_of[2], (C3, M3), C3 ** -0.5, 0.1875),
        "spatial_a": normal_values(streams_of[3], (3, 3, M3, M3), (9 * M3) ** -0.5, 0.125),
        "expand_a": normal_values(streams_of[4], (M3, C3), M3 ** -0.5, 0.375),
        "reduce_b": normal_values(streams_of[5], (C3, M4), C3 ** -0.5, 0.1875),
        "spatial_b": normal_values(streams_of[6], (3, 3, M4, M4), (9 * M4) ** -0.5, 0.09375),
        "expand_b": normal_values(streams_of[7], (M4, C4), M4 ** -0.5, 0.25),
        "shortcut_b": normal_values(streams_of[8], (C3, C4), C3 ** -0.5, 0.1875),
        "scale_reduce_a": jnp.clip(1.0 + 0.1 * jax.random.normal(streams_of[9], (M3,), jnp.float32), 0.5, 1.5),
        "shift_reduce_a": normal_values(streams_of[10], (M3,), 0.3, 3.0, (), jnp.float32),
        "scale_spatial_a": jnp.clip(1.0 + 0.1 * jax.random.normal(streams_of[11], (M3,), jnp.float32), 0.5, 1.5),
        "shift_spatial_a": normal_values(streams_of[12], (M3,), 0.3, 3.0, (), jnp.float32),
        "scale_expand_a": jnp.clip(1.0 + 0.1 * jax.random.normal(streams_of[13], (C3,), jnp.float32), 0.5, 1.5),
        "shift_expand_a": normal_values(streams_of[14], (C3,), 0.3, 3.0, (), jnp.float32),
        "scale_reduce_b": jnp.clip(1.0 + 0.1 * jax.random.normal(streams_of[15], (M4,), jnp.float32), 0.5, 1.5),
        "shift_reduce_b": normal_values(streams_of[16], (M4,), 0.3, 3.0, (), jnp.float32),
        "scale_spatial_b": jnp.clip(1.0 + 0.1 * jax.random.normal(streams_of[17], (M4,), jnp.float32), 0.5, 1.5),
        "shift_spatial_b": normal_values(streams_of[18], (M4,), 0.3, 3.0, (), jnp.float32),
        "scale_expand_b": jnp.clip(1.0 + 0.1 * jax.random.normal(streams_of[19], (C4,), jnp.float32), 0.5, 1.5),
        "shift_expand_b": normal_values(streams_of[20], (C4,), 0.3, 3.0, (), jnp.float32),
        "scale_shortcut": jnp.clip(1.0 + 0.1 * jax.random.normal(streams_of[21], (C4,), jnp.float32), 0.5, 1.5),
        "shift_shortcut": normal_values(streams_of[22], (C4,), 0.3, 3.0, (), jnp.float32),
    }


@jax.custom_vjp
def low(v):
    return lax.optimization_barrier(v.astype(jnp.bfloat16)).astype(jnp.float32)

@jax.custom_vjp
def low_back(v):
    return v

def low_keep(v):
    return (low(v), None)

def low_pass(kept, grad):
    return (grad,)

def back_keep(v):
    return (v, None)

def back_low(kept, grad):
    return (low(grad),)
low.defvjp(low_keep, low_pass)
low_back.defvjp(back_keep, back_low)
eps_norm = 1e-05
eps_cos = 1e-06
loss_scale = 65536.0

def build_masks(resolution, height, divisor):
    bounds = resolution // divisor
    places = jnp.arange(height, dtype=jnp.int32)
    inside = (places[:, None] < bounds[..., None, None]) & (places[None, :] < bounds[..., None, None])
    return inside.astype(jnp.float32)[..., None]

def smooth(tensor):
    return jax.nn.gelu(tensor, approximate=False)

def pointwise(tensor, weight):
    return jnp.einsum('vnhwc,cd->vnhwd', tensor, weight, precision=lax.Precision.HIGHEST)

def spatial(tensor, weight, stride):
    dims_in = tensor.shape
    merged = tensor.reshape((dims_in[0] * dims_in[1],) + dims_in[2:])
    result = lax.conv_general_dilated(merged, weight, (stride, stride), ((1, 1), (1, 1)), dimension_numbers=('NHWC', 'HWIO', 'NHWC'), precision=lax.Precision.HIGHEST)
    return result.reshape(dims_in[:2] + result.shape[1:])

def normalize(tensor, keep_mask, total_count, factor, offset):
    center = lax.optimization_barrier(jnp.sum(tensor * keep_mask, axis=(1, 2, 3), keepdims=True)) / total_count
    second = lax.optimization_barrier(jnp.sum(tensor * tensor * keep_mask, axis=(1, 2, 3), keepdims=True)) / total_count
    inverse = lax.rsqrt(second - center * center + eps_norm)
    return factor * ((tensor - center) * inverse) + offset

def forward(start, weights, norms, mask_big, mask_small, count_big, count_small, pixels):
    reduce_a, spatial_a, expand_a, reduce_b, spatial_b, expand_b, shortcut_b = weights
    reduced_a = low_back(pointwise(start, reduce_a))
    hidden_one_a = low(smooth(normalize(reduced_a, mask_big, count_big, norms[0], norms[1])) * mask_big)
    mixed_a = low_back(spatial(hidden_one_a, spatial_a, 1))
    hidden_two_a = low(smooth(normalize(mixed_a, mask_big, count_big, norms[2], norms[3])) * mask_big)
    expanded_a = low_back(pointwise(hidden_two_a, expand_a))
    block_a = low(smooth(normalize(expanded_a, mask_big, count_big, norms[4], norms[5]) + start) * mask_big)
    reduced_b = low_back(pointwise(block_a, reduce_b))
    side_b = low_back(pointwise(block_a[:, :, ::2, ::2, :], shortcut_b))
    hidden_one_b = low(smooth(normalize(reduced_b, mask_big, count_big, norms[6], norms[7])) * mask_big)
    mixed_b = low_back(spatial(hidden_one_b, spatial_b, 2))
    hidden_two_b = low(smooth(normalize(mixed_b, mask_small, count_small, norms[8], norms[9])) * mask_small)
    expanded_b = low_back(pointwise(hidden_two_b, expand_b))
    joined_b = normalize(expanded_b, mask_small, count_small, norms[10], norms[11])
    joined_b = joined_b + normalize(side_b, mask_small, count_small, norms[12], norms[13])
    out_b = smooth(joined_b) * mask_small
    pooled = lax.optimization_barrier(jnp.sum(out_b, axis=(2, 3))) / pixels[..., None]
    return (block_a, out_b, pooled)

def pack_flat(parts):
    return jnp.concatenate([part_item.reshape(-1) for part_item in parts])

def reference(inputs, resolution, reduce_a, spatial_a, expand_a, reduce_b, spatial_b, expand_b, shortcut_b, scale_reduce_a, shift_reduce_a, scale_spatial_a, shift_spatial_a, scale_expand_a, shift_expand_a, scale_reduce_b, shift_reduce_b, scale_spatial_b, shift_spatial_b, scale_expand_b, shift_expand_b, scale_shortcut, shift_shortcut):
    mask_big = build_masks(resolution, H3, 16)
    mask_small = build_masks(resolution, H4, 32)
    count_big = lax.optimization_barrier(jnp.sum(mask_big, axis=(1, 2, 3, 4), keepdims=True))
    count_small = lax.optimization_barrier(jnp.sum(mask_small, axis=(1, 2, 3, 4), keepdims=True))
    pixels = (resolution // 32 * (resolution // 32)).astype(jnp.float32)
    start = inputs.astype(jnp.float32) * mask_big
    weights = tuple((matrix.astype(jnp.float32) for matrix in (reduce_a, spatial_a, expand_a, reduce_b, spatial_b, expand_b, shortcut_b)))
    norms = (scale_reduce_a, shift_reduce_a, scale_spatial_a, shift_spatial_a, scale_expand_a, shift_expand_a, scale_reduce_b, shift_reduce_b, scale_spatial_b, shift_spatial_b, scale_expand_b, shift_expand_b, scale_shortcut, shift_shortcut)
    targets = forward(start, weights, norms, mask_big, mask_small, count_big, count_small, pixels)[2]
    partner = targets[::-1]
    unit_other = partner * lax.rsqrt(lax.optimization_barrier(jnp.sum(partner * partner, axis=2, keepdims=True)) + eps_cos)

    def objective(start_in, weight_in, norm_in):
        block_a, out_b, pooled = forward(start_in, weight_in, norm_in, mask_big, mask_small, count_big, count_small, pixels)
        unit_own = pooled * lax.rsqrt(lax.optimization_barrier(jnp.sum(pooled * pooled, axis=2, keepdims=True)) + eps_cos)
        cosine = lax.optimization_barrier(jnp.sum(unit_own * unit_other, axis=2))
        return (-0.5 * loss_scale * jnp.sum(cosine), (block_a, out_b, cosine))
    scaled, pullback, extras = jax.vjp(objective, start, weights, norms, has_aux=True)
    grad_start, grad_weights, grad_norms = pullback(jnp.ones_like(scaled))
    block_a, out_b, cosine = extras
    loss = -0.5 * cosine
    input_grad = (grad_start * mask_big).astype(jnp.bfloat16)
    grads_a = pack_flat([grad_weights[0], grad_weights[1], grad_weights[2], grad_norms[1], grad_norms[0], grad_norms[3], grad_norms[2], grad_norms[5], grad_norms[4]])
    grads_b = pack_flat([grad_weights[3], grad_weights[4], grad_weights[5], grad_weights[6], grad_norms[7], grad_norms[6], grad_norms[9], grad_norms[8], grad_norms[11], grad_norms[10], grad_norms[13], grad_norms[12]])
    return (loss, block_a.astype(jnp.bfloat16), out_b.astype(jnp.bfloat16), input_grad, grads_a, grads_b)
```

```python
import functools

import jax
import jax.numpy as jnp
from jax import lax
from jax.experimental import pallas as pl
from jax.experimental.pallas import tpu as pltpu
from jax.sharding import PartitionSpec as P

eps_norm = 1e-05
eps_cos = 1e-06
loss_scale = 65536.0
low_type = jnp.bfloat16
full_type = jnp.float32
vmem_bytes = 40 * 1024 * 1024

even_width = 8


def call(body, outs, args, cost_us=2, scratch=()):
    whole = pl.BlockSpec(memory_space=pltpu.VMEM)
    sizes = [len(item) if isinstance(item, tuple) else None for item in args]
    flat = [one for item in args for one in (item if isinstance(item, tuple) else (item,))]

    def run(*refs):
        rest = iter(refs)
        given = [next(rest) if size is None else tuple(next(rest) for _ in range(size)) for size in sizes]
        body(*given, *rest)

    return pl.pallas_call(
        run,
        out_shape=outs,
        in_specs=[whole] * len(flat),
        out_specs=[whole] * len(outs),
        scratch_shapes=[pltpu.VMEM(dims, kind) for dims, kind in scratch],
        compiler_params=pltpu.CompilerParams(vmem_limit_bytes=vmem_bytes),
        cost_estimate=pl.CostEstimate(flops=int(cost_us * 1e9), bytes_accessed=int(cost_us * 1e6), transcendentals=0),
    )(*flat)


def shaped(*dims, kind=full_type):
    return jax.ShapeDtypeStruct(dims, kind)


def tail_parts(pre):
    size = jnp.abs(pre)
    base = 1.0 + (0.3275911 * 0.7071067811865476) * size
    guess = pl.reciprocal(base, approx=True)
    guess = guess * (2.0 - base * guess)
    guess = guess * (2.0 - base * guess)
    bell = jnp.exp(-0.5 * (pre * pre))
    series = 0.5 * 1.061405429
    for term in (-1.453152027, 1.421413741, -0.284496736, 0.254829592):
        series = series * guess + 0.5 * term
    return size, bell, series * guess * bell


def smooth(pre):
    size, _, tail = tail_parts(pre)
    return jnp.maximum(pre, 0.0) - size * tail


def smooth_slope(pre):
    _, bell, tail = tail_parts(pre)
    return jnp.where(pre >= 0.0, 1.0 - tail, tail) + 0.3989422804014327 * (pre * bell)


def wide(mask, width):
    return jnp.concatenate([mask] * (width // mask.shape[1]), axis=1)


def fold(value):
    rows, width = value.shape
    return jnp.sum(value.reshape(rows // 8, 8, width), axis=0)


def column_sum(value):
    return jnp.sum(value, axis=0, keepdims=True)


def total(parts):
    result = parts[0][...]
    for part in parts[1:]:
        result = result + part[...]
    return result


def statistics(sums, count):
    center = sums[0:1] / count
    inverse = lax.rsqrt(sums[1:2] / count - center * center + eps_norm)
    return center, inverse


def add_rows(store, row, value):
    store[row * 8 : row * 8 + 8, :] += fold(value)


def finish_rows(store, out_ref, rows):
    for row in range(rows):
        out_ref[row : row + 1, :] = column_sum(store[row * 8 : row * 8 + 8, :])


def times(lhs, rhs):
    return lax.dot_general(lhs, rhs, (((1,), (0,)), ((), ())), preferred_element_type=full_type)


def times_back(lhs, rhs):
    return lax.dot_general(lhs, rhs, (((1,), (1,)), ((), ())), preferred_element_type=full_type)


def times_rows(lhs, rhs):
    return lax.dot_general(lhs, rhs, (((0,), (0,)), ((), ())), preferred_element_type=full_type)


def low(value):
    return value.astype(low_type)


def enter_body(images, x_ref, mask_ref, filter_ref, start_ref, out_ref, sums_ref, store):
    height, pairs = x_ref.shape[0], x_ref.shape[1]
    depth = x_ref.shape[4]
    line = even_width * images
    blank = jnp.zeros((even_width - pairs, images, depth), low_type)
    store[...] = jnp.zeros_like(store)

    def step(index, carry):
        rows = pl.ds(pl.multiple_of(index * 4 * line, 4 * line), 4 * line)
        parts = []
        for row in range(2):
            for side in range(2):
                cells = jnp.concatenate([x_ref[index * 2 + row, :, side], blank], axis=0)
                parts.append(cells.reshape(line, depth))
        value = jnp.concatenate(parts, axis=0).astype(full_type) * wide(mask_ref[rows, :], depth)
        value = low(value)
        start_ref[rows, :] = value
        result = times(value, filter_ref[...])
        out_ref[rows, :] = result
        add_rows(store, 0, result)
        add_rows(store, 1, result * result)
        return carry

    lax.fori_loop(0, height // 2, step, 0)
    finish_rows(store, sums_ref, 2)


def split_store(even_ref, moved_ref, place, value, line):
    even, odd = value[:line], value[line:]
    even_ref[place, 0] = low(even)
    even_ref[place, 1] = low(odd)
    moved_ref[place, 0] = low(pltpu.roll(even, line - line // even_width, 0))
    moved_ref[place, 1] = low(pltpu.roll(odd, line // even_width, 0))


def blank_border(*refs):
    for ref in refs:
        empty = jnp.zeros(ref.shape[1:], ref.dtype)
        ref[0] = empty
        ref[ref.shape[0] - 1] = empty


def tap_sources(even_ref, moved_ref):
    return (
        ((moved_ref, 1), (even_ref, 0), (even_ref, 1)),
        ((even_ref, 0), (even_ref, 1), (moved_ref, 0)),
    )


def block_body(images, parts, u_ref, count_ref, scale_ref, shift_ref, mask_ref, filter_ref, even_ref, moved_ref, out_ref, sums_ref, store):
    depth = filter_ref.shape[1]
    line = even_width * images
    height = even_ref.shape[0] - 2
    center, inverse = statistics(total(parts), count_ref[0:1, 0:1])
    factor = scale_ref[...] * inverse
    shift = shift_ref[...]
    blank_border(even_ref, moved_ref)
    store[...] = jnp.zeros_like(store)

    def first(index, carry):
        rows = pl.ds(pl.multiple_of(index * 2 * line, 2 * line), 2 * line)
        pre = (u_ref[rows, :] - center) * factor + shift
        value = smooth(pre) * wide(mask_ref[rows, :], depth)
        split_store(even_ref, moved_ref, index + 1, value, line)
        return carry

    lax.fori_loop(0, height, first, 0)
    half = height // 2
    sources = tap_sources(even_ref, moved_ref)
    for side in range(2):
        for part in range(2):
            lhs = jnp.concatenate(
                [
                    ref[half * part + row : half * part + row + half, plane].reshape(half * line, depth)
                    for row in range(3)
                    for ref, plane in sources[side]
                ],
                axis=1,
            )
            result = times(lhs, filter_ref[...])
            for index in range(half):
                begin = (half * part + index) * 2 * line + side * line
                piece = result[index * line : index * line + line]
                out_ref[begin : begin + line, :] = piece
                kept = piece * wide(mask_ref[begin : begin + line, :], piece.shape[1])
                add_rows(store, 0, kept)
                add_rows(store, 1, kept * piece)
    finish_rows(store, sums_ref, 2)


def expand_body(parts, u_ref, count_ref, scale_ref, shift_ref, mask_ref, filter_ref, hidden_ref, out_ref, sums_ref, store, which, rows_step):
    center, inverse = statistics(total(parts), count_ref[which : which + 1, 0:1])
    factor = scale_ref[...] * inverse
    shift = shift_ref[...]
    depth = u_ref.shape[1]
    store[...] = jnp.zeros_like(store)

    def step(index, carry):
        rows = pl.ds(pl.multiple_of(index * rows_step, rows_step), rows_step)
        pre = (u_ref[rows, :] - center) * factor + shift
        value = low(smooth(pre) * wide(mask_ref[rows, :], depth))
        hidden_ref[rows, :] = value
        result = times(value, filter_ref[...])
        out_ref[rows, :] = result
        add_rows(store, 0, result)
        add_rows(store, 1, result * result)
        return carry

    lax.fori_loop(0, u_ref.shape[0] // rows_step, step, 0)
    finish_rows(store, sums_ref, 2)


def join_body(images, parts, u_ref, count_ref, scale_ref, shift_ref, mask_ref, start_ref, reduce_ref, side_ref, block_ref, reduced_ref, picked_ref, sided_ref, sums_ref, side_sums_ref, store, side_store):
    center, inverse = statistics(total(parts), count_ref[0:1, 0:1])
    factor = scale_ref[...] * inverse
    shift = shift_ref[...]
    depth = u_ref.shape[1]
    line = even_width * images
    store[...] = jnp.zeros_like(store)
    side_store[...] = jnp.zeros_like(side_store)

    def step(index, carry):
        rows = pl.ds(pl.multiple_of(index * 4 * line, 4 * line), 4 * line)
        pre = (u_ref[rows, :] - center) * factor + shift + start_ref[rows, :].astype(full_type)
        value = low(smooth(pre) * wide(mask_ref[rows, :], depth))
        block_ref[rows, :] = value
        picked_ref[pl.ds(pl.multiple_of(index * line, line), line), :] = value[:line]
        result = times(value, reduce_ref[...])
        reduced_ref[rows, :] = result
        add_rows(store, 0, result)
        add_rows(store, 1, result * result)
        return carry

    lax.fori_loop(0, u_ref.shape[0] // (4 * line), step, 0)
    finish_rows(store, sums_ref, 2)
    width = 512

    def side(index, carry):
        columns = pl.ds(pl.multiple_of(index * width, width), width)
        result = times(picked_ref[...], side_ref[:, columns])
        sided_ref[:, columns] = result
        side_sums_ref[0:1, columns] = column_sum(fold(result))
        side_sums_ref[1:2, columns] = column_sum(fold(result * result))
        return carry

    lax.fori_loop(0, side_ref.shape[1] // width, side, 0)


def shrink_body(images, parts, u_ref, count_ref, scale_ref, shift_ref, mask_ref, small_ref, filter_ref, even_ref, moved_ref, out_ref, sums_ref):
    depth = u_ref.shape[1]
    line = even_width * images
    height = even_ref.shape[0] - 2
    center, inverse = statistics(total(parts), count_ref[0:1, 0:1])
    factor = scale_ref[...] * inverse
    shift = shift_ref[...]
    blank_border(even_ref, moved_ref)

    def first(index, carry):
        rows = pl.ds(pl.multiple_of(index * 2 * line, 2 * line), 2 * line)
        pre = (u_ref[rows, :] - center) * factor + shift
        value = smooth(pre) * wide(mask_ref[rows, :], depth)
        split_store(even_ref, moved_ref, index + 1, value, line)
        return carry

    lax.fori_loop(0, height, first, 0)
    half = height // 2
    result = None
    for row in range(3):
        lhs = jnp.concatenate(
            [
                jnp.concatenate([ref[2 * index + row, plane] for index in range(half)], axis=0)
                for ref, plane in ((moved_ref, 1), (even_ref, 0), (even_ref, 1))
            ],
            axis=1,
        )
        term = times(lhs, filter_ref[row * 3 * depth : row * 3 * depth + 3 * depth, :])
        result = term if result is None else result + term
    out_ref[...] = result
    kept = result * wide(small_ref[...], result.shape[1])
    sums_ref[0:1, :] = column_sum(fold(kept))
    sums_ref[1:2, :] = column_sum(fold(kept * result))


def leave_body(images, parts, side_parts, u_ref, side_ref, count_ref, scale_ref, shift_ref, side_scale_ref, side_shift_ref, small_ref, pixel_ref, block_ref, joined_ref, pooled_ref, store):
    center, inverse = statistics(total(parts), count_ref[1:2, 0:1])
    factor = scale_ref[...] * inverse
    side_center, side_inverse = statistics(total(side_parts), count_ref[1:2, 0:1])
    side_factor = side_scale_ref[...] * side_inverse
    shift = shift_ref[...] + side_shift_ref[...]
    depth = u_ref.shape[1]
    line = even_width * images
    pairs = block_ref.shape[1]
    store[...] = jnp.zeros_like(store)

    def step(index, carry):
        rows = pl.ds(pl.multiple_of(index * line, line), line)
        pre = (u_ref[rows, :] - center) * factor + (side_ref[rows, :] - side_center) * side_factor + shift
        joined_ref[rows, :] = pre
        value = smooth(pre) * wide(small_ref[rows, :], depth)
        block_ref[index] = low(value).reshape(even_width, images, depth)[:pairs]
        add_rows(store, 0, value)
        return carry

    lax.fori_loop(0, u_ref.shape[0] // line, step, 0)
    summed = store[0:images, :]
    for begin in range(images, 8, images):
        summed = summed + store[begin : begin + images, :]
    pooled_ref[...] = summed * pixel_ref[:, 0:1]


def gather_images(store, row, images):
    summed = store[row * 8 : row * 8 + images, :]
    for begin in range(images, 8, images):
        summed = summed + store[row * 8 + begin : row * 8 + begin + images, :]
    return summed


def slope_sums_body(images, parts, side_parts, joined_ref, u_ref, side_ref, count_ref, small_ref, slope_ref, plain_ref, unit_ref, side_unit_ref, store):
    center, inverse = statistics(total(parts), count_ref[1:2, 0:1])
    side_center, side_inverse = statistics(total(side_parts), count_ref[1:2, 0:1])
    depth = u_ref.shape[1]
    line = even_width * images
    store[...] = jnp.zeros_like(store)

    def step(index, carry):
        rows = pl.ds(pl.multiple_of(index * line, line), line)
        slope = smooth_slope(joined_ref[rows, :]) * wide(small_ref[rows, :], depth)
        slope_ref[rows, :] = slope
        add_rows(store, 0, slope)
        add_rows(store, 1, slope * (u_ref[rows, :] - center))
        add_rows(store, 2, slope * (side_ref[rows, :] - side_center))
        return carry

    lax.fori_loop(0, u_ref.shape[0] // line, step, 0)
    plain_ref[...] = gather_images(store, 0, images)
    unit_ref[...] = gather_images(store, 1, images) * inverse
    side_unit_ref[...] = gather_images(store, 2, images) * side_inverse


def compare_body(pooled_ref, partner_ref, pixel_ref, plain_ref, unit_ref, side_unit_ref, loss_ref, grad_ref, sums_ref):
    pooled, partner = pooled_ref[...], partner_ref[...]
    inverse_own = lax.rsqrt(jnp.sum(pooled * pooled, axis=1, keepdims=True) + eps_cos)
    unit_own = pooled * inverse_own
    unit_other = partner * lax.rsqrt(jnp.sum(partner * partner, axis=1, keepdims=True) + eps_cos)
    cosine = jnp.sum(unit_own * unit_other, axis=1, keepdims=True)
    loss_ref[...] = jnp.broadcast_to(-0.5 * cosine, loss_ref.shape)
    grad = (-0.5 * loss_scale) * inverse_own * (unit_other - cosine * unit_own) * pixel_ref[:, 0:1]
    grad_ref[...] = grad
    sums_ref[0:1, :] = column_sum(grad * plain_ref[...])
    sums_ref[1:2, :] = column_sum(grad * unit_ref[...])
    sums_ref[2:3, :] = column_sum(grad * side_unit_ref[...])


def norm_back(sums, totals, count, scale):
    center, inverse = statistics(sums, count)
    factor = scale * inverse
    return center, inverse, factor, -(factor * inverse * totals[1:2] / count), -(factor * totals[0:1] / count)


def leave_back_body(images, parts, side_parts, grads, slope_ref, grad_ref, u_ref, side_ref, count_ref, scale_ref, side_scale_ref, small_ref, filter_ref, inner_parts, inner_u_ref, inner_slope_ref, low_ref, side_low_ref, out_ref, sums_ref, store):
    totals = total(grads)
    count = count_ref[1:2, 0:1]
    center, _, factor, along, level = norm_back(total(parts), totals, count, scale_ref[...])
    side_totals = jnp.concatenate([totals[0:1], totals[2:3]], axis=0)
    side_center, _, side_factor, side_along, side_level = norm_back(total(side_parts), side_totals, count, side_scale_ref[...])
    depth = u_ref.shape[1]
    line = even_width * images
    grad = jnp.concatenate([grad_ref[...]] * (line // images), axis=0)

    def step(index, carry):
        rows = pl.ds(pl.multiple_of(index * line, line), line)
        mask = wide(small_ref[rows, :], depth)
        joined = slope_ref[rows, :] * grad
        low_ref[rows, :] = low((joined * factor + (u_ref[rows, :] - center) * along + level) * mask)
        side_low_ref[rows, :] = low((joined * side_factor + (side_ref[rows, :] - side_center) * side_along + side_level) * mask)
        return carry

    lax.fori_loop(0, u_ref.shape[0] // line, step, 0)
    inner_center, inner_inverse = statistics(total(inner_parts), count)
    result = times_back(low_ref[...], filter_ref[...]) * inner_slope_ref[...]
    out_ref[...] = result
    sums_ref[0:1, :] = column_sum(fold(result))
    sums_ref[1:2, :] = column_sum(fold(result * (inner_u_ref[...] - inner_center))) * inner_inverse


def shrink_back_body(images, parts, grads, g_ref, u_ref, count_ref, scale_ref, small_ref, filter_ref, inner_parts, inner_u_ref, inner_slope_ref, low_ref, out_ref, sums_ref, store):
    depth = u_ref.shape[1]
    inner = filter_ref.shape[2]
    line = even_width * images
    half = u_ref.shape[0] // line
    center, _, factor, along, level = norm_back(total(parts), total(grads), count_ref[1:2, 0:1], scale_ref[...])
    exact = (g_ref[...] * factor + (u_ref[...] - center) * along + level) * wide(small_ref[...], depth)
    here = low(exact)
    low_ref[...] = here
    right = low(pltpu.roll(exact, exact.shape[0] - images, 0))
    blank = jnp.zeros((line, depth), low_type)
    below = jnp.concatenate([here[line:], blank], axis=0)
    below_right = jnp.concatenate([right[line:], blank], axis=0)
    inner_center, inner_inverse = statistics(total(inner_parts), count_ref[0:1, 0:1])
    store[...] = jnp.zeros_like(store)
    for row in range(2):
        for side in range(2):
            terms = [(here, 1 + row, 1 + side)]
            if side:
                terms.append((right, 1 + row, 0))
            if row:
                terms.append((below, 0, 1 + side))
            if row and side:
                terms.append((below_right, 0, 0))
            lhs = jnp.concatenate([value for value, _, _ in terms], axis=1)
            rhs = jnp.concatenate([filter_ref[down * 3 + over] for _, down, over in terms], axis=1)
            result = times_back(lhs, rhs)
            for index in range(half):
                begin = (index * 4 + row * 2 + side) * line
                rows = slice(begin, begin + line)
                piece = result[index * line : index * line + line] * inner_slope_ref[rows, :]
                out_ref[rows, :] = piece
                add_rows(store, 0, piece)
                add_rows(store, 1, piece * (inner_u_ref[rows, :] - inner_center))
    sums_ref[0:1, :] = column_sum(store[0:8, :])
    sums_ref[1:2, :] = column_sum(store[8:16, :]) * inner_inverse


def join_back_body(images, parts, grads, g_ref, u_ref, count_ref, scale_ref, mask_ref, filter_ref, picked_ref, inner_parts, inner_u_ref, inner_slope_ref, low_ref, out_ref, sums_ref, store):
    depth = u_ref.shape[1]
    line = even_width * images
    center, _, factor, along, level = norm_back(total(parts), total(grads), count_ref[0:1, 0:1], scale_ref[...])
    inner_center, inner_inverse = statistics(total(inner_parts), count_ref[0:1, 0:1])
    store[...] = jnp.zeros_like(store)

    def step(index, carry):
        rows = pl.ds(pl.multiple_of(index * 4 * line, 4 * line), 4 * line)
        value = low((g_ref[rows, :] * factor + (u_ref[rows, :] - center) * along + level) * wide(mask_ref[rows, :], depth))
        low_ref[rows, :] = value
        result = times_back(value, filter_ref[...])
        extra = picked_ref[pl.ds(pl.multiple_of(index * line, line), line), :]
        result = jnp.concatenate([result[:line] + extra, result[line:]], axis=0) * inner_slope_ref[rows, :]
        out_ref[rows, :] = result
        add_rows(store, 0, result)
        add_rows(store, 1, result * (inner_u_ref[rows, :] - inner_center))
        return carry

    lax.fori_loop(0, u_ref.shape[0] // (4 * line), step, 0)
    sums_ref[0:1, :] = column_sum(store[0:8, :])
    sums_ref[1:2, :] = column_sum(store[8:16, :]) * inner_inverse


def expand_back_body(parts, grads, g_ref, u_ref, count_ref, scale_ref, mask_ref, filter_ref, inner_parts, inner_u_ref, inner_slope_ref, low_ref, out_ref, sums_ref, store, rows_step):
    depth = u_ref.shape[1]
    center, _, factor, along, level = norm_back(total(parts), total(grads), count_ref[0:1, 0:1], scale_ref[...])
    inner_center, inner_inverse = statistics(total(inner_parts), count_ref[0:1, 0:1])
    store[...] = jnp.zeros_like(store)

    def step(index, carry):
        rows = pl.ds(pl.multiple_of(index * rows_step, rows_step), rows_step)
        value = low((g_ref[rows, :] * factor + (u_ref[rows, :] - center) * along + level) * wide(mask_ref[rows, :], depth))
        low_ref[rows, :] = value
        result = times_back(value, filter_ref[...]) * inner_slope_ref[rows, :]
        out_ref[rows, :] = result
        add_rows(store, 0, result)
        add_rows(store, 1, result * (inner_u_ref[rows, :] - inner_center))
        return carry

    lax.fori_loop(0, u_ref.shape[0] // rows_step, step, 0)
    sums_ref[0:1, :] = column_sum(store[0:8, :])
    sums_ref[1:2, :] = column_sum(store[8:16, :]) * inner_inverse


def block_back_body(images, parts, grads, g_ref, u_ref, count_ref, scale_ref, mask_ref, filter_ref, inner_parts, inner_u_ref, inner_slope_ref, low_ref, out_ref, sums_ref, even_ref, moved_ref, store):
    depth = u_ref.shape[1]
    line = even_width * images
    height = even_ref.shape[0] - 2
    center, _, factor, along, level = norm_back(total(parts), total(grads), count_ref[0:1, 0:1], scale_ref[...])
    inner_center, inner_inverse = statistics(total(inner_parts), count_ref[0:1, 0:1])
    blank_border(even_ref, moved_ref)
    store[...] = jnp.zeros_like(store)

    def first(index, carry):
        rows = pl.ds(pl.multiple_of(index * 2 * line, 2 * line), 2 * line)
        value = (g_ref[rows, :] * factor + (u_ref[rows, :] - center) * along + level) * wide(mask_ref[rows, :], depth)
        low_ref[rows, :] = low(value)
        split_store(even_ref, moved_ref, index + 1, value, line)
        return carry

    lax.fori_loop(0, height, first, 0)
    half = height // 2
    sources = tap_sources(even_ref, moved_ref)
    rhs = jnp.concatenate([filter_ref[8 - tap] for tap in range(9)], axis=1)
    for side in range(2):
        for part in range(2):
            lhs = jnp.concatenate(
                [
                    ref[half * part + row : half * part + row + half, plane].reshape(half * line, depth)
                    for row in range(3)
                    for ref, plane in sources[side]
                ],
                axis=1,
            )
            result = times_back(lhs, rhs)
            for index in range(half):
                begin = (half * part + index) * 2 * line + side * line
                rows = slice(begin, begin + line)
                piece = result[index * line : index * line + line] * inner_slope_ref[rows, :]
                out_ref[rows, :] = piece
                add_rows(store, 0, piece)
                add_rows(store, 1, piece * (inner_u_ref[rows, :] - inner_center))
    sums_ref[0:1, :] = column_sum(store[0:8, :])
    sums_ref[1:2, :] = column_sum(store[8:16, :]) * inner_inverse


def exit_body(images, parts, grads, g_ref, u_ref, count_ref, scale_ref, mask_ref, filter_ref, joined_ref, low_ref, out_ref):
    depth = u_ref.shape[1]
    pairs = out_ref.shape[1]
    line = even_width * images
    center, _, factor, along, level = norm_back(total(parts), total(grads), count_ref[0:1, 0:1], scale_ref[...])

    def step(index, carry):
        rows = pl.ds(pl.multiple_of(index * 4 * line, 4 * line), 4 * line)
        mask = mask_ref[rows, :]
        value = low((g_ref[rows, :] * factor + (u_ref[rows, :] - center) * along + level) * wide(mask, depth))
        low_ref[rows, :] = value
        result = low((times_back(value, filter_ref[...]) + joined_ref[rows, :]) * wide(mask, joined_ref.shape[1]))
        for row in range(2):
            for side in range(2):
                begin = (row * 2 + side) * line
                cells = result[begin : begin + line].reshape(even_width, images, result.shape[1])
                out_ref[index * 2 + row, :, side] = cells[:pairs]
        return carry

    lax.fori_loop(0, u_ref.shape[0] // (4 * line), step, 0)


def natural_body(images, value_ref, out_ref):
    pairs = out_ref.shape[1]
    line = even_width * images
    depth = value_ref.shape[1]

    def step(index, carry):
        for side in range(2):
            rows = pl.ds(pl.multiple_of(index * 2 * line + side * line, line), line)
            out_ref[index, :, side] = value_ref[rows, :].reshape(even_width, images, depth)[:pairs]
        return carry

    lax.fori_loop(0, out_ref.shape[0], step, 0)


def slope_body(parts, u_ref, count_ref, scale_ref, shift_ref, mask_ref, extras, out_ref, which, rows_step):
    center, inverse = statistics(total(parts), count_ref[which : which + 1, 0:1])
    factor = scale_ref[...] * inverse
    shift = shift_ref[...]
    depth = u_ref.shape[1]

    def step(index, carry):
        rows = pl.ds(pl.multiple_of(index * rows_step, rows_step), rows_step)
        pre = (u_ref[rows, :] - center) * factor + shift
        for extra_ref in extras:
            pre = pre + extra_ref[rows, :].astype(full_type)
        out_ref[rows, :] = smooth_slope(pre) * wide(mask_ref[rows, :], depth)
        return carry

    lax.fori_loop(0, u_ref.shape[0] // rows_step, step, 0)


def times_back_body(value_ref, filter_ref, out_ref):
    out_ref[...] = times_back(value_ref[...], filter_ref[...])


def filter_grad_body(value_ref, grad_ref, out_ref):
    out_ref[...] = times_rows(value_ref[...], grad_ref[...])


def block_filter_body(even_ref, moved_ref, grad_ref, out_ref):
    height, _, line, depth = even_ref.shape
    height = height - 2
    width = grad_ref.shape[1]
    grad = grad_ref[...].reshape(height, 2, line, width)
    grad = jnp.concatenate([grad[:, side].reshape(height * line, width) for side in range(2)], axis=0)
    sources = tap_sources(even_ref, moved_ref)
    for row in range(3):
        for over in range(3):
            lhs = jnp.concatenate(
                [
                    sources[side][over][0][row : row + height, sources[side][over][1]].reshape(height * line, depth)
                    for side in range(2)
                ],
                axis=0,
            )
            out_ref[row * 3 + over] = times_rows(lhs, grad)


def shrink_filter_body(even_ref, moved_ref, grad_ref, out_ref):
    half = even_ref.shape[0] // 2 - 1
    for row in range(3):
        for over, (ref, plane) in enumerate(((moved_ref, 1), (even_ref, 0), (even_ref, 1))):
            lhs = jnp.concatenate([ref[2 * index + row, plane] for index in range(half)], axis=0)
            out_ref[row * 3 + over] = times_rows(lhs, grad_ref[...])


def exchange(value, axis, bits):
    return lax.ppermute(value, axis, [(i, i ^ bits) for i in range(lax.axis_size(axis))])


def share(sums):
    size = lax.axis_size("dp")
    if size > 1:
        sums = sums + exchange(sums, "dp", 1)
    if size > 2:
        sums = sums + exchange(sums, "dp", 3)
    parts = (sums,)
    bit = 4
    while bit < size:
        if len(parts) > 1:
            parts = (sum(parts[1:], parts[0]),)
        steps = [bit + 1, 2 * bit + 1, 3 * bit + 1] if 2 * bit < size else [bit + 1]
        parts = parts + tuple(exchange(parts[0], "dp", step) for step in steps)
        bit *= 4
    return parts


def pack_flat(parts):
    return jnp.concatenate([part.reshape(-1) for part in parts])


def as_row(value):
    return value.reshape(1, -1)


def per_device(
    inputs,
    resolution,
    reduce_a,
    spatial_a,
    expand_a,
    reduce_b,
    spatial_b,
    expand_b,
    shortcut_b,
    scale_reduce_a,
    shift_reduce_a,
    scale_spatial_a,
    shift_spatial_a,
    scale_expand_a,
    shift_expand_a,
    scale_reduce_b,
    shift_reduce_b,
    scale_spatial_b,
    shift_spatial_b,
    scale_expand_b,
    shift_expand_b,
    scale_shortcut,
    shift_shortcut,
):
    images, height, depth_a = inputs.shape[1], inputs.shape[2], inputs.shape[4]
    pairs = height // 2
    middle_a, middle_b, depth_b = reduce_a.shape[1], reduce_b.shape[1], shortcut_b.shape[1]
    line = even_width * images
    rows_big, rows_small = height * 2 * line, pairs * line
    sizes = resolution[0]
    places_h = jnp.arange(height).reshape(height, 1, 1, 1, 1)
    places_w = (2 * jnp.arange(even_width) + jnp.arange(2).reshape(2, 1)).reshape(1, 2, even_width, 1, 1)
    bound = (sizes // 16).reshape(1, 1, 1, images, 1)
    mask_big = ((places_h < bound) & (places_w < bound)).astype(full_type)
    count_big = jnp.sum(mask_big)
    mask_big = jnp.broadcast_to(mask_big, (height, 2, even_width, images, 128)).reshape(rows_big, 128)
    places_h = jnp.arange(pairs).reshape(pairs, 1, 1, 1)
    places_w = jnp.arange(even_width).reshape(1, even_width, 1, 1)
    bound = (sizes // 32).reshape(1, 1, images, 1)
    mask_small = ((places_h < bound) & (places_w < bound)).astype(full_type)
    count_small = jnp.sum(mask_small)
    mask_small = jnp.broadcast_to(mask_small, (pairs, even_width, images, 128)).reshape(rows_small, 128)
    pixel = 1.0 / (sizes // 32 * (sizes // 32)).astype(full_type)
    pixel = jnp.broadcast_to(pixel.reshape(images, 1), (images, 128))
    counts = jnp.broadcast_to(jnp.stack([count_big, count_small]).reshape(2, 1), (2, 128))
    counts = sum(share(counts)[1:], share(counts)[0])
    spatial_a9 = spatial_a.reshape(9, middle_a, middle_a)
    spatial_b9 = spatial_b.reshape(9, middle_b, middle_b)
    cells = inputs[0].transpose(1, 2, 0, 3).reshape(height, pairs, 2, images, depth_a)

    def padded(width):
        return shaped(height + 2, 2, line, width, kind=low_type)

    def with_images(body):
        return functools.partial(body, images)

    start, reduced_a, sums = call(
        with_images(enter_body),
        [shaped(rows_big, depth_a, kind=low_type), shaped(rows_big, middle_a), shaped(2, middle_a)],
        [cells, mask_big, reduce_a],
        scratch=[((16, middle_a), full_type)],
    )
    sums_ra = share(sums)
    scale_ra, shift_ra = as_row(scale_reduce_a), as_row(shift_reduce_a)
    even_a, moved_a, mixed_a, sums = call(
        with_images(block_body),
        [padded(middle_a), padded(middle_a), shaped(rows_big, middle_a), shaped(2, middle_a)],
        [sums_ra, reduced_a, counts, scale_ra, shift_ra, mask_big, spatial_a.reshape(9 * middle_a, middle_a)],
        scratch=[((16, middle_a), full_type)],
    )
    sums_sa = share(sums)
    scale_sa, shift_sa = as_row(scale_spatial_a), as_row(shift_spatial_a)
    hidden_two_a, expanded_a, sums = call(
        functools.partial(expand_body, which=0, rows_step=4 * line),
        [shaped(rows_big, middle_a, kind=low_type), shaped(rows_big, depth_a), shaped(2, depth_a)],
        [sums_sa, mixed_a, counts, scale_sa, shift_sa, mask_big, expand_a],
        scratch=[((16, depth_a), full_type)],
    )
    sums_ea = share(sums)
    scale_ea, shift_ea = as_row(scale_expand_a), as_row(shift_expand_a)
    block_a, reduced_b, picked, side_b, sums, side_sums = call(
        with_images(join_body),
        [
            shaped(rows_big, depth_a, kind=low_type),
            shaped(rows_big, middle_b),
            shaped(rows_small, depth_a, kind=low_type),
            shaped(rows_small, depth_b),
            shaped(2, middle_b),
            shaped(2, depth_b),
        ],
        [sums_ea, expanded_a, counts, scale_ea, shift_ea, mask_big, start, reduce_b, shortcut_b],
        scratch=[((16, middle_b), full_type), ((16, 128), full_type)],
    )
    shared = share(jnp.concatenate([sums, side_sums], axis=1))
    sums_rb = tuple(part[:, :middle_b] for part in shared)
    sums_sc = tuple(part[:, middle_b:] for part in shared)
    scale_rb, shift_rb = as_row(scale_reduce_b), as_row(shift_reduce_b)
    scale_sc, shift_sc = as_row(scale_shortcut), as_row(shift_shortcut)
    even_b, moved_b, mixed_b, sums = call(
        with_images(shrink_body),
        [padded(middle_b), padded(middle_b), shaped(rows_small, middle_b), shaped(2, middle_b)],
        [sums_rb, reduced_b, counts, scale_rb, shift_rb, mask_big, mask_small, spatial_b.reshape(9 * middle_b, middle_b)],
    )
    sums_sb = share(sums)
    scale_sb, shift_sb = as_row(scale_spatial_b), as_row(shift_spatial_b)
    hidden_two_b, expanded_b, sums = call(
        functools.partial(expand_body, which=1, rows_step=line),
        [shaped(rows_small, middle_b, kind=low_type), shaped(rows_small, depth_b), shaped(2, depth_b)],
        [sums_sb, mixed_b, counts, scale_sb, shift_sb, mask_small, expand_b],
        scratch=[((16, depth_b), full_type)],
    )
    sums_eb = share(sums)
    scale_eb, shift_eb = as_row(scale_expand_b), as_row(shift_expand_b)
    block_b, joined_b, pooled = call(
        with_images(leave_body),
        [shaped(pairs, pairs, images, depth_b, kind=low_type), shaped(rows_small, depth_b), shaped(images, depth_b)],
        [sums_eb, sums_sc, expanded_b, side_b, counts, scale_eb, shift_eb, scale_sc, shift_sc, mask_small, pixel],
        scratch=[((8, depth_b), full_type)],
    )
    partner = exchange(pooled, "view", 1)
    slope_b, plain, unit, side_unit = call(
        with_images(slope_sums_body),
        [shaped(rows_small, depth_b)] + [shaped(images, depth_b)] * 3,
        [sums_eb, sums_sc, joined_b, expanded_b, side_b, counts, mask_small],
        scratch=[((24, depth_b), full_type)],
    )
    loss, grad_out, sums = call(
        compare_body,
        [shaped(images, 128), shaped(images, depth_b), shaped(3, depth_b)],
        [pooled, partner, pixel, plain, unit, side_unit],
        cost_us=1,
    )
    grads_eb = share(sums)

    def slope(parts, value, scale, shift, mask, extras, which, rows_step):
        return call(
            functools.partial(slope_body, which=which, rows_step=rows_step),
            [shaped(*value.shape)],
            [parts, value, counts, scale, shift, mask, extras],
        )[0]

    slope_sb = slope(sums_sb, mixed_b, scale_sb, shift_sb, mask_small, (), 1, line)
    slope_rb = slope(sums_rb, reduced_b, scale_rb, shift_rb, mask_big, (), 0, 2 * line)
    slope_ea = slope(sums_ea, expanded_a, scale_ea, shift_ea, mask_big, (start,), 0, 2 * line)
    slope_sa = slope(sums_sa, mixed_a, scale_sa, shift_sa, mask_big, (), 0, 2 * line)
    slope_ra = slope(sums_ra, reduced_a, scale_ra, shift_ra, mask_big, (), 0, 2 * line)

    low_eb, low_sc, grad_sb, sums = call(
        with_images(leave_back_body),
        [
            shaped(rows_small, depth_b, kind=low_type),
            shaped(rows_small, depth_b, kind=low_type),
            shaped(rows_small, middle_b),
            shaped(2, middle_b),
        ],
        [
            sums_eb,
            sums_sc,
            grads_eb,
            slope_b,
            grad_out,
            expanded_b,
            side_b,
            counts,
            scale_eb,
            scale_sc,
            mask_small,
            expand_b,
            sums_sb,
            mixed_b,
            slope_sb,
        ],
        scratch=[((8, 128), full_type)],
    )
    grads_sb = share(sums)
    low_sb, grad_rb, sums = call(
        with_images(shrink_back_body),
        [shaped(rows_small, middle_b, kind=low_type), shaped(rows_big, middle_b), shaped(2, middle_b)],
        [sums_sb, grads_sb, grad_sb, mixed_b, counts, scale_sb, mask_small, spatial_b9, sums_rb, reduced_b, slope_rb],
        scratch=[((16, middle_b), full_type)],
    )
    grads_rb = share(sums)
    grad_picked = call(times_back_body, [shaped(rows_small, depth_a)], [low_sc, shortcut_b])[0]
    low_rb, joined_grad, sums = call(
        with_images(join_back_body),
        [shaped(rows_big, middle_b, kind=low_type), shaped(rows_big, depth_a), shaped(2, depth_a)],
        [sums_rb, grads_rb, grad_rb, reduced_b, counts, scale_rb, mask_big, reduce_b, grad_picked, sums_ea, expanded_a, slope_ea],
        scratch=[((16, depth_a), full_type)],
    )
    grads_ea = share(sums)
    low_ea, grad_sa, sums = call(
        functools.partial(expand_back_body, rows_step=4 * line),
        [shaped(rows_big, depth_a, kind=low_type), shaped(rows_big, middle_a), shaped(2, middle_a)],
        [sums_ea, grads_ea, joined_grad, expanded_a, counts, scale_ea, mask_big, expand_a, sums_sa, mixed_a, slope_sa],
        scratch=[((16, middle_a), full_type)],
    )
    grads_sa = share(sums)
    low_sa, grad_ra, sums = call(
        with_images(block_back_body),
        [shaped(rows_big, middle_a, kind=low_type), shaped(rows_big, middle_a), shaped(2, middle_a)],
        [sums_sa, grads_sa, grad_sa, mixed_a, counts, scale_sa, mask_big, spatial_a9, sums_ra, reduced_a, slope_ra],
        scratch=[
            ((height + 2, 2, line, middle_a), low_type),
            ((height + 2, 2, line, middle_a), low_type),
            ((16, middle_a), full_type),
        ],
    )
    grads_ra = share(sums)
    low_ra, input_grad = call(
        with_images(exit_body),
        [shaped(rows_big, middle_a, kind=low_type), shaped(height, pairs, 2, images, depth_a, kind=low_type)],
        [sums_ra, grads_ra, grad_ra, reduced_a, counts, scale_ra, mask_big, reduce_a, joined_grad],
    )

    def filter_grad(value, grad):
        return call(filter_grad_body, [shaped(value.shape[1], grad.shape[1])], [value, grad])[0]

    grad_expand_b = filter_grad(hidden_two_b, low_eb)
    grad_shortcut = filter_grad(picked, low_sc)
    grad_spatial_b = call(shrink_filter_body, [shaped(9, middle_b, middle_b)], [even_b, moved_b, low_sb])[0]
    grad_reduce_b = filter_grad(block_a, low_rb)
    grad_expand_a = filter_grad(hidden_two_a, low_ea)
    grad_spatial_a = call(block_filter_body, [shaped(9, middle_a, middle_a)], [even_a, moved_a, low_sa])[0]
    grad_reduce_a = filter_grad(start, low_ra)
    block_out = call(
        with_images(natural_body), [shaped(height, pairs, 2, images, depth_a, kind=low_type)], [block_a]
    )[0]

    def both_views(parts):
        value = sum(parts[1:], parts[0])
        return value + exchange(value, "view", 1)

    def once(value):
        first = (lax.axis_index("dp") == 0) & (lax.axis_index("view") == 0)
        return jnp.where(first, value, 0.0)

    all_eb = both_views(grads_eb)
    late_flat = pack_flat(
        [grad_reduce_b, grad_spatial_b, grad_expand_b, grad_shortcut]
        + [once(v) for v in (both_views(grads_rb), both_views(grads_sb), all_eb[:2], all_eb[0], all_eb[2])]
    )
    early_flat = pack_flat(
        [grad_reduce_a, grad_spatial_a, grad_expand_a]
        + [once(v) for v in (both_views(grads_ra), both_views(grads_sa), both_views(grads_ea))]
    )
    late_done = lax.psum_scatter(late_flat, ("view", "dp"), scatter_dimension=0, tiled=True)
    early_done = lax.psum_scatter(early_flat, ("view", "dp"), scatter_dimension=0, tiled=True)

    def natural(value):
        return value.reshape(height, height, images, depth_a).transpose(2, 0, 1, 3)[None]

    return (
        loss[:, 0][None],
        natural(block_out),
        block_b.transpose(2, 0, 1, 3)[None],
        natural(input_grad),
        early_done,
        late_done,
    )


def solution(mesh):
    copied = (P(),) * 21
    images = P("view", "dp", None, None, None)
    packed = P(("view", "dp"))
    return jax.shard_map(
        per_device,
        mesh=mesh,
        in_specs=(images, P("view", "dp")) + copied,
        out_specs=(P("view", "dp"), images, images, images, packed, packed),
        check_vma=False,
    )
```

```python
import functools

import jax
import jax.numpy as jnp
from jax import lax
from jax.experimental import pallas as pl
from jax.experimental.pallas import tpu as pltpu
from jax.sharding import PartitionSpec as P

eps_norm = 1e-05
eps_cos = 1e-06
loss_scale = 65536.0
low_type = jnp.bfloat16
full_type = jnp.float32
vmem_small, vmem_large = 6 * 1024 * 1024, 18 * 1024 * 1024
cost_small, cost_large = 0.1, 0.1
halved_of_128 = 56

even_width = 8


class View:
    def __init__(self, value, rows, columns):
        self.value, self.rows, self.columns = value, slice(*rows), slice(*columns)


def call(body, outs, args, cost_us=cost_small, scratch=(), copies=0, vmem=vmem_small, after=(), scalars=()):
    whole = pl.BlockSpec(memory_space=pltpu.VMEM)
    placed = [pl.BlockSpec(memory_space=pltpu.HBM) if copies and len(out.shape) == 3 else whole for out in outs]
    flat, places = [], {}

    def place(item):
        value = item.value if isinstance(item, View) else item
        if id(value) not in places:
            places[id(value)] = len(flat)
            flat.append(value)
        return places[id(value)]

    for item in args:
        for one in item if isinstance(item, tuple) else (item,):
            place(one)

    def run(*refs):
        def found(item):
            if isinstance(item, tuple):
                return tuple(found(one) for one in item)
            ref = refs[place(item)]
            return ref.at[item.rows, item.columns] if isinstance(item, View) else ref

        body(*[found(item) for item in args], *refs[len(flat) + len(after) :])

    return pl.pallas_call(
        run,
        out_shape=outs,
        in_specs=[pl.BlockSpec(memory_space=pltpu.SMEM) if i in scalars else whole for i in range(len(flat))]
        + [pl.BlockSpec(memory_space=pl.ANY)] * len(after),
        out_specs=placed,
        scratch_shapes=[pltpu.VMEM(dims, kind) for dims, kind in scratch]
        + ([pltpu.SemaphoreType.DMA((copies,))] if copies else []),
        compiler_params=pltpu.CompilerParams(vmem_limit_bytes=vmem),
        cost_estimate=pl.CostEstimate(flops=int(cost_us * 1e9), bytes_accessed=int(cost_us * 1e6), transcendentals=0),
    )(*flat, *after)


def shaped(*dims, kind=full_type):
    return jax.ShapeDtypeStruct(dims, kind)


def tail_parts(pre):
    size = jnp.abs(pre)
    base = 1.0 + (0.3275911 * 0.7071067811865476) * size
    guess = pl.reciprocal(base, approx=True)
    guess = guess * (2.0 - base * guess)
    guess = guess * (2.0 - base * guess)
    bell = jnp.exp(-0.5 * (pre * pre))
    series = 0.5 * 1.061405429
    for term in (-1.453152027, 1.421413741, -0.284496736, 0.254829592):
        series = series * guess + 0.5 * term
    return size, bell, series * guess * bell


def smooth(pre):
    size, _, tail = tail_parts(pre)
    return jnp.maximum(pre, 0.0) - size * tail


def smooth_slope(pre):
    _, bell, tail = tail_parts(pre)
    return jnp.where(pre >= 0.0, 1.0 - tail, tail) + 0.3989422804014327 * (pre * bell)


def wide(mask, width):
    return jnp.concatenate([mask] * (width // mask.shape[1]), axis=1)


def fold(value):
    rows, width = value.shape
    return jnp.sum(value.reshape(rows // 8, 8, width), axis=0)


def column_sum(value):
    return jnp.sum(value, axis=0, keepdims=True)


def total(parts):
    result = parts[0][...]
    for part in parts[1:]:
        result = result + part[...]
    return result


def statistics(sums, count):
    center = sums[0:1] / count
    inverse = lax.rsqrt(sums[1:2] / count - center * center + eps_norm)
    return center, inverse


def add_rows(store, row, value):
    store[row * 8 : row * 8 + 8, :] += fold(value)


def finish_rows(store, out_ref, rows):
    for row in range(rows):
        out_ref[row : row + 1, :] = column_sum(store[row * 8 : row * 8 + 8, :])


def times(lhs, rhs):
    return lax.dot_general(lhs, rhs, (((1,), (0,)), ((), ())), preferred_element_type=full_type)


def times_back(lhs, rhs):
    return lax.dot_general(lhs, rhs, (((1,), (1,)), ((), ())), preferred_element_type=full_type)


def times_rows(lhs, rhs):
    return lax.dot_general(lhs, rhs, (((0,), (0,)), ((), ())), preferred_element_type=full_type)


def low(value):
    return value.astype(low_type)


def inside(rows, sides, size_ref, unit):
    images = size_ref.shape[1]
    place = lax.broadcasted_iota(jnp.int32, (rows, 128), 0)
    image = place % images
    bound = jnp.zeros((rows, 128), jnp.int32)
    for index in range(images):
        bound = jnp.where(image == index, size_ref[0, index] // unit, bound)
    pair = place // images
    over = pair % even_width * sides + pair // even_width % sides
    down = pair // (even_width * sides)
    return jnp.where((over < bound) & (down < bound), 1.0, 0.0)


def enter_body(images, x_ref, size_ref, filter_ref, start_ref, out_ref, sums_ref, mask_ref, small_ref, pixel_ref, store):
    height, pairs = x_ref.shape[0], x_ref.shape[1]
    depth = x_ref.shape[4]
    line = even_width * images
    blank = jnp.zeros((even_width - pairs, images, depth), low_type)
    store[...] = jnp.zeros_like(store)
    mask_ref[...] = inside(mask_ref.shape[0], 2, size_ref, 16)
    small_ref[...] = inside(small_ref.shape[0], 1, size_ref, 32)
    for index in range(images):
        bound = (size_ref[0, index] // 32).astype(full_type)
        pixel_ref[index : index + 1, :] = 1.0 / jnp.full((1, 128), bound * bound)

    def step(index, carry):
        rows = pl.ds(pl.multiple_of(index * 4 * line, 4 * line), 4 * line)
        parts = []
        for row in range(2):
            for side in range(2):
                cells = jnp.concatenate([x_ref[index * 2 + row, :, side], blank], axis=0)
                parts.append(cells.reshape(line, depth))
        value = jnp.concatenate(parts, axis=0).astype(full_type) * wide(mask_ref[rows, :], depth)
        value = low(value)
        start_ref[rows, :] = value
        result = times(value, filter_ref[...])
        out_ref[rows, :] = result
        add_rows(store, 0, result)
        add_rows(store, 1, result * result)
        return carry

    lax.fori_loop(0, height // 2, step, 0)
    finish_rows(store, sums_ref, 2)
    sums_ref[2:3, :] = wide(column_sum(fold(mask_ref[...])), sums_ref.shape[1])
    sums_ref[3:4, :] = wide(column_sum(fold(small_ref[...])), sums_ref.shape[1])


def split_store(even_ref, moved_ref, place, value, line):
    even, odd = value[:line], value[line:]
    even_ref[place, 0] = low(even)
    even_ref[place, 1] = low(odd)
    moved_ref[place, 0] = low(pltpu.roll(even, line - line // even_width, 0))
    moved_ref[place, 1] = low(pltpu.roll(odd, line // even_width, 0))


def blank_border(*refs):
    for ref in refs:
        empty = jnp.zeros(ref.shape[1:], ref.dtype)
        ref[0] = empty
        ref[ref.shape[0] - 1] = empty


def tap_sources(even_ref, moved_ref):
    return (
        ((moved_ref, 1), (even_ref, 0), (even_ref, 1)),
        ((even_ref, 0), (even_ref, 1), (moved_ref, 0)),
    )


def block_body(images, parts, u_ref, scale_ref, shift_ref, mask_ref, filter_ref, even_ref, moved_ref, out_ref, sums_ref, count_ref, store):
    depth = filter_ref.shape[1]
    line = even_width * images
    height = even_ref.shape[0] - 2
    sums = total(parts)
    count_ref[...] = sums[2:4, 0:128]
    center, inverse = statistics(sums, sums[2:3, 0:1])
    factor = scale_ref[...] * inverse
    shift = shift_ref[...]
    blank_border(even_ref, moved_ref)
    store[...] = jnp.zeros_like(store)

    def first(index, carry):
        rows = pl.ds(pl.multiple_of(index * 2 * line, 2 * line), 2 * line)
        pre = (u_ref[rows, :] - center) * factor + shift
        value = smooth(pre) * wide(mask_ref[rows, :], depth)
        split_store(even_ref, moved_ref, index + 1, value, line)
        return carry

    lax.fori_loop(0, height, first, 0)
    half = height // 2
    sources = tap_sources(even_ref, moved_ref)
    for side in range(2):
        for part in range(2):
            lhs = jnp.concatenate(
                [
                    ref[half * part + row : half * part + row + half, plane].reshape(half * line, depth)
                    for row in range(3)
                    for ref, plane in sources[side]
                ],
                axis=1,
            )
            result = times(lhs, filter_ref[...])
            for index in range(half):
                begin = (half * part + index) * 2 * line + side * line
                piece = result[index * line : index * line + line]
                out_ref[begin : begin + line, :] = piece
                kept = piece * wide(mask_ref[begin : begin + line, :], piece.shape[1])
                add_rows(store, 0, kept)
                add_rows(store, 1, kept * piece)
    finish_rows(store, sums_ref, 2)


def expand_body(parts, u_ref, count_ref, scale_ref, shift_ref, mask_ref, filter_ref, hidden_ref, out_ref, sums_ref, store, which, rows_step):
    center, inverse = statistics(total(parts), count_ref[which : which + 1, 0:1])
    factor = scale_ref[...] * inverse
    shift = shift_ref[...]
    depth = u_ref.shape[1]
    store[...] = jnp.zeros_like(store)

    def step(index, carry):
        rows = pl.ds(pl.multiple_of(index * rows_step, rows_step), rows_step)
        pre = (u_ref[rows, :] - center) * factor + shift
        value = low(smooth(pre) * wide(mask_ref[rows, :], depth))
        hidden_ref[rows, :] = value
        result = times(value, filter_ref[...])
        out_ref[rows, :] = result
        add_rows(store, 0, result)
        add_rows(store, 1, result * result)
        return carry

    lax.fori_loop(0, u_ref.shape[0] // rows_step, step, 0)
    finish_rows(store, sums_ref, 2)


def join_body(images, parts, u_ref, count_ref, scale_ref, shift_ref, mask_ref, start_ref, reduce_ref, side_ref, block_ref, reduced_ref, picked_ref, sided_ref, sums_ref, side_sums_ref, store, side_store):
    center, inverse = statistics(total(parts), count_ref[0:1, 0:1])
    factor = scale_ref[...] * inverse
    shift = shift_ref[...]
    depth = u_ref.shape[1]
    line = even_width * images
    store[...] = jnp.zeros_like(store)
    side_store[...] = jnp.zeros_like(side_store)

    def step(index, carry):
        rows = pl.ds(pl.multiple_of(index * 4 * line, 4 * line), 4 * line)
        pre = (u_ref[rows, :] - center) * factor + shift + start_ref[rows, :].astype(full_type)
        value = low(smooth(pre) * wide(mask_ref[rows, :], depth))
        block_ref[rows, :] = value
        picked_ref[pl.ds(pl.multiple_of(index * line, line), line), :] = value[:line]
        result = times(value, reduce_ref[...])
        reduced_ref[rows, :] = result
        add_rows(store, 0, result)
        add_rows(store, 1, result * result)
        return carry

    lax.fori_loop(0, u_ref.shape[0] // (4 * line), step, 0)
    finish_rows(store, sums_ref, 2)
    width = 512

    def side(index, carry):
        columns = pl.ds(pl.multiple_of(index * width, width), width)
        result = times(picked_ref[...], side_ref[:, columns])
        sided_ref[:, columns] = result
        side_sums_ref[0:1, columns] = column_sum(fold(result))
        side_sums_ref[1:2, columns] = column_sum(fold(result * result))
        return carry

    lax.fori_loop(0, side_ref.shape[1] // width, side, 0)


def shrink_body(images, parts, u_ref, count_ref, scale_ref, shift_ref, mask_ref, small_ref, filter_ref, even_ref, moved_ref, out_ref, sums_ref):
    depth = u_ref.shape[1]
    line = even_width * images
    height = even_ref.shape[0] - 2
    center, inverse = statistics(total(parts), count_ref[0:1, 0:1])
    factor = scale_ref[...] * inverse
    shift = shift_ref[...]
    blank_border(even_ref, moved_ref)

    def first(index, carry):
        rows = pl.ds(pl.multiple_of(index * 2 * line, 2 * line), 2 * line)
        pre = (u_ref[rows, :] - center) * factor + shift
        value = smooth(pre) * wide(mask_ref[rows, :], depth)
        split_store(even_ref, moved_ref, index + 1, value, line)
        return carry

    lax.fori_loop(0, height, first, 0)
    half = height // 2
    result = None
    for row in range(3):
        lhs = jnp.concatenate(
            [
                jnp.concatenate([ref[2 * index + row, plane] for index in range(half)], axis=0)
                for ref, plane in ((moved_ref, 1), (even_ref, 0), (even_ref, 1))
            ],
            axis=1,
        )
        term = times(lhs, filter_ref[row * 3 * depth : row * 3 * depth + 3 * depth, :])
        result = term if result is None else result + term
    out_ref[...] = result
    kept = result * wide(small_ref[...], result.shape[1])
    sums_ref[0:1, :] = column_sum(fold(kept))
    sums_ref[1:2, :] = column_sum(fold(kept * result))


def leave_body(images, parts, side_parts, u_ref, side_ref, count_ref, scale_ref, shift_ref, side_scale_ref, side_shift_ref, small_ref, pixel_ref, block_ref, joined_ref, pooled_ref, store):
    center, inverse = statistics(total(parts), count_ref[1:2, 0:1])
    factor = scale_ref[...] * inverse
    side_center, side_inverse = statistics(total(side_parts), count_ref[1:2, 0:1])
    side_factor = side_scale_ref[...] * side_inverse
    shift = shift_ref[...] + side_shift_ref[...]
    depth = u_ref.shape[1]
    line = even_width * images
    pairs = block_ref.shape[1]
    store[...] = jnp.zeros_like(store)

    def step(index, carry):
        rows = pl.ds(pl.multiple_of(index * line, line), line)
        pre = (u_ref[rows, :] - center) * factor + (side_ref[rows, :] - side_center) * side_factor + shift
        joined_ref[rows, :] = pre
        value = smooth(pre) * wide(small_ref[rows, :], depth)
        block_ref[index] = low(value).reshape(even_width, images, depth)[:pairs]
        add_rows(store, 0, value)
        return carry

    lax.fori_loop(0, u_ref.shape[0] // line, step, 0)
    summed = store[0:images, :]
    for begin in range(images, 8, images):
        summed = summed + store[begin : begin + images, :]
    pooled_ref[...] = summed * pixel_ref[:, 0:1]


def gather_images(store, row, images):
    summed = store[row * 8 : row * 8 + images, :]
    for begin in range(images, 8, images):
        summed = summed + store[row * 8 + begin : row * 8 + begin + images, :]
    return summed


def slope_sums_body(images, parts, side_parts, joined_ref, u_ref, side_ref, count_ref, small_ref, slope_ref, plain_ref, unit_ref, side_unit_ref, store):
    center, inverse = statistics(total(parts), count_ref[1:2, 0:1])
    side_center, side_inverse = statistics(total(side_parts), count_ref[1:2, 0:1])
    depth = u_ref.shape[1]
    line = even_width * images
    store[...] = jnp.zeros_like(store)

    def step(index, carry):
        rows = pl.ds(pl.multiple_of(index * line, line), line)
        slope = smooth_slope(joined_ref[rows, :]) * wide(small_ref[rows, :], depth)
        slope_ref[rows, :] = slope
        add_rows(store, 0, slope)
        add_rows(store, 1, slope * (u_ref[rows, :] - center))
        add_rows(store, 2, slope * (side_ref[rows, :] - side_center))
        return carry

    lax.fori_loop(0, u_ref.shape[0] // line, step, 0)
    plain_ref[...] = gather_images(store, 0, images)
    unit_ref[...] = gather_images(store, 1, images) * inverse
    side_unit_ref[...] = gather_images(store, 2, images) * side_inverse


def compare_body(pooled_ref, partner_ref, pixel_ref, plain_ref, unit_ref, side_unit_ref, loss_ref, grad_ref, sums_ref):
    pooled, partner = pooled_ref[...], partner_ref[...]
    inverse_own = lax.rsqrt(jnp.sum(pooled * pooled, axis=1, keepdims=True) + eps_cos)
    unit_own = pooled * inverse_own
    unit_other = partner * lax.rsqrt(jnp.sum(partner * partner, axis=1, keepdims=True) + eps_cos)
    cosine = jnp.sum(unit_own * unit_other, axis=1, keepdims=True)
    loss_ref[...] = jnp.broadcast_to(-0.5 * cosine, loss_ref.shape)
    grad = (-0.5 * loss_scale) * inverse_own * (unit_other - cosine * unit_own) * pixel_ref[:, 0:1]
    grad_ref[...] = grad
    sums_ref[0:1, :] = column_sum(grad * plain_ref[...])
    sums_ref[1:2, :] = column_sum(grad * unit_ref[...])
    sums_ref[2:3, :] = column_sum(grad * side_unit_ref[...])


def norm_back(sums, totals, count, scale):
    center, inverse = statistics(sums, count)
    factor = scale * inverse
    return center, inverse, factor, -(factor * inverse * totals[1:2] / count), -(factor * totals[0:1] / count)


def leave_back_body(images, parts, side_parts, grads, slope_ref, grad_ref, u_ref, side_ref, count_ref, scale_ref, side_scale_ref, small_ref, filter_ref, inner_parts, inner_u_ref, inner_slope_ref, low_ref, side_low_ref, out_ref, sums_ref, store):
    totals = total(grads)
    count = count_ref[1:2, 0:1]
    center, _, factor, along, level = norm_back(total(parts), totals, count, scale_ref[...])
    side_totals = jnp.concatenate([totals[0:1], totals[2:3]], axis=0)
    side_center, _, side_factor, side_along, side_level = norm_back(total(side_parts), side_totals, count, side_scale_ref[...])
    depth = u_ref.shape[1]
    line = even_width * images
    grad = jnp.concatenate([grad_ref[...]] * (line // images), axis=0)

    def step(index, carry):
        rows = pl.ds(pl.multiple_of(index * line, line), line)
        mask = wide(small_ref[rows, :], depth)
        joined = slope_ref[rows, :] * grad
        low_ref[rows, :] = low((joined * factor + (u_ref[rows, :] - center) * along + level) * mask)
        side_low_ref[rows, :] = low((joined * side_factor + (side_ref[rows, :] - side_center) * side_along + side_level) * mask)
        return carry

    lax.fori_loop(0, u_ref.shape[0] // line, step, 0)
    inner_center, inner_inverse = statistics(total(inner_parts), count)
    result = times_back(low_ref[...], filter_ref[...]) * inner_slope_ref[...]
    out_ref[...] = result
    sums_ref[0:1, :] = column_sum(fold(result))
    sums_ref[1:2, :] = column_sum(fold(result * (inner_u_ref[...] - inner_center))) * inner_inverse


def shrink_back_body(images, parts, grads, g_ref, u_ref, count_ref, scale_ref, small_ref, filter_ref, inner_parts, inner_u_ref, inner_slope_ref, low_ref, out_ref, sums_ref, store):
    depth = u_ref.shape[1]
    inner = filter_ref.shape[2]
    line = even_width * images
    half = u_ref.shape[0] // line
    center, _, factor, along, level = norm_back(total(parts), total(grads), count_ref[1:2, 0:1], scale_ref[...])
    exact = (g_ref[...] * factor + (u_ref[...] - center) * along + level) * wide(small_ref[...], depth)
    here = low(exact)
    low_ref[...] = here
    right = low(pltpu.roll(exact, exact.shape[0] - images, 0))
    blank = jnp.zeros((line, depth), low_type)
    below = jnp.concatenate([here[line:], blank], axis=0)
    below_right = jnp.concatenate([right[line:], blank], axis=0)
    inner_center, inner_inverse = statistics(total(inner_parts), count_ref[0:1, 0:1])
    store[...] = jnp.zeros_like(store)
    for row in range(2):
        for side in range(2):
            terms = [(here, 1 + row, 1 + side)]
            if side:
                terms.append((right, 1 + row, 0))
            if row:
                terms.append((below, 0, 1 + side))
            if row and side:
                terms.append((below_right, 0, 0))
            lhs = jnp.concatenate([value for value, _, _ in terms], axis=1)
            rhs = jnp.concatenate([filter_ref[down * 3 + over] for _, down, over in terms], axis=1)
            result = times_back(lhs, rhs)
            for index in range(half):
                begin = (index * 4 + row * 2 + side) * line
                rows = slice(begin, begin + line)
                piece = result[index * line : index * line + line] * inner_slope_ref[rows, :]
                out_ref[rows, :] = piece
                add_rows(store, 0, piece)
                add_rows(store, 1, piece * (inner_u_ref[rows, :] - inner_center))
    sums_ref[0:1, :] = column_sum(store[0:8, :])
    sums_ref[1:2, :] = column_sum(store[8:16, :]) * inner_inverse


def join_back_body(images, parts, grads, g_ref, u_ref, count_ref, scale_ref, mask_ref, filter_ref, picked_ref, inner_parts, inner_u_ref, inner_slope_ref, low_ref, out_ref, sums_ref, store):
    depth = u_ref.shape[1]
    line = even_width * images
    center, _, factor, along, level = norm_back(total(parts), total(grads), count_ref[0:1, 0:1], scale_ref[...])
    inner_center, inner_inverse = statistics(total(inner_parts), count_ref[0:1, 0:1])
    store[...] = jnp.zeros_like(store)

    def step(index, carry):
        rows = pl.ds(pl.multiple_of(index * 4 * line, 4 * line), 4 * line)
        value = low((g_ref[rows, :] * factor + (u_ref[rows, :] - center) * along + level) * wide(mask_ref[rows, :], depth))
        low_ref[rows, :] = value
        result = times_back(value, filter_ref[...])
        extra = picked_ref[pl.ds(pl.multiple_of(index * line, line), line), :]
        result = jnp.concatenate([result[:line] + extra, result[line:]], axis=0) * inner_slope_ref[rows, :]
        out_ref[rows, :] = result
        add_rows(store, 0, result)
        add_rows(store, 1, result * (inner_u_ref[rows, :] - inner_center))
        return carry

    lax.fori_loop(0, u_ref.shape[0] // (4 * line), step, 0)
    sums_ref[0:1, :] = column_sum(store[0:8, :])
    sums_ref[1:2, :] = column_sum(store[8:16, :]) * inner_inverse


def expand_back_body(parts, grads, g_ref, u_ref, count_ref, scale_ref, mask_ref, filter_ref, inner_parts, inner_u_ref, inner_slope_ref, low_ref, out_ref, sums_ref, store, rows_step):
    depth = u_ref.shape[1]
    center, _, factor, along, level = norm_back(total(parts), total(grads), count_ref[0:1, 0:1], scale_ref[...])
    inner_center, inner_inverse = statistics(total(inner_parts), count_ref[0:1, 0:1])
    store[...] = jnp.zeros_like(store)

    def step(index, carry):
        rows = pl.ds(pl.multiple_of(index * rows_step, rows_step), rows_step)
        value = low((g_ref[rows, :] * factor + (u_ref[rows, :] - center) * along + level) * wide(mask_ref[rows, :], depth))
        low_ref[rows, :] = value
        result = times_back(value, filter_ref[...]) * inner_slope_ref[rows, :]
        out_ref[rows, :] = result
        add_rows(store, 0, result)
        add_rows(store, 1, result * (inner_u_ref[rows, :] - inner_center))
        return carry

    lax.fori_loop(0, u_ref.shape[0] // rows_step, step, 0)
    sums_ref[0:1, :] = column_sum(store[0:8, :])
    sums_ref[1:2, :] = column_sum(store[8:16, :]) * inner_inverse


def block_back_body(images, parts, grads, g_ref, u_ref, count_ref, scale_ref, mask_ref, filter_ref, inner_parts, inner_u_ref, inner_slope_ref, low_ref, out_ref, sums_ref, even_ref, moved_ref, store):
    depth = u_ref.shape[1]
    line = even_width * images
    height = even_ref.shape[0] - 2
    center, _, factor, along, level = norm_back(total(parts), total(grads), count_ref[0:1, 0:1], scale_ref[...])
    inner_center, inner_inverse = statistics(total(inner_parts), count_ref[0:1, 0:1])
    blank_border(even_ref, moved_ref)
    store[...] = jnp.zeros_like(store)

    def first(index, carry):
        rows = pl.ds(pl.multiple_of(index * 2 * line, 2 * line), 2 * line)
        value = (g_ref[rows, :] * factor + (u_ref[rows, :] - center) * along + level) * wide(mask_ref[rows, :], depth)
        low_ref[rows, :] = low(value)
        split_store(even_ref, moved_ref, index + 1, value, line)
        return carry

    lax.fori_loop(0, height, first, 0)
    half = height // 2
    sources = tap_sources(even_ref, moved_ref)
    rhs = jnp.concatenate([filter_ref[8 - tap] for tap in range(9)], axis=1)
    for side in range(2):
        for part in range(2):
            lhs = jnp.concatenate(
                [
                    ref[half * part + row : half * part + row + half, plane].reshape(half * line, depth)
                    for row in range(3)
                    for ref, plane in sources[side]
                ],
                axis=1,
            )
            result = times_back(lhs, rhs)
            for index in range(half):
                begin = (half * part + index) * 2 * line + side * line
                rows = slice(begin, begin + line)
                piece = result[index * line : index * line + line] * inner_slope_ref[rows, :]
                out_ref[rows, :] = piece
                add_rows(store, 0, piece)
                add_rows(store, 1, piece * (inner_u_ref[rows, :] - inner_center))
    sums_ref[0:1, :] = column_sum(store[0:8, :])
    sums_ref[1:2, :] = column_sum(store[8:16, :]) * inner_inverse


def exit_body(images, parts, grads, g_ref, u_ref, count_ref, scale_ref, mask_ref, filter_ref, joined_ref, low_ref, out_ref):
    depth = u_ref.shape[1]
    pairs = out_ref.shape[1]
    line = even_width * images
    center, _, factor, along, level = norm_back(total(parts), total(grads), count_ref[0:1, 0:1], scale_ref[...])

    def step(index, carry):
        rows = pl.ds(pl.multiple_of(index * 4 * line, 4 * line), 4 * line)
        mask = mask_ref[rows, :]
        value = low((g_ref[rows, :] * factor + (u_ref[rows, :] - center) * along + level) * wide(mask, depth))
        low_ref[rows, :] = value
        result = low((times_back(value, filter_ref[...]) + joined_ref[rows, :]) * wide(mask, joined_ref.shape[1]))
        for row in range(2):
            for side in range(2):
                begin = (row * 2 + side) * line
                cells = result[begin : begin + line].reshape(even_width, images, result.shape[1])
                out_ref[index * 2 + row, :, side] = cells[:pairs]
        return carry

    lax.fori_loop(0, u_ref.shape[0] // (4 * line), step, 0)


def natural_body(images, value_ref, out_ref):
    pairs = out_ref.shape[1]
    line = even_width * images
    depth = value_ref.shape[1]

    def step(index, carry):
        for side in range(2):
            rows = pl.ds(pl.multiple_of(index * 2 * line + side * line, line), line)
            out_ref[index, :, side] = value_ref[rows, :].reshape(even_width, images, depth)[:pairs]
        return carry

    lax.fori_loop(0, out_ref.shape[0], step, 0)


def slope_body(parts, u_ref, count_ref, scale_ref, shift_ref, mask_ref, extras, out_ref, which, rows_step):
    center, inverse = statistics(total(parts), count_ref[which : which + 1, 0:1])
    factor = scale_ref[...] * inverse
    shift = shift_ref[...]
    depth = u_ref.shape[1]

    def step(index, carry):
        rows = pl.ds(pl.multiple_of(index * rows_step, rows_step), rows_step)
        pre = (u_ref[rows, :] - center) * factor + shift
        for extra_ref in extras:
            pre = pre + extra_ref[rows, :].astype(full_type)
        out_ref[rows, :] = low(smooth_slope(pre) * wide(mask_ref[rows, :], depth))
        return carry

    lax.fori_loop(0, u_ref.shape[0] // rows_step, step, 0)


def times_back_body(value_ref, filter_ref, out_ref):
    out_ref[...] = times_back(value_ref[...], filter_ref[...])


def window_start(device, share_size, width):
    return (device * share_size) // (8 * width) * 8


def window_rows(share_size, width):
    return -(-(share_size + 8 * width) // (16 * width)) * 16


def low_rows(rows):
    part = rows * halved_of_128 // 2048 * 8
    return [part, part, rows - 2 * part]


def copy_windows(source, outs, sems, first_device, first_row, share_size, offsets):
    owners, _, width = outs[0].shape
    pieces = len(offsets)
    core = lax.axis_index("dp") % 2
    copies = []
    for piece in range(pieces):
        for which, chosen in enumerate((1 - core, core)):
            out = outs[which * pieces + piece]
            for owner in range(owners):
                begin = window_start(first_device + 2 * owner + chosen, share_size, width) - first_row + offsets[piece]
                rows_here = pl.ds(pl.multiple_of(begin, 8), out.shape[1])
                copies.append(pltpu.make_async_copy(source.at[rows_here], out.at[owner], sems.at[len(copies)]))
    for copy in copies:
        copy.start()
    for copy in copies:
        copy.wait()


def put_filter(store, begin, value, grad):
    step, across = 256, min(512, grad.shape[1])
    lanes = store.shape[1]
    cuts = grad.shape[1] // lanes
    for row in range(0, value.shape[1], step):
        for column in range(0, grad.shape[1], across):
            result = times_rows(value[:, row : row + step], grad[:, column : column + across])
            for cut in range(across // lanes):
                place = begin + row * cuts + column // lanes + cut
                store[pl.ds(place, step, stride=cuts), :] = result[:, cut * lanes : cut * lanes + lanes]
    return begin + value.shape[1] * cuts


def late_filters_body(first_device, first_row, share_size, hidden_ref, picked_ref, low_ref, side_low_ref, *rest):
    *outs, spill_ref, store, sems = rest
    filled = put_filter(store, 0, hidden_ref, low_ref)
    filled = put_filter(store, filled, picked_ref, side_low_ref)
    store[filled:, :] = jnp.zeros((store.shape[0] - filled, store.shape[1]), full_type)
    spill_ref[...] = store[: spill_ref.shape[0], :]
    view = lax.axis_index("view")
    rows = outs[0].shape[1]
    copy_windows(store, outs, sems, first_device, first_row, share_size, ((1 - view) * rows, view * rows))


def middle_filters_body(share_size, block_ref, low_ref, even_ref, moved_ref, inner_low_ref, spill_ref, *rest):
    *outs, store, sems = rest
    filled = put_filter(store, 0, block_ref, low_ref)
    half = even_ref.shape[0] // 2 - 1
    for row in range(3):
        for ref, plane in ((moved_ref, 1), (even_ref, 0), (even_ref, 1)):
            lhs = jnp.concatenate([ref[2 * index + row, plane] for index in range(half)], axis=0)
            filled = put_filter(store, filled, lhs, inner_low_ref)
    store[filled:, :] = spill_ref[...]
    view = lax.axis_index("view")
    rows = outs[0].shape[1]
    copy_windows(store, outs, sems, 0, 0, share_size, ((1 - view) * rows, view * rows, 2 * rows))


def block_filter_body(even_ref, moved_ref, inner_low_ref, hidden_ref, outer_low_ref, out_ref):
    height, _, line, inner = even_ref.shape
    height = height - 2
    width = inner_low_ref.shape[1]
    grad = inner_low_ref[...].reshape(height, 2, line, width)
    grad = jnp.concatenate([grad[:, side].reshape(height * line, width) for side in range(2)], axis=0)
    sources = tap_sources(even_ref, moved_ref)
    filled = 0
    for row in range(3):
        for over in range(3):
            lhs = jnp.concatenate(
                [
                    sources[side][over][0][row : row + height, sources[side][over][1]].reshape(height * line, inner)
                    for side in range(2)
                ],
                axis=0,
            )
            filled = put_filter(out_ref, filled, lhs, grad)
    put_filter(out_ref, filled, hidden_ref, outer_low_ref)


def early_filters_body(share_size, start_ref, low_ref, later_ref, *rest):
    *outs, store, sems = rest
    filled = put_filter(store, 0, start_ref, low_ref)
    later = later_ref.shape[0]
    store[filled : filled + later, :] = later_ref[...]
    filled += later
    store[filled:, :] = jnp.zeros((store.shape[0] - filled, store.shape[1]), full_type)
    copy_windows(store, outs, sems, 0, 0, share_size, (0,))


def exchange(value, axis, bits):
    return lax.ppermute(value, axis, [(i, i ^ bits) for i in range(lax.axis_size(axis))])


def share(sums):
    size = lax.axis_size("dp")
    if size > 1:
        sums = sums + exchange(sums, "dp", 1)
    if size > 2:
        sums = sums + exchange(sums, "dp", 3)
    parts = (sums,)
    bit = 4
    while bit < size:
        if len(parts) > 1:
            parts = (sum(parts[1:], parts[0]),)
        steps = [bit + 1, 2 * bit + 1, 3 * bit + 1] if 2 * bit < size else [bit + 1]
        parts = parts + tuple(exchange(parts[0], "dp", step) for step in steps)
        bit *= 4
    return parts


def own_bit(axis, bit):
    return (lax.axis_index(axis) >> bit) & 1


class Windows:
    def __init__(self, kept, received, bits):
        self.kept, self.received, self.bits = kept, received, list(bits)

    def step(self, item, *gates):
        axis, bit = item
        place = self.bits.index(item)
        own = own_bit(axis, bit)
        rows, width = self.kept.shape[1:]
        before, after = 1 << place, 1 << (len(self.bits) - place - 1)

        def pick(value, index):
            cut = value.reshape(before, 2, after, rows, width)
            part = lax.dynamic_slice(cut, (0, index, 0, 0, 0), (before, 1, after, rows, width))
            return part.reshape(before * after, rows, width)

        self.sent = pick(self.kept, 1 - own) + pick(self.received, 1 - own) + sum(gates, 0.0)
        self.kept = pick(self.kept, own) + pick(self.received, own)
        self.received = exchange(self.sent, axis, 1 << bit)
        self.bits.pop(place)

    def total(self):
        return (self.kept + self.received)[0]


def gate(value):
    corner = value[(slice(0, 1),) * (value.ndim - 1) + (slice(0, 128),)]
    return 0.0 * corner.reshape(1, 1, 128)


def per_device(
    inputs,
    resolution,
    reduce_a,
    spatial_a,
    expand_a,
    reduce_b,
    spatial_b,
    expand_b,
    shortcut_b,
    scale_reduce_a,
    shift_reduce_a,
    scale_spatial_a,
    shift_spatial_a,
    scale_expand_a,
    shift_expand_a,
    scale_reduce_b,
    shift_reduce_b,
    scale_spatial_b,
    shift_spatial_b,
    scale_expand_b,
    shift_expand_b,
    scale_shortcut,
    shift_shortcut,
):
    images, height, depth_a = inputs.shape[1], inputs.shape[2], inputs.shape[4]
    pairs = height // 2
    middle_a, middle_b, depth_b = reduce_a.shape[1], reduce_b.shape[1], shortcut_b.shape[1]
    line = even_width * images
    rows_big, rows_small = height * 2 * line, pairs * line
    spatial_a9 = spatial_a.reshape(9, middle_a, middle_a)
    spatial_b9 = spatial_b.reshape(9, middle_b, middle_b)
    cells = inputs[0].transpose(1, 2, 0, 3).reshape(height, pairs, 2, images, depth_a)

    vectors = [
        (scale_reduce_a, shift_reduce_a),
        (scale_spatial_a, shift_spatial_a),
        (scale_expand_a, shift_expand_a),
        (scale_reduce_b, shift_reduce_b),
        (scale_spatial_b, shift_spatial_b),
        (scale_expand_b, shift_expand_b),
        (scale_shortcut, shift_shortcut),
    ]
    packed = jnp.stack([jnp.pad(vector, (0, depth_b - vector.size)) for pair in vectors for vector in pair])

    def affine(index):
        width = vectors[index][0].size
        return tuple(View(packed, (row, row + 1), (0, width)) for row in (2 * index, 2 * index + 1))

    def padded(width):
        return shaped(height + 2, 2, line, width, kind=low_type)

    def with_images(body):
        return functools.partial(body, images)

    start, reduced_a, sums, mask_big, mask_small, pixel = call(
        with_images(enter_body),
        [
            shaped(rows_big, depth_a, kind=low_type),
            shaped(rows_big, middle_a),
            shaped(4, middle_a),
            shaped(rows_big, 128),
            shaped(rows_small, 128),
            shaped(images, 128),
        ],
        [cells, resolution, reduce_a],
        scratch=[((16, middle_a), full_type)],
        scalars=(1,),
    )
    sums_ra = share(sums)
    scale_ra, shift_ra = affine(0)
    even_a, moved_a, mixed_a, sums, counts = call(
        with_images(block_body),
        [padded(middle_a), padded(middle_a), shaped(rows_big, middle_a), shaped(2, middle_a), shaped(2, 128)],
        [sums_ra, reduced_a, scale_ra, shift_ra, mask_big, spatial_a.reshape(9 * middle_a, middle_a)],
        scratch=[((16, middle_a), full_type)],
    )
    def slope(parts, value, scale, shift, mask, extras, which, rows_step):
        return call(
            functools.partial(slope_body, which=which, rows_step=rows_step),
            [shaped(*value.shape, kind=low_type)],
            [parts, value, counts, scale, shift, mask, extras],
        )[0]

    slope_ra = slope(sums_ra, reduced_a, scale_ra, shift_ra, mask_big, (), 0, 2 * line)
    sums_sa = share(sums)
    scale_sa, shift_sa = affine(1)
    hidden_two_a, expanded_a, sums = call(
        functools.partial(expand_body, which=0, rows_step=4 * line),
        [shaped(rows_big, middle_a, kind=low_type), shaped(rows_big, depth_a), shaped(2, depth_a)],
        [sums_sa, mixed_a, counts, scale_sa, shift_sa, mask_big, expand_a],
        scratch=[((16, depth_a), full_type)],
        after=(slope_ra,),
    )
    slope_sa = slope(sums_sa, mixed_a, scale_sa, shift_sa, mask_big, (), 0, 2 * line)
    sums_ea = share(sums)
    scale_ea, shift_ea = affine(2)
    block_a, reduced_b, picked, side_b, sums, side_sums = call(
        with_images(join_body),
        [
            shaped(rows_big, depth_a, kind=low_type),
            shaped(rows_big, middle_b),
            shaped(rows_small, depth_a, kind=low_type),
            shaped(rows_small, depth_b),
            shaped(2, middle_b),
            shaped(2, depth_b),
        ],
        [sums_ea, expanded_a, counts, scale_ea, shift_ea, mask_big, start, reduce_b, shortcut_b],
        scratch=[((16, middle_b), full_type), ((16, 128), full_type)],
        after=(slope_sa,),
    )
    slope_ea = slope(sums_ea, expanded_a, scale_ea, shift_ea, mask_big, (start,), 0, 2 * line)
    shared = share(jnp.concatenate([sums, side_sums], axis=1))
    sums_rb = tuple(View(part, (0, 2), (0, middle_b)) for part in shared)
    sums_sc = tuple(View(part, (0, 2), (middle_b, middle_b + depth_b)) for part in shared)
    scale_rb, shift_rb = affine(3)
    scale_sc, shift_sc = affine(6)
    even_b, moved_b, mixed_b, sums = call(
        with_images(shrink_body),
        [padded(middle_b), padded(middle_b), shaped(rows_small, middle_b), shaped(2, middle_b)],
        [sums_rb, reduced_b, counts, scale_rb, shift_rb, mask_big, mask_small, spatial_b.reshape(9 * middle_b, middle_b)],
        after=(slope_ea,),
    )
    block_out = call(
        with_images(natural_body), [shaped(height, pairs, 2, images, depth_a, kind=low_type)], [block_a]
    )[0]
    slope_rb = slope(sums_rb, reduced_b, scale_rb, shift_rb, mask_big, (), 0, 2 * line)
    sums_sb = share(sums)
    scale_sb, shift_sb = affine(4)
    hidden_two_b, expanded_b, sums = call(
        functools.partial(expand_body, which=1, rows_step=line),
        [shaped(rows_small, middle_b, kind=low_type), shaped(rows_small, depth_b), shaped(2, depth_b)],
        [sums_sb, mixed_b, counts, scale_sb, shift_sb, mask_small, expand_b],
        scratch=[((16, depth_b), full_type)],
        after=(slope_rb, block_out),
    )
    slope_sb = slope(sums_sb, mixed_b, scale_sb, shift_sb, mask_small, (), 1, line)
    sums_eb = share(sums)
    scale_eb, shift_eb = affine(5)
    block_b, joined_b, pooled = call(
        with_images(leave_body),
        [shaped(pairs, pairs, images, depth_b, kind=low_type), shaped(rows_small, depth_b), shaped(images, depth_b)],
        [sums_eb, sums_sc, expanded_b, side_b, counts, scale_eb, shift_eb, scale_sc, shift_sc, mask_small, pixel],
        scratch=[((8, depth_b), full_type)],
        after=(slope_sb,),
    )
    partner = exchange(pooled, "view", 1)
    slope_b, plain, unit, side_unit = call(
        with_images(slope_sums_body),
        [shaped(rows_small, depth_b)] + [shaped(images, depth_b)] * 3,
        [sums_eb, sums_sc, joined_b, expanded_b, side_b, counts, mask_small],
        scratch=[((24, depth_b), full_type)],
    )
    loss, grad_out, sums = call(
        compare_body,
        [shaped(images, 128), shaped(images, depth_b), shaped(3, depth_b)],
        [pooled, partner, pixel, plain, unit, side_unit],
    )
    grads_eb = share(sums)

    size = lax.axis_size("dp")
    half = size // 2
    bits = [("dp", bit) for bit in range(size.bit_length() - 2, 0, -1)]
    low_first = sorted(bits, key=lambda item: item[1])
    high_first = low_first[1:] + low_first[:1]
    lanes = 128
    first_rows = (depth_a + 9 * middle_b) * middle_b // lanes
    norm_rows_b = (4 * middle_b + 4 * depth_b) // lanes
    total_b = first_rows + (middle_b + depth_a) * depth_b // lanes + norm_rows_b
    share_b = total_b * lanes // (2 * size)
    window_b = window_rows(share_b, lanes)
    end_low = window_start(size - 1, share_b, lanes) + window_b
    end_high = window_start(2 * size - 1, share_b, lanes) + window_b

    def windows(count, pieces):
        return [pltpu.HBM((count, piece, lanes), full_type) for piece in pieces] * 2

    def pairs_of(outs):
        count = len(outs) // 2
        return [(kept, exchange(send, "dp", 1)) for send, kept in zip(outs[:count], outs[count:])]

    low_eb, low_sc, grad_sb, sums = call(
        with_images(leave_back_body),
        [
            shaped(rows_small, depth_b, kind=low_type),
            shaped(rows_small, depth_b, kind=low_type),
            shaped(rows_small, middle_b),
            shaped(2, middle_b),
        ],
        [
            sums_eb,
            sums_sc,
            grads_eb,
            slope_b,
            grad_out,
            expanded_b,
            side_b,
            counts,
            scale_eb,
            scale_sc,
            mask_small,
            expand_b,
            sums_sb,
            mixed_b,
            slope_sb,
        ],
        scratch=[((8, 128), full_type)],
    )
    grads_sb = share(sums)
    *outs, spill = call(
        functools.partial(late_filters_body, size, first_rows, share_b),
        windows(half, [window_b // 2] * 2) + [shaped(end_low - first_rows, lanes)],
        [hidden_two_b, picked, low_eb, low_sc],
        scratch=[((end_high - first_rows, lanes), full_type)],
        copies=4 * half,
        vmem=vmem_large,
        cost_us=cost_large,
        after=(grads_sb[0],),
    )
    grad_picked = call(times_back_body, [shaped(rows_small, depth_a)], [low_sc, shortcut_b])[0]
    far, near = pairs_of(outs)
    far_sum = far[0] + far[1]
    high = Windows(near[0] + near[1], exchange(far_sum, "view", 1), bits)
    low_sb, grad_rb, sums = call(
        with_images(shrink_back_body),
        [shaped(rows_small, middle_b, kind=low_type), shaped(rows_big, middle_b), shaped(2, middle_b)],
        [sums_sb, grads_sb, grad_sb, mixed_b, counts, scale_sb, mask_small, spatial_b9, sums_rb, reduced_b, slope_rb],
        scratch=[((16, middle_b), full_type)],
        after=(far_sum, grad_picked),
    )
    grads_rb = share(sums)
    low_rb, joined_grad, sums = call(
        with_images(join_back_body),
        [shaped(rows_big, middle_b, kind=low_type), shaped(rows_big, depth_a), shaped(2, depth_a)],
        [sums_rb, grads_rb, grad_rb, reduced_b, counts, scale_rb, mask_big, reduce_b, grad_picked, sums_ea, expanded_a, slope_ea],
        scratch=[((16, depth_a), full_type)],
    )
    grads_ea = share(sums)
    low_ea, grad_sa, sums = call(
        functools.partial(expand_back_body, rows_step=4 * line),
        [shaped(rows_big, depth_a, kind=low_type), shaped(rows_big, middle_a), shaped(2, middle_a)],
        [sums_ea, grads_ea, joined_grad, expanded_a, counts, scale_ea, mask_big, expand_a, sums_sa, mixed_a, slope_sa],
        scratch=[((16, middle_a), full_type)],
    )
    grads_sa = share(sums)
    outs = call(
        functools.partial(middle_filters_body, share_b),
        windows(half, low_rows(window_b)),
        [block_a, low_rb, even_b, moved_b, low_sb, spill],
        scratch=[((end_low, lanes), full_type)],
        copies=6 * half,
        vmem=vmem_large,
        cost_us=cost_large,
        after=(grads_ea[0],),
    )
    far, near, whole = pairs_of(outs)
    far_sum = far[0] + far[1]
    low_half = Windows(near[0] + near[1], exchange(far_sum, "view", 1), bits)
    low_whole = Windows(*whole, bits)
    low_sa, grad_ra, sums = call(
        with_images(block_back_body),
        [shaped(rows_big, middle_a, kind=low_type), shaped(rows_big, middle_a), shaped(2, middle_a)],
        [sums_sa, grads_sa, grad_sa, mixed_a, counts, scale_sa, mask_big, spatial_a9, sums_ra, reduced_a, slope_ra],
        scratch=[
            ((height + 2, 2, line, middle_a), low_type),
            ((height + 2, 2, line, middle_a), low_type),
            ((16, middle_a), full_type),
        ],
        after=(far_sum, high.received),
    )
    grads_ra = share(sums)
    ready, x_bit, z_bits = [], low_first[:1], low_first[1:]
    if bits:
        x_bit = x_bit[0]
        high.step(x_bit, gate(grads_ra[0]))
        low_whole.step(z_bits[0] if z_bits else x_bit, *(gate(part) for part in grads_ra[1:]))
        ready = [high.sent, low_whole.sent]
    low_ra, input_grad = call(
        with_images(exit_body),
        [shaped(rows_big, middle_a, kind=low_type), shaped(height, pairs, 2, images, depth_a, kind=low_type)],
        [sums_ra, grads_ra, grad_ra, reduced_a, counts, scale_ra, mask_big, reduce_a, joined_grad],
        after=ready,
    )
    norm_rows_a = (4 * middle_a + 2 * depth_a) // lanes
    total_a = (depth_a * 2 + 9 * middle_a) * middle_a // lanes + norm_rows_a
    share_a = total_a * lanes // (2 * size)
    window_a = window_rows(share_a, lanes)
    end_a = window_start(2 * size - 1, share_a, lanes) + window_a
    later = call(
        block_filter_body,
        [shaped((total_a - norm_rows_a) - depth_a * middle_a // lanes, lanes)],
        [even_a, moved_a, low_sa, hidden_two_a, low_ea],
        cost_us=cost_large,
    )[0]
    outs = call(
        functools.partial(early_filters_body, share_a),
        windows(size, [window_a]),
        [start, low_ra, later],
        scratch=[((end_a, lanes), full_type)],
        copies=2 * size,
        vmem=2 * vmem_small,
        cost_us=cost_large,
        after=(low_half.received,),
    )
    early = Windows(*pairs_of(outs)[0], [("view", 0)] + bits)
    early.step(("view", 0))
    if z_bits:
        high.step(z_bits[0])
        low_whole.step(x_bit)
        low_half.step(x_bit, gate(low_whole.sent))
        for item in z_bits[1:]:
            high.step(item)
            low_whole.step(item)
        early.step(x_bit, gate(low_half.sent))
        low_half.step(z_bits[0], gate(high.sent))
        early.step(z_bits[0], gate(low_half.sent))
        for item in z_bits[1:]:
            low_half.step(item)
            early.step(item)
    elif bits:
        low_half.step(x_bit)
        early.step(x_bit)
    early_window = early.total()
    view = lax.axis_index("view")
    all_grads = [sum(parts[1:], parts[0]) for parts in (grads_rb, grads_sb, grads_eb, grads_ra, grads_sa, grads_ea)]
    norms = jnp.concatenate([value.reshape(-1, lanes) for value in all_grads], axis=0)
    norms = norms + exchange(norms + gate(early.received)[0], "view", 1)
    high_half, low_half, low_rest = high.total(), low_half.total(), low_whole.total()
    short = low_half.shape[0] + low_rest.shape[0] - high_half.shape[0]
    swapped = exchange(
        jnp.where(
            view == 0, jnp.pad(high_half, ((0, short), (0, 0))), jnp.concatenate([low_half, low_rest], axis=0)
        ),
        "view",
        1,
    )
    late_window = jnp.where(
        view == 0,
        jnp.concatenate([low_half, swapped[: low_half.shape[0]], low_rest + swapped[low_half.shape[0] :]], axis=0),
        jnp.concatenate([swapped[: high_half.shape[0]], high_half], axis=0),
    )
    cut = []
    for value in all_grads:
        rows = value.size // lanes
        cut.append(norms[:rows].reshape(value.shape))
        norms = norms[rows:]
    norms_b = [cut[0], cut[1], cut[2][:2], cut[2][0], cut[2][2]]
    norms_a = cut[3:]
    device = lax.axis_index("view") * size + lax.axis_index("dp")

    def finish(window, norms, rows, norm_rows, share_size):
        width = window.shape[1]
        place = rows - norm_rows - window_start(2 * size - 1, share_size, width)
        values = jnp.concatenate([value.reshape(-1) for value in norms]).reshape(norm_rows, width)
        values = jnp.where(device == 2 * size - 1, values, 0.0)
        window = window + jnp.pad(values, ((place, window.shape[0] - place - norm_rows), (0, 0)))
        begin = device * share_size - window_start(device, share_size, width) * width
        return lax.dynamic_slice(window.reshape(-1), (begin,), (share_size,))

    late_done = finish(late_window, norms_b, total_b, norm_rows_b, share_b)
    early_done = finish(early_window, norms_a, total_a, norm_rows_a, share_a)

    def natural(value):
        return value.reshape(height, height, images, depth_a).transpose(2, 0, 1, 3)[None]

    return (
        loss[:, 0][None],
        natural(block_out),
        block_b.transpose(2, 0, 1, 3)[None],
        natural(input_grad),
        early_done,
        late_done,
    )


def solution(mesh):
    copied = (P(),) * 21
    images = P("view", "dp", None, None, None)
    packed = P(("view", "dp"))
    return jax.shard_map(
        per_device,
        mesh=mesh,
        in_specs=(images, P("view", "dp")) + copied,
        out_specs=(P("view", "dp"), images, images, images, packed, packed),
        check_vma=False,
    )
```

```python
import functools

import jax
import jax.numpy as jnp
from jax import lax
from jax.experimental import pallas as pl
from jax.experimental.pallas import tpu as pltpu
from jax.sharding import PartitionSpec as P

eps_norm = 1e-05
eps_cos = 1e-06
loss_scale = 65536.0
low_type = jnp.bfloat16
full_type = jnp.float32
vmem_small, vmem_large = 6 * 1024 * 1024, 18 * 1024 * 1024
cost_small = 0.1

even_width = 8


class View:
    def __init__(self, value, rows, columns):
        self.value, self.rows, self.columns = value, slice(*rows), slice(*columns)


def call(body, outs, args, cost_us=cost_small, scratch=(), copies=0, vmem=vmem_small, after=(), scalars=()):
    whole = pl.BlockSpec(memory_space=pltpu.VMEM)
    placed = [pl.BlockSpec(memory_space=pltpu.HBM) if copies and len(out.shape) == 3 else whole for out in outs]
    flat, places = [], {}

    def place(item):
        value = item.value if isinstance(item, View) else item
        if id(value) not in places:
            places[id(value)] = len(flat)
            flat.append(value)
        return places[id(value)]

    for item in args:
        for one in item if isinstance(item, tuple) else (item,):
            place(one)

    def run(*refs):
        def found(item):
            if isinstance(item, tuple):
                return tuple(found(one) for one in item)
            ref = refs[place(item)]
            return ref.at[item.rows, item.columns] if isinstance(item, View) else ref

        body(*[found(item) for item in args], *refs[len(flat) + len(after) :])

    return pl.pallas_call(
        run,
        out_shape=outs,
        in_specs=[pl.BlockSpec(memory_space=pltpu.SMEM) if i in scalars else whole for i in range(len(flat))]
        + [pl.BlockSpec(memory_space=pl.ANY)] * len(after),
        out_specs=placed,
        scratch_shapes=[pltpu.VMEM(dims, kind) for dims, kind in scratch]
        + ([pltpu.SemaphoreType.DMA((copies,))] if copies else []),
        compiler_params=pltpu.CompilerParams(vmem_limit_bytes=vmem),
        cost_estimate=pl.CostEstimate(flops=int(cost_us * 1e9), bytes_accessed=int(cost_us * 1e6), transcendentals=0),
    )(*flat, *after)


def shaped(*dims, kind=full_type):
    return jax.ShapeDtypeStruct(dims, kind)


def tail_parts(pre):
    size = jnp.abs(pre)
    base = 1.0 + (0.3275911 * 0.7071067811865476) * size
    guess = pl.reciprocal(base, approx=True)
    guess = guess * (2.0 - base * guess)
    guess = guess * (2.0 - base * guess)
    bell = jnp.exp(-0.5 * (pre * pre))
    series = 0.5 * 1.061405429
    for term in (-1.453152027, 1.421413741, -0.284496736, 0.254829592):
        series = series * guess + 0.5 * term
    return size, bell, series * guess * bell


def smooth(pre):
    size, _, tail = tail_parts(pre)
    return jnp.maximum(pre, 0.0) - size * tail


def smooth_slope(pre):
    _, bell, tail = tail_parts(pre)
    return jnp.where(pre >= 0.0, 1.0 - tail, tail) + 0.3989422804014327 * (pre * bell)


def wide(mask, width):
    return jnp.concatenate([mask] * (width // mask.shape[1]), axis=1)


def fold(value):
    rows, width = value.shape
    return jnp.sum(value.reshape(rows // 8, 8, width), axis=0)


def column_sum(value):
    return jnp.sum(value, axis=0, keepdims=True)


def total(parts):
    result = parts[0][...]
    for part in parts[1:]:
        result = result + part[...]
    return result


def statistics(sums, count):
    center = sums[0:1] / count
    inverse = lax.rsqrt(sums[1:2] / count - center * center + eps_norm)
    return center, inverse


def add_rows(store, row, value):
    store[row * 8 : row * 8 + 8, :] += fold(value)


def finish_rows(store, out_ref, rows):
    for row in range(rows):
        out_ref[row : row + 1, :] = column_sum(store[row * 8 : row * 8 + 8, :])


def times(lhs, rhs):
    return lax.dot_general(lhs, rhs, (((1,), (0,)), ((), ())), preferred_element_type=full_type)


def times_back(lhs, rhs):
    return lax.dot_general(lhs, rhs, (((1,), (1,)), ((), ())), preferred_element_type=full_type)


def times_rows(lhs, rhs):
    return lax.dot_general(lhs, rhs, (((0,), (0,)), ((), ())), preferred_element_type=full_type)


def low(value):
    return value.astype(low_type)


def inside(rows, sides, size_ref, unit):
    images = size_ref.shape[1]
    place = lax.broadcasted_iota(jnp.int32, (rows, 128), 0)
    image = place % images
    bound = jnp.zeros((rows, 128), jnp.int32)
    for index in range(images):
        bound = jnp.where(image == index, size_ref[0, index] // unit, bound)
    pair = place // images
    over = pair % even_width * sides + pair // even_width % sides
    down = pair // (even_width * sides)
    return jnp.where((over < bound) & (down < bound), 1.0, 0.0)


def enter_body(images, x_ref, size_ref, filter_ref, start_ref, out_ref, sums_ref, mask_ref, small_ref, pixel_ref, store):
    height, pairs = x_ref.shape[0], x_ref.shape[1]
    depth = x_ref.shape[4]
    line = even_width * images
    blank = jnp.zeros((even_width - pairs, images, depth), low_type)
    store[...] = jnp.zeros_like(store)
    mask_ref[...] = inside(mask_ref.shape[0], 2, size_ref, 16)
    small_ref[...] = inside(small_ref.shape[0], 1, size_ref, 32)
    for index in range(images):
        bound = (size_ref[0, index] // 32).astype(full_type)
        pixel_ref[index : index + 1, :] = 1.0 / jnp.full((1, 128), bound * bound)

    def step(index, carry):
        rows = pl.ds(pl.multiple_of(index * 4 * line, 4 * line), 4 * line)
        parts = []
        for row in range(2):
            for side in range(2):
                cells = jnp.concatenate([x_ref[index * 2 + row, :, side], blank], axis=0)
                parts.append(cells.reshape(line, depth))
        value = jnp.concatenate(parts, axis=0).astype(full_type) * wide(mask_ref[rows, :], depth)
        value = low(value)
        start_ref[rows, :] = value
        result = times(value, filter_ref[...])
        out_ref[rows, :] = result
        add_rows(store, 0, result)
        add_rows(store, 1, result * result)
        return carry

    lax.fori_loop(0, height // 2, step, 0)
    finish_rows(store, sums_ref, 2)
    sums_ref[2:3, :] = wide(column_sum(fold(mask_ref[...])), sums_ref.shape[1])
    sums_ref[3:4, :] = wide(column_sum(fold(small_ref[...])), sums_ref.shape[1])


def split_store(even_ref, moved_ref, place, value, line):
    even, odd = value[:line], value[line:]
    even_ref[place, 0] = low(even)
    even_ref[place, 1] = low(odd)
    moved_ref[place, 0] = low(pltpu.roll(even, line - line // even_width, 0))
    moved_ref[place, 1] = low(pltpu.roll(odd, line // even_width, 0))


def blank_border(*refs):
    for ref in refs:
        empty = jnp.zeros(ref.shape[1:], ref.dtype)
        ref[0] = empty
        ref[ref.shape[0] - 1] = empty


def tap_sources(even_ref, moved_ref):
    return (
        ((moved_ref, 1), (even_ref, 0), (even_ref, 1)),
        ((even_ref, 0), (even_ref, 1), (moved_ref, 0)),
    )


def block_body(images, parts, u_ref, scale_ref, shift_ref, mask_ref, filter_ref, even_ref, moved_ref, out_ref, sums_ref, count_ref, store):
    depth = filter_ref.shape[1]
    line = even_width * images
    height = even_ref.shape[0] - 2
    sums = total(parts)
    count_ref[...] = sums[2:4, 0:128]
    center, inverse = statistics(sums, sums[2:3, 0:1])
    factor = scale_ref[...] * inverse
    shift = shift_ref[...]
    blank_border(even_ref, moved_ref)
    store[...] = jnp.zeros_like(store)

    def first(index, carry):
        rows = pl.ds(pl.multiple_of(index * 2 * line, 2 * line), 2 * line)
        pre = (u_ref[rows, :] - center) * factor + shift
        value = smooth(pre) * wide(mask_ref[rows, :], depth)
        split_store(even_ref, moved_ref, index + 1, value, line)
        return carry

    lax.fori_loop(0, height, first, 0)
    half = height // 2
    sources = tap_sources(even_ref, moved_ref)
    for side in range(2):
        for part in range(2):
            lhs = jnp.concatenate(
                [
                    ref[half * part + row : half * part + row + half, plane].reshape(half * line, depth)
                    for row in range(3)
                    for ref, plane in sources[side]
                ],
                axis=1,
            )
            result = times(lhs, filter_ref[...])
            for index in range(half):
                begin = (half * part + index) * 2 * line + side * line
                piece = result[index * line : index * line + line]
                out_ref[begin : begin + line, :] = piece
                kept = piece * wide(mask_ref[begin : begin + line, :], piece.shape[1])
                add_rows(store, 0, kept)
                add_rows(store, 1, kept * piece)
    finish_rows(store, sums_ref, 2)


def expand_body(parts, u_ref, count_ref, scale_ref, shift_ref, mask_ref, filter_ref, hidden_ref, out_ref, sums_ref, store, which, rows_step):
    center, inverse = statistics(total(parts), count_ref[which : which + 1, 0:1])
    factor = scale_ref[...] * inverse
    shift = shift_ref[...]
    depth = u_ref.shape[1]
    store[...] = jnp.zeros_like(store)

    def step(index, carry):
        rows = pl.ds(pl.multiple_of(index * rows_step, rows_step), rows_step)
        pre = (u_ref[rows, :] - center) * factor + shift
        value = low(smooth(pre) * wide(mask_ref[rows, :], depth))
        hidden_ref[rows, :] = value
        result = times(value, filter_ref[...])
        out_ref[rows, :] = result
        add_rows(store, 0, result)
        add_rows(store, 1, result * result)
        return carry

    lax.fori_loop(0, u_ref.shape[0] // rows_step, step, 0)
    finish_rows(store, sums_ref, 2)


def join_body(images, parts, u_ref, count_ref, scale_ref, shift_ref, mask_ref, start_ref, reduce_ref, side_ref, block_ref, reduced_ref, picked_ref, sided_ref, sums_ref, side_sums_ref, store, side_store):
    center, inverse = statistics(total(parts), count_ref[0:1, 0:1])
    factor = scale_ref[...] * inverse
    shift = shift_ref[...]
    depth = u_ref.shape[1]
    line = even_width * images
    store[...] = jnp.zeros_like(store)
    side_store[...] = jnp.zeros_like(side_store)

    def step(index, carry):
        rows = pl.ds(pl.multiple_of(index * 4 * line, 4 * line), 4 * line)
        pre = (u_ref[rows, :] - center) * factor + shift + start_ref[rows, :].astype(full_type)
        value = low(smooth(pre) * wide(mask_ref[rows, :], depth))
        block_ref[rows, :] = value
        picked_ref[pl.ds(pl.multiple_of(index * line, line), line), :] = value[:line]
        result = times(value, reduce_ref[...])
        reduced_ref[rows, :] = result
        add_rows(store, 0, result)
        add_rows(store, 1, result * result)
        return carry

    lax.fori_loop(0, u_ref.shape[0] // (4 * line), step, 0)
    finish_rows(store, sums_ref, 2)
    width = 512

    def side(index, carry):
        columns = pl.ds(pl.multiple_of(index * width, width), width)
        result = times(picked_ref[...], side_ref[:, columns])
        sided_ref[:, columns] = result
        side_sums_ref[0:1, columns] = column_sum(fold(result))
        side_sums_ref[1:2, columns] = column_sum(fold(result * result))
        return carry

    lax.fori_loop(0, side_ref.shape[1] // width, side, 0)


def shrink_body(images, parts, u_ref, count_ref, scale_ref, shift_ref, mask_ref, small_ref, filter_ref, even_ref, moved_ref, out_ref, sums_ref):
    depth = u_ref.shape[1]
    line = even_width * images
    height = even_ref.shape[0] - 2
    center, inverse = statistics(total(parts), count_ref[0:1, 0:1])
    factor = scale_ref[...] * inverse
    shift = shift_ref[...]
    blank_border(even_ref, moved_ref)

    def first(index, carry):
        rows = pl.ds(pl.multiple_of(index * 2 * line, 2 * line), 2 * line)
        pre = (u_ref[rows, :] - center) * factor + shift
        value = smooth(pre) * wide(mask_ref[rows, :], depth)
        split_store(even_ref, moved_ref, index + 1, value, line)
        return carry

    lax.fori_loop(0, height, first, 0)
    half = height // 2
    result = None
    for row in range(3):
        lhs = jnp.concatenate(
            [
                jnp.concatenate([ref[2 * index + row, plane] for index in range(half)], axis=0)
                for ref, plane in ((moved_ref, 1), (even_ref, 0), (even_ref, 1))
            ],
            axis=1,
        )
        term = times(lhs, filter_ref[row * 3 * depth : row * 3 * depth + 3 * depth, :])
        result = term if result is None else result + term
    out_ref[...] = result
    kept = result * wide(small_ref[...], result.shape[1])
    sums_ref[0:1, :] = column_sum(fold(kept))
    sums_ref[1:2, :] = column_sum(fold(kept * result))


def leave_body(images, parts, side_parts, u_ref, side_ref, count_ref, scale_ref, shift_ref, side_scale_ref, side_shift_ref, small_ref, pixel_ref, block_ref, joined_ref, pooled_ref, store):
    center, inverse = statistics(total(parts), count_ref[1:2, 0:1])
    factor = scale_ref[...] * inverse
    side_center, side_inverse = statistics(total(side_parts), count_ref[1:2, 0:1])
    side_factor = side_scale_ref[...] * side_inverse
    shift = shift_ref[...] + side_shift_ref[...]
    depth = u_ref.shape[1]
    line = even_width * images
    pairs = block_ref.shape[1]
    store[...] = jnp.zeros_like(store)

    def step(index, carry):
        rows = pl.ds(pl.multiple_of(index * line, line), line)
        pre = (u_ref[rows, :] - center) * factor + (side_ref[rows, :] - side_center) * side_factor + shift
        joined_ref[rows, :] = pre
        value = smooth(pre) * wide(small_ref[rows, :], depth)
        block_ref[index] = low(value).reshape(even_width, images, depth)[:pairs]
        add_rows(store, 0, value)
        return carry

    lax.fori_loop(0, u_ref.shape[0] // line, step, 0)
    summed = store[0:images, :]
    for begin in range(images, 8, images):
        summed = summed + store[begin : begin + images, :]
    pooled_ref[...] = summed * pixel_ref[:, 0:1]


def gather_images(store, row, images):
    summed = store[row * 8 : row * 8 + images, :]
    for begin in range(images, 8, images):
        summed = summed + store[row * 8 + begin : row * 8 + begin + images, :]
    return summed


def slope_sums_body(images, parts, side_parts, joined_ref, u_ref, side_ref, count_ref, small_ref, slope_ref, plain_ref, unit_ref, side_unit_ref, store):
    center, inverse = statistics(total(parts), count_ref[1:2, 0:1])
    side_center, side_inverse = statistics(total(side_parts), count_ref[1:2, 0:1])
    depth = u_ref.shape[1]
    line = even_width * images
    store[...] = jnp.zeros_like(store)

    def step(index, carry):
        rows = pl.ds(pl.multiple_of(index * line, line), line)
        slope = smooth_slope(joined_ref[rows, :]) * wide(small_ref[rows, :], depth)
        slope_ref[rows, :] = slope
        add_rows(store, 0, slope)
        add_rows(store, 1, slope * (u_ref[rows, :] - center))
        add_rows(store, 2, slope * (side_ref[rows, :] - side_center))
        return carry

    lax.fori_loop(0, u_ref.shape[0] // line, step, 0)
    plain_ref[...] = gather_images(store, 0, images)
    unit_ref[...] = gather_images(store, 1, images) * inverse
    side_unit_ref[...] = gather_images(store, 2, images) * side_inverse


def compare_body(pooled_ref, partner_ref, pixel_ref, plain_ref, unit_ref, side_unit_ref, loss_ref, grad_ref, sums_ref):
    pooled, partner = pooled_ref[...], partner_ref[...]
    inverse_own = lax.rsqrt(jnp.sum(pooled * pooled, axis=1, keepdims=True) + eps_cos)
    unit_own = pooled * inverse_own
    unit_other = partner * lax.rsqrt(jnp.sum(partner * partner, axis=1, keepdims=True) + eps_cos)
    cosine = jnp.sum(unit_own * unit_other, axis=1, keepdims=True)
    loss_ref[...] = jnp.broadcast_to(-0.5 * cosine, loss_ref.shape)
    grad = (-0.5 * loss_scale) * inverse_own * (unit_other - cosine * unit_own) * pixel_ref[:, 0:1]
    grad_ref[...] = grad
    sums_ref[0:1, :] = column_sum(grad * plain_ref[...])
    sums_ref[1:2, :] = column_sum(grad * unit_ref[...])
    sums_ref[2:3, :] = column_sum(grad * side_unit_ref[...])


def norm_back(sums, totals, count, scale):
    center, inverse = statistics(sums, count)
    factor = scale * inverse
    return center, inverse, factor, -(factor * inverse * totals[1:2] / count), -(factor * totals[0:1] / count)


def leave_back_body(images, parts, side_parts, grads, slope_ref, grad_ref, u_ref, side_ref, count_ref, scale_ref, side_scale_ref, small_ref, filter_ref, inner_parts, inner_u_ref, inner_slope_ref, low_ref, side_low_ref, out_ref, sums_ref, store):
    totals = total(grads)
    count = count_ref[1:2, 0:1]
    center, _, factor, along, level = norm_back(total(parts), totals, count, scale_ref[...])
    side_totals = jnp.concatenate([totals[0:1], totals[2:3]], axis=0)
    side_center, _, side_factor, side_along, side_level = norm_back(total(side_parts), side_totals, count, side_scale_ref[...])
    depth = u_ref.shape[1]
    line = even_width * images
    grad = jnp.concatenate([grad_ref[...]] * (line // images), axis=0)

    def step(index, carry):
        rows = pl.ds(pl.multiple_of(index * line, line), line)
        mask = wide(small_ref[rows, :], depth)
        joined = slope_ref[rows, :] * grad
        low_ref[rows, :] = low((joined * factor + (u_ref[rows, :] - center) * along + level) * mask)
        side_low_ref[rows, :] = low((joined * side_factor + (side_ref[rows, :] - side_center) * side_along + side_level) * mask)
        return carry

    lax.fori_loop(0, u_ref.shape[0] // line, step, 0)
    inner_center, inner_inverse = statistics(total(inner_parts), count)
    result = times_back(low_ref[...], filter_ref[...]) * inner_slope_ref[...]
    out_ref[...] = result
    sums_ref[0:1, :] = column_sum(fold(result))
    sums_ref[1:2, :] = column_sum(fold(result * (inner_u_ref[...] - inner_center))) * inner_inverse


def shrink_back_body(images, parts, grads, g_ref, u_ref, count_ref, scale_ref, small_ref, filter_ref, inner_parts, inner_u_ref, inner_slope_ref, low_ref, out_ref, sums_ref, store):
    depth = u_ref.shape[1]
    inner = filter_ref.shape[2]
    line = even_width * images
    half = u_ref.shape[0] // line
    center, _, factor, along, level = norm_back(total(parts), total(grads), count_ref[1:2, 0:1], scale_ref[...])
    exact = (g_ref[...] * factor + (u_ref[...] - center) * along + level) * wide(small_ref[...], depth)
    here = low(exact)
    low_ref[...] = here
    right = low(pltpu.roll(exact, exact.shape[0] - images, 0))
    blank = jnp.zeros((line, depth), low_type)
    below = jnp.concatenate([here[line:], blank], axis=0)
    below_right = jnp.concatenate([right[line:], blank], axis=0)
    inner_center, inner_inverse = statistics(total(inner_parts), count_ref[0:1, 0:1])
    store[...] = jnp.zeros_like(store)
    for row in range(2):
        for side in range(2):
            terms = [(here, 1 + row, 1 + side)]
            if side:
                terms.append((right, 1 + row, 0))
            if row:
                terms.append((below, 0, 1 + side))
            if row and side:
                terms.append((below_right, 0, 0))
            lhs = jnp.concatenate([value for value, _, _ in terms], axis=1)
            rhs = jnp.concatenate([filter_ref[down * 3 + over] for _, down, over in terms], axis=1)
            result = times_back(lhs, rhs)
            for index in range(half):
                begin = (index * 4 + row * 2 + side) * line
                rows = slice(begin, begin + line)
                piece = result[index * line : index * line + line] * inner_slope_ref[rows, :]
                out_ref[rows, :] = piece
                add_rows(store, 0, piece)
                add_rows(store, 1, piece * (inner_u_ref[rows, :] - inner_center))
    sums_ref[0:1, :] = column_sum(store[0:8, :])
    sums_ref[1:2, :] = column_sum(store[8:16, :]) * inner_inverse


def join_back_body(images, parts, grads, g_ref, u_ref, count_ref, scale_ref, mask_ref, filter_ref, picked_ref, inner_parts, inner_u_ref, inner_slope_ref, low_ref, out_ref, sums_ref, store):
    depth = u_ref.shape[1]
    line = even_width * images
    center, _, factor, along, level = norm_back(total(parts), total(grads), count_ref[0:1, 0:1], scale_ref[...])
    inner_center, inner_inverse = statistics(total(inner_parts), count_ref[0:1, 0:1])
    store[...] = jnp.zeros_like(store)

    def step(index, carry):
        rows = pl.ds(pl.multiple_of(index * 4 * line, 4 * line), 4 * line)
        value = low((g_ref[rows, :] * factor + (u_ref[rows, :] - center) * along + level) * wide(mask_ref[rows, :], depth))
        low_ref[rows, :] = value
        result = times_back(value, filter_ref[...])
        extra = picked_ref[pl.ds(pl.multiple_of(index * line, line), line), :]
        result = jnp.concatenate([result[:line] + extra, result[line:]], axis=0) * inner_slope_ref[rows, :]
        out_ref[rows, :] = result
        add_rows(store, 0, result)
        add_rows(store, 1, result * (inner_u_ref[rows, :] - inner_center))
        return carry

    lax.fori_loop(0, u_ref.shape[0] // (4 * line), step, 0)
    sums_ref[0:1, :] = column_sum(store[0:8, :])
    sums_ref[1:2, :] = column_sum(store[8:16, :]) * inner_inverse


def expand_back_body(parts, grads, g_ref, u_ref, count_ref, scale_ref, mask_ref, filter_ref, inner_parts, inner_u_ref, inner_slope_ref, low_ref, out_ref, sums_ref, store, rows_step):
    depth = u_ref.shape[1]
    center, _, factor, along, level = norm_back(total(parts), total(grads), count_ref[0:1, 0:1], scale_ref[...])
    inner_center, inner_inverse = statistics(total(inner_parts), count_ref[0:1, 0:1])
    store[...] = jnp.zeros_like(store)

    def step(index, carry):
        rows = pl.ds(pl.multiple_of(index * rows_step, rows_step), rows_step)
        value = low((g_ref[rows, :] * factor + (u_ref[rows, :] - center) * along + level) * wide(mask_ref[rows, :], depth))
        low_ref[rows, :] = value
        result = times_back(value, filter_ref[...]) * inner_slope_ref[rows, :]
        out_ref[rows, :] = result
        add_rows(store, 0, result)
        add_rows(store, 1, result * (inner_u_ref[rows, :] - inner_center))
        return carry

    lax.fori_loop(0, u_ref.shape[0] // rows_step, step, 0)
    sums_ref[0:1, :] = column_sum(store[0:8, :])
    sums_ref[1:2, :] = column_sum(store[8:16, :]) * inner_inverse


def block_back_body(images, parts, grads, g_ref, u_ref, count_ref, scale_ref, mask_ref, filter_ref, inner_parts, inner_u_ref, inner_slope_ref, low_ref, out_ref, sums_ref, even_ref, moved_ref, store):
    depth = u_ref.shape[1]
    line = even_width * images
    height = even_ref.shape[0] - 2
    center, _, factor, along, level = norm_back(total(parts), total(grads), count_ref[0:1, 0:1], scale_ref[...])
    inner_center, inner_inverse = statistics(total(inner_parts), count_ref[0:1, 0:1])
    blank_border(even_ref, moved_ref)
    store[...] = jnp.zeros_like(store)

    def first(index, carry):
        rows = pl.ds(pl.multiple_of(index * 2 * line, 2 * line), 2 * line)
        value = (g_ref[rows, :] * factor + (u_ref[rows, :] - center) * along + level) * wide(mask_ref[rows, :], depth)
        low_ref[rows, :] = low(value)
        split_store(even_ref, moved_ref, index + 1, value, line)
        return carry

    lax.fori_loop(0, height, first, 0)
    half = height // 2
    sources = tap_sources(even_ref, moved_ref)
    rhs = jnp.concatenate([filter_ref[8 - tap] for tap in range(9)], axis=1)
    for side in range(2):
        for part in range(2):
            lhs = jnp.concatenate(
                [
                    ref[half * part + row : half * part + row + half, plane].reshape(half * line, depth)
                    for row in range(3)
                    for ref, plane in sources[side]
                ],
                axis=1,
            )
            result = times_back(lhs, rhs)
            for index in range(half):
                begin = (half * part + index) * 2 * line + side * line
                rows = slice(begin, begin + line)
                piece = result[index * line : index * line + line] * inner_slope_ref[rows, :]
                out_ref[rows, :] = piece
                add_rows(store, 0, piece)
                add_rows(store, 1, piece * (inner_u_ref[rows, :] - inner_center))
    sums_ref[0:1, :] = column_sum(store[0:8, :])
    sums_ref[1:2, :] = column_sum(store[8:16, :]) * inner_inverse


def exit_body(images, parts, grads, g_ref, u_ref, count_ref, scale_ref, mask_ref, filter_ref, joined_ref, low_ref, out_ref):
    depth = u_ref.shape[1]
    pairs = out_ref.shape[1]
    line = even_width * images
    center, _, factor, along, level = norm_back(total(parts), total(grads), count_ref[0:1, 0:1], scale_ref[...])

    def step(index, carry):
        rows = pl.ds(pl.multiple_of(index * 4 * line, 4 * line), 4 * line)
        mask = mask_ref[rows, :]
        value = low((g_ref[rows, :] * factor + (u_ref[rows, :] - center) * along + level) * wide(mask, depth))
        low_ref[rows, :] = value
        result = low((times_back(value, filter_ref[...]) + joined_ref[rows, :]) * wide(mask, joined_ref.shape[1]))
        for row in range(2):
            for side in range(2):
                begin = (row * 2 + side) * line
                cells = result[begin : begin + line].reshape(even_width, images, result.shape[1])
                out_ref[index * 2 + row, :, side] = cells[:pairs]
        return carry

    lax.fori_loop(0, u_ref.shape[0] // (4 * line), step, 0)


def natural_body(images, value_ref, out_ref):
    pairs = out_ref.shape[1]
    line = even_width * images
    depth = value_ref.shape[1]

    def step(index, carry):
        for side in range(2):
            rows = pl.ds(pl.multiple_of(index * 2 * line + side * line, line), line)
            out_ref[index, :, side] = value_ref[rows, :].reshape(even_width, images, depth)[:pairs]
        return carry

    lax.fori_loop(0, out_ref.shape[0], step, 0)


def slope_body(parts, u_ref, count_ref, scale_ref, shift_ref, mask_ref, extras, out_ref, which, rows_step):
    center, inverse = statistics(total(parts), count_ref[which : which + 1, 0:1])
    factor = scale_ref[...] * inverse
    shift = shift_ref[...]
    depth = u_ref.shape[1]

    def step(index, carry):
        rows = pl.ds(pl.multiple_of(index * rows_step, rows_step), rows_step)
        pre = (u_ref[rows, :] - center) * factor + shift
        for extra_ref in extras:
            pre = pre + extra_ref[rows, :].astype(full_type)
        out_ref[rows, :] = low(smooth_slope(pre) * wide(mask_ref[rows, :], depth))
        return carry

    lax.fori_loop(0, u_ref.shape[0] // rows_step, step, 0)


def times_back_body(value_ref, filter_ref, out_ref):
    out_ref[...] = times_back(value_ref[...], filter_ref[...])


def window_start(device, share_size, width):
    return (device * share_size) // (8 * width) * 8


def window_rows(share_size, width):
    return -(-(share_size + 8 * width) // (16 * width)) * 16


def low_rows(rows):
    first = rows // 32 * 8
    return [first, rows // 2 - first] * 2


class AllCopies:
    def __init__(self, source, out, sems, first_device, first_row, share_size):
        self.waiting, self.started = [], []
        owners, rows, width = out.shape
        for owner in range(owners):
            begin = window_start(first_device + owner, share_size, width) - first_row
            copy = pltpu.make_async_copy(source.at[pl.ds(begin, rows)], out.at[owner], sems.at[owner])
            self.waiting.append((begin + rows, copy))

    def start(self, filled):
        for end, copy in self.waiting:
            if end <= filled:
                copy.start()
                self.started.append(copy)
        self.waiting = [item for item in self.waiting if item[0] > filled]

    def finish(self, filled):
        self.start(filled)
        for copy in self.started:
            copy.wait()


class Copies:
    def __init__(self, source, outs, sems, first_device, first_row, share_size, offsets):
        self.waiting, self.started = [], []
        owners, _, width = outs[0].shape
        pieces = len(offsets)
        core = lax.axis_index("dp") % 2
        for owner in range(owners):
            device = first_device + 2 * owner
            end = window_start(device + 1, share_size, width) + window_rows(share_size, width) - first_row
            for piece in range(pieces):
                for which, chosen in enumerate((1 - core, core)):
                    out = outs[which * pieces + piece]
                    begin = window_start(device + chosen, share_size, width) - first_row + offsets[piece]
                    rows = pl.ds(pl.multiple_of(begin, 8), out.shape[1])
                    sem = sems.at[(owner * pieces + piece) * 2 + which]
                    self.waiting.append((end, pltpu.make_async_copy(source.at[rows], out.at[owner], sem)))

    def start(self, filled):
        for end, copy in self.waiting:
            if end <= filled:
                copy.start()
                self.started.append(copy)
        self.waiting = [item for item in self.waiting if item[0] > filled]

    def finish(self, filled):
        self.start(filled)
        for copy in self.started:
            copy.wait()


def put_filter(store, begin, value, grad, copies=None):
    step, across = 256, min(512, grad.shape[1])
    lanes = store.shape[1]
    cuts = grad.shape[1] // lanes
    for row in range(0, value.shape[1], step):
        for column in range(0, grad.shape[1], across):
            result = times_rows(value[:, row : row + step], grad[:, column : column + across])
            for cut in range(across // lanes):
                place = begin + row * cuts + column // lanes + cut
                store[pl.ds(place, step, stride=cuts), :] = result[:, cut * lanes : cut * lanes + lanes]
        if copies is not None:
            copies.start(begin + (row + step) * cuts)
    return begin + value.shape[1] * cuts


def late_filters_body(first_device, first_row, share_size, hidden_ref, picked_ref, low_ref, side_low_ref, out_ref, spill_ref, store, sems):
    copies = AllCopies(store, out_ref, sems, first_device, first_row, share_size)
    filled = hidden_ref.shape[1] * low_ref.shape[1] // 128 + picked_ref.shape[1] * side_low_ref.shape[1] // 128
    store[filled:, :] = jnp.zeros((store.shape[0] - filled, store.shape[1]), full_type)
    filled = put_filter(store, 0, hidden_ref, low_ref, copies)
    spill_ref[...] = store[: spill_ref.shape[0], :]
    put_filter(store, filled, picked_ref, side_low_ref, copies)
    copies.finish(store.shape[0])


def middle_filters_body(share_size, block_ref, low_ref, even_ref, moved_ref, inner_low_ref, spill_ref, *rest):
    *outs, store, sems = rest
    view = lax.axis_index("view")
    first, half = outs[0].shape[1], outs[0].shape[1] + outs[1].shape[1]
    far, near = (1 - view) * half, view * half
    copies = Copies(store, outs, sems, 0, 0, share_size, (far, far + first, near, near + first))
    store[store.shape[0] - spill_ref.shape[0] :, :] = spill_ref[...]
    filled = put_filter(store, 0, block_ref, low_ref, copies)
    half = even_ref.shape[0] // 2 - 1
    for row in range(3):
        for ref, plane in ((moved_ref, 1), (even_ref, 0), (even_ref, 1)):
            lhs = jnp.concatenate([ref[2 * index + row, plane] for index in range(half)], axis=0)
            filled = put_filter(store, filled, lhs, inner_low_ref, copies)
    copies.finish(store.shape[0])


def block_filter_body(even_ref, moved_ref, inner_low_ref, hidden_ref, outer_low_ref, out_ref):
    height, _, line, inner = even_ref.shape
    height = height - 2
    width = inner_low_ref.shape[1]
    grad = inner_low_ref[...].reshape(height, 2, line, width)
    grad = jnp.concatenate([grad[:, side].reshape(height * line, width) for side in range(2)], axis=0)
    sources = tap_sources(even_ref, moved_ref)
    filled = 0
    for row in range(3):
        for over in range(3):
            lhs = jnp.concatenate(
                [
                    sources[side][over][0][row : row + height, sources[side][over][1]].reshape(height * line, inner)
                    for side in range(2)
                ],
                axis=0,
            )
            filled = put_filter(out_ref, filled, lhs, grad)
    put_filter(out_ref, filled, hidden_ref, outer_low_ref)


def early_filters_body(share_size, start_ref, low_ref, later_ref, *rest):
    *outs, store, sems = rest
    copies = Copies(store, outs, sems, 0, 0, share_size, (0,))
    filled = put_filter(store, 0, start_ref, low_ref)
    later = later_ref.shape[0]
    store[filled : filled + later, :] = later_ref[...]
    filled += later
    store[filled:, :] = jnp.zeros((store.shape[0] - filled, store.shape[1]), full_type)
    copies.finish(store.shape[0])


def late_window_body(place, high_ref, high_got_ref, low_ref, low_got_ref, norms_ref, out_ref):
    view = lax.axis_index("view")
    half = low_ref.shape[0]

    @pl.when(view == 0)
    def _():
        out_ref[:half, :] = low_ref[...]
        out_ref[half:, :] = low_got_ref[...]

    @pl.when(view == 1)
    def _():
        out_ref[...] = high_ref[...] + high_got_ref[...]

    rows = pl.ds(place, norms_ref.shape[0])
    out_ref[rows, :] += norms_ref[...]


def early_window_body(place, refs, norms_ref, out_ref):
    out_ref[...] = add_terms(refs)
    rows = pl.ds(place, norms_ref.shape[0])
    out_ref[rows, :] += norms_ref[...]


def exchange(value, axis, bits):
    return lax.ppermute(value, axis, [(i, i ^ bits) for i in range(lax.axis_size(axis))])


def share(sums):
    size = lax.axis_size("dp")
    if size > 1:
        sums = sums + exchange(sums, "dp", 1)
    if size > 2:
        sums = sums + exchange(sums, "dp", 3)
    parts = (sums,)
    bit = 4
    while bit < size:
        if len(parts) > 1:
            parts = (sum(parts[1:], parts[0]),)
        steps = [bit + 1, 2 * bit + 1, 3 * bit + 1] if 2 * bit < size else [bit + 1]
        parts = parts + tuple(exchange(parts[0], "dp", step) for step in steps)
        bit *= 4
    return parts


def add_terms(refs):
    result = refs[0][...]
    for ref in refs[1:]:
        result = result + ref[...]
    return result


def gate(value):
    corner = value[(slice(0, 1),) * (value.ndim - 1) + (slice(0, 128),)]
    return 0.0 * corner.reshape(1, 1, 128)


class Term:
    def __init__(self, value, bits):
        self.value, self.bits, self.chosen = value, list(bits), {}

    def part(self, chosen):
        rows, width = self.value.shape[1:]
        cut = self.value.reshape((2,) * len(self.bits) + (rows, width))
        starts = [chosen.get(item, 0) for item in self.bits] + [0, 0]
        sizes = [1 if item in chosen else 2 for item in self.bits] + [rows, width]
        return lax.dynamic_slice(cut, starts, sizes).reshape(-1, rows, width)


class Windows:
    def __init__(self, terms, bits):
        self.terms, self.bits, self.chosen = [Term(value, bits) for value in terms], list(bits), {}

    def step(self, item, *after):
        axis, bit = item
        own = (lax.axis_index(axis) >> bit) & 1
        chosen = dict(self.chosen)
        chosen[item] = 1 - own
        self.sent = sum([term.part(chosen) for term in self.terms[1:]], self.terms[0].part(chosen))
        if after:
            self.sent = self.sent + sum(gate(value) for value in after)
        self.received = exchange(self.sent, axis, 1 << bit)
        self.chosen[item] = own
        self.bits.remove(item)
        self.terms.append(Term(self.received, self.bits))

    def total(self):
        return (sum([term.part(self.chosen)[0] for term in self.terms[1:]], self.terms[0].part(self.chosen)[0]),)


def per_device(
    inputs,
    resolution,
    reduce_a,
    spatial_a,
    expand_a,
    reduce_b,
    spatial_b,
    expand_b,
    shortcut_b,
    scale_reduce_a,
    shift_reduce_a,
    scale_spatial_a,
    shift_spatial_a,
    scale_expand_a,
    shift_expand_a,
    scale_reduce_b,
    shift_reduce_b,
    scale_spatial_b,
    shift_spatial_b,
    scale_expand_b,
    shift_expand_b,
    scale_shortcut,
    shift_shortcut,
):
    images, height, depth_a = inputs.shape[1], inputs.shape[2], inputs.shape[4]
    pairs = height // 2
    middle_a, middle_b, depth_b = reduce_a.shape[1], reduce_b.shape[1], shortcut_b.shape[1]
    line = even_width * images
    rows_big, rows_small = height * 2 * line, pairs * line
    spatial_a9 = spatial_a.reshape(9, middle_a, middle_a)
    spatial_b9 = spatial_b.reshape(9, middle_b, middle_b)
    cells = inputs[0].transpose(1, 2, 0, 3).reshape(height, pairs, 2, images, depth_a)

    vectors = [
        (scale_reduce_a, shift_reduce_a),
        (scale_spatial_a, shift_spatial_a),
        (scale_expand_a, shift_expand_a),
        (scale_reduce_b, shift_reduce_b),
        (scale_spatial_b, shift_spatial_b),
        (scale_expand_b, shift_expand_b),
        (scale_shortcut, shift_shortcut),
    ]
    packed = jnp.stack([jnp.pad(vector, (0, depth_b - vector.size)) for pair in vectors for vector in pair])

    def affine(index):
        width = vectors[index][0].size
        return tuple(View(packed, (row, row + 1), (0, width)) for row in (2 * index, 2 * index + 1))

    def padded(width):
        return shaped(height + 2, 2, line, width, kind=low_type)

    def with_images(body):
        return functools.partial(body, images)

    start, reduced_a, sums, mask_big, mask_small, pixel = call(
        with_images(enter_body),
        [
            shaped(rows_big, depth_a, kind=low_type),
            shaped(rows_big, middle_a),
            shaped(4, middle_a),
            shaped(rows_big, 128),
            shaped(rows_small, 128),
            shaped(images, 128),
        ],
        [cells, resolution, reduce_a],
        scratch=[((16, middle_a), full_type)],
        scalars=(1,),
    )
    sums_ra = share(sums)
    scale_ra, shift_ra = affine(0)
    even_a, moved_a, mixed_a, sums, counts = call(
        with_images(block_body),
        [padded(middle_a), padded(middle_a), shaped(rows_big, middle_a), shaped(2, middle_a), shaped(2, 128)],
        [sums_ra, reduced_a, scale_ra, shift_ra, mask_big, spatial_a.reshape(9 * middle_a, middle_a)],
        scratch=[((16, middle_a), full_type)],
    )
    def slope(parts, value, scale, shift, mask, extras, which, rows_step):
        return call(
            functools.partial(slope_body, which=which, rows_step=rows_step),
            [shaped(*value.shape, kind=low_type)],
            [parts, value, counts, scale, shift, mask, extras],
        )[0]

    slope_ra = slope(sums_ra, reduced_a, scale_ra, shift_ra, mask_big, (), 0, 2 * line)
    sums_sa = share(sums)
    scale_sa, shift_sa = affine(1)
    hidden_two_a, expanded_a, sums = call(
        functools.partial(expand_body, which=0, rows_step=4 * line),
        [shaped(rows_big, middle_a, kind=low_type), shaped(rows_big, depth_a), shaped(2, depth_a)],
        [sums_sa, mixed_a, counts, scale_sa, shift_sa, mask_big, expand_a],
        scratch=[((16, depth_a), full_type)],
        after=(slope_ra,),
    )
    slope_sa = slope(sums_sa, mixed_a, scale_sa, shift_sa, mask_big, (), 0, 2 * line)
    sums_ea = share(sums)
    scale_ea, shift_ea = affine(2)
    block_a, reduced_b, picked, side_b, sums, side_sums = call(
        with_images(join_body),
        [
            shaped(rows_big, depth_a, kind=low_type),
            shaped(rows_big, middle_b),
            shaped(rows_small, depth_a, kind=low_type),
            shaped(rows_small, depth_b),
            shaped(2, middle_b),
            shaped(2, depth_b),
        ],
        [sums_ea, expanded_a, counts, scale_ea, shift_ea, mask_big, start, reduce_b, shortcut_b],
        scratch=[((16, middle_b), full_type), ((16, 128), full_type)],
        after=(slope_sa,),
    )
    slope_ea = slope(sums_ea, expanded_a, scale_ea, shift_ea, mask_big, (start,), 0, 2 * line)
    shared = share(jnp.concatenate([sums, side_sums], axis=1))
    sums_rb = tuple(View(part, (0, 2), (0, middle_b)) for part in shared)
    sums_sc = tuple(View(part, (0, 2), (middle_b, middle_b + depth_b)) for part in shared)
    scale_rb, shift_rb = affine(3)
    scale_sc, shift_sc = affine(6)
    even_b, moved_b, mixed_b, sums = call(
        with_images(shrink_body),
        [padded(middle_b), padded(middle_b), shaped(rows_small, middle_b), shaped(2, middle_b)],
        [sums_rb, reduced_b, counts, scale_rb, shift_rb, mask_big, mask_small, spatial_b.reshape(9 * middle_b, middle_b)],
        after=(slope_ea,),
    )
    block_out = call(
        with_images(natural_body), [shaped(height, pairs, 2, images, depth_a, kind=low_type)], [block_a]
    )[0]
    slope_rb = slope(sums_rb, reduced_b, scale_rb, shift_rb, mask_big, (), 0, 2 * line)
    sums_sb = share(sums)
    scale_sb, shift_sb = affine(4)
    hidden_two_b, expanded_b, sums = call(
        functools.partial(expand_body, which=1, rows_step=line),
        [shaped(rows_small, middle_b, kind=low_type), shaped(rows_small, depth_b), shaped(2, depth_b)],
        [sums_sb, mixed_b, counts, scale_sb, shift_sb, mask_small, expand_b],
        scratch=[((16, depth_b), full_type)],
        after=(slope_rb, block_out),
    )
    slope_sb = slope(sums_sb, mixed_b, scale_sb, shift_sb, mask_small, (), 1, line)
    sums_eb = share(sums)
    scale_eb, shift_eb = affine(5)
    block_b, joined_b, pooled = call(
        with_images(leave_body),
        [shaped(pairs, pairs, images, depth_b, kind=low_type), shaped(rows_small, depth_b), shaped(images, depth_b)],
        [sums_eb, sums_sc, expanded_b, side_b, counts, scale_eb, shift_eb, scale_sc, shift_sc, mask_small, pixel],
        scratch=[((8, depth_b), full_type)],
        after=(slope_sb,),
    )
    partner = exchange(pooled, "view", 1)
    slope_b, plain, unit, side_unit = call(
        with_images(slope_sums_body),
        [shaped(rows_small, depth_b)] + [shaped(images, depth_b)] * 3,
        [sums_eb, sums_sc, joined_b, expanded_b, side_b, counts, mask_small],
        scratch=[((24, depth_b), full_type)],
    )
    loss, grad_out, sums = call(
        compare_body,
        [shaped(images, 128), shaped(images, depth_b), shaped(3, depth_b)],
        [pooled, partner, pixel, plain, unit, side_unit],
    )
    grads_eb = share(sums)

    size = lax.axis_size("dp")
    half = size // 2
    bits = [("dp", bit) for bit in range(size.bit_length() - 2, 0, -1)]
    low_first = sorted(bits, key=lambda item: item[1])
    high_first = low_first[1:] + low_first[:1]
    lanes = 128
    first_rows = (depth_a + 9 * middle_b) * middle_b // lanes
    norm_rows_b = (4 * middle_b + 4 * depth_b) // lanes
    total_b = first_rows + (middle_b + depth_a) * depth_b // lanes + norm_rows_b
    share_b = total_b * lanes // (2 * size)
    window_b = window_rows(share_b, lanes)
    end_low = window_start(size - 1, share_b, lanes) + window_b
    end_high = window_start(2 * size - 1, share_b, lanes) + window_b

    def windows(count, pieces):
        return [pltpu.HBM((count, piece, lanes), full_type) for piece in pieces] * 2

    def pairs_of(outs):
        count = len(outs) // 2
        return [(kept, exchange(send, "dp", 1)) for send, kept in zip(outs[:count], outs[count:])]

    low_eb, low_sc, grad_sb, sums = call(
        with_images(leave_back_body),
        [
            shaped(rows_small, depth_b, kind=low_type),
            shaped(rows_small, depth_b, kind=low_type),
            shaped(rows_small, middle_b),
            shaped(2, middle_b),
        ],
        [
            sums_eb,
            sums_sc,
            grads_eb,
            slope_b,
            grad_out,
            expanded_b,
            side_b,
            counts,
            scale_eb,
            scale_sc,
            mask_small,
            expand_b,
            sums_sb,
            mixed_b,
            slope_sb,
        ],
        scratch=[((8, 128), full_type)],
    )
    grads_sb = share(sums)
    late_windows, spill = call(
        functools.partial(late_filters_body, size, first_rows, share_b),
        [pltpu.HBM((size, window_b, lanes), full_type), shaped(end_low - first_rows, lanes)],
        [hidden_two_b, picked, low_eb, low_sc],
        scratch=[((end_high - first_rows, lanes), full_type)],
        copies=size,
        vmem=vmem_large,
        after=(grads_sb[0],),
    )
    grad_picked = call(times_back_body, [shaped(rows_small, depth_a)], [low_sc, shortcut_b])[0]
    high_sum = lax.psum_scatter(late_windows, "dp", scatter_dimension=0, tiled=False)
    low_sb, grad_rb, sums = call(
        with_images(shrink_back_body),
        [shaped(rows_small, middle_b, kind=low_type), shaped(rows_big, middle_b), shaped(2, middle_b)],
        [sums_sb, grads_sb, grad_sb, mixed_b, counts, scale_sb, mask_small, spatial_b9, sums_rb, reduced_b, slope_rb],
        scratch=[((16, middle_b), full_type)],
        after=(spill, grad_picked),
    )
    grads_rb = share(sums)
    low_rb, joined_grad, sums = call(
        with_images(join_back_body),
        [shaped(rows_big, middle_b, kind=low_type), shaped(rows_big, depth_a), shaped(2, depth_a)],
        [sums_rb, grads_rb, grad_rb, reduced_b, counts, scale_rb, mask_big, reduce_b, grad_picked, sums_ea, expanded_a, slope_ea],
        scratch=[((16, depth_a), full_type)],
    )
    grads_ea = share(sums)
    outs_low = call(
        functools.partial(middle_filters_body, share_b),
        windows(half, low_rows(window_b)),
        [block_a, low_rb, even_b, moved_b, low_sb, spill],
        scratch=[((end_low, lanes), full_type)],
        copies=8 * half,
        vmem=vmem_large,
        after=(grads_ea[0],),
    )
    low_ea, grad_sa, sums = call(
        functools.partial(expand_back_body, rows_step=4 * line),
        [shaped(rows_big, depth_a, kind=low_type), shaped(rows_big, middle_a), shaped(2, middle_a)],
        [sums_ea, grads_ea, joined_grad, expanded_a, counts, scale_ea, mask_big, expand_a, sums_sa, mixed_a, slope_sa],
        scratch=[((16, middle_a), full_type)],
        after=(outs_low[0],),
    )
    grads_sa = share(sums)
    far_one, far_two, near_one, near_two = pairs_of(outs_low)
    far_sum_one = far_one[0] + far_one[1]
    far_sum_two = far_two[0] + far_two[1]
    got_one, got_two = exchange(far_sum_one, "view", 1), exchange(far_sum_two, "view", 1)
    low_one = Windows(near_one + (got_one,), bits)
    low_two = Windows(near_two + (got_two,), bits)
    low_sa, grad_ra, sums = call(
        with_images(block_back_body),
        [shaped(rows_big, middle_a, kind=low_type), shaped(rows_big, middle_a), shaped(2, middle_a)],
        [sums_sa, grads_sa, grad_sa, mixed_a, counts, scale_sa, mask_big, spatial_a9, sums_ra, reduced_a, slope_ra],
        scratch=[
            ((height + 2, 2, line, middle_a), low_type),
            ((height + 2, 2, line, middle_a), low_type),
            ((16, middle_a), full_type),
        ],
        after=(far_sum_one, far_sum_two),
    )
    grads_ra = share(sums)
    ready, x_bit, z_bits = [], low_first[:1], low_first[1:]
    if bits:
        x_bit = x_bit[0]
        low_one.step(x_bit, *grads_ra[1:])
        ready = [low_one.sent]
    low_ra, input_grad = call(
        with_images(exit_body),
        [shaped(rows_big, middle_a, kind=low_type), shaped(height, pairs, 2, images, depth_a, kind=low_type)],
        [sums_ra, grads_ra, grad_ra, reduced_a, counts, scale_ra, mask_big, reduce_a, joined_grad],
        after=ready,
    )
    norm_rows_a = (4 * middle_a + 2 * depth_a) // lanes
    total_a = (depth_a * 2 + 9 * middle_a) * middle_a // lanes + norm_rows_a
    share_a = total_a * lanes // (2 * size)
    window_a = window_rows(share_a, lanes)
    end_a = window_start(2 * size - 1, share_a, lanes) + window_a
    later = call(
        block_filter_body,
        [shaped((total_a - norm_rows_a) - depth_a * middle_a // lanes, lanes)],
        [even_a, moved_a, low_sa, hidden_two_a, low_ea],
        after=(low_ra,),
    )[0]
    outs = call(
        functools.partial(early_filters_body, share_a),
        windows(size, [window_a]),
        [start, low_ra, later],
        scratch=[((end_a, lanes), full_type)],
        copies=2 * size,
        vmem=2 * vmem_small,
        after=(got_two,) + ((low_one.received,) if bits else ()),
    )
    early = Windows(pairs_of(outs)[0], [("view", 0)] + bits)
    early.step(("view", 0))
    early_got = early.received
    if bits:
        for item in z_bits[:1]:
            low_one.step(item)
        low_two.step(x_bit, early.sent)
        for item in z_bits[1:]:
            low_one.step(item)
        early.step(x_bit)
        for item in z_bits:
            low_two.step(item)
        for item in z_bits:
            early.step(item)
    all_grads = [sum(parts[1:], parts[0]) for parts in (grads_rb, grads_sb, grads_eb, grads_ra, grads_sa, grads_ea)]
    norms = jnp.concatenate([value.reshape(-1, lanes) for value in all_grads], axis=0)
    norms = norms + exchange(norms + 0.0 * early_got[0, :1], "view", 1)
    packed_last = jnp.concatenate([low_one.total()[0], low_two.total()[0]], axis=0)
    high_got = lax.ppermute(high_sum, "view", [(0, 1)])
    low_last = lax.ppermute(packed_last, "view", [(1, 0)])
    cut = []
    for value in all_grads:
        rows = value.size // lanes
        cut.append(norms[:rows].reshape(value.shape))
        norms = norms[rows:]
    norms_b = [cut[0], cut[1], cut[2][:2], cut[2][0], cut[2][2]]
    norms_a = cut[3:]
    device = lax.axis_index("view") * size + lax.axis_index("dp")

    def norm_block(norms):
        values = jnp.concatenate([value.reshape(-1, lanes) for value in norms], axis=0)
        return jnp.where(device == 2 * size - 1, values, 0.0)

    def cut_out(window, share_size):
        begin = device * share_size - window_start(device, share_size, lanes) * lanes
        return lax.dynamic_slice(window.reshape(-1), (begin,), (share_size,))

    late_place = total_b - norm_rows_b - window_start(2 * size - 1, share_b, lanes)
    late_window = call(
        functools.partial(late_window_body, late_place),
        [shaped(window_b, lanes)],
        [high_sum, high_got, packed_last, low_last, norm_block(norms_b)],
        cost_us=0,
    )[0]
    early_place = total_a - norm_rows_a - window_start(2 * size - 1, share_a, lanes)
    early_window = call(
        functools.partial(early_window_body, early_place),
        [shaped(window_a, lanes)],
        [early.total(), norm_block(norms_a)],
        cost_us=0,
    )[0]
    late_done, early_done = cut_out(late_window, share_b), cut_out(early_window, share_a)

    def natural(value):
        return value.reshape(height, height, images, depth_a).transpose(2, 0, 1, 3)[None]

    return (
        loss[:, 0][None],
        natural(block_out),
        block_b.transpose(2, 0, 1, 3)[None],
        natural(input_grad),
        early_done,
        late_done,
    )


def solution(mesh):
    copied = (P(),) * 21
    images = P("view", "dp", None, None, None)
    packed = P(("view", "dp"))
    return jax.shard_map(
        per_device,
        mesh=mesh,
        in_specs=(images, P("view", "dp")) + copied,
        out_specs=(P("view", "dp"), images, images, images, packed, packed),
        check_vma=False,
    )
```

```python
import functools

import jax
import jax.numpy as jnp
from jax import lax
from jax.experimental import pallas as pl
from jax.experimental.pallas import tpu as pltpu
from jax.sharding import PartitionSpec as P

eps_norm = 1e-05
eps_cos = 1e-06
loss_scale = 65536.0
low_type = jnp.bfloat16
full_type = jnp.float32
vmem_small, vmem_large = 6 * 1024 * 1024, 18 * 1024 * 1024
cost_small = 0.1

even_width = 8
spare_rows = 16


class View:
    def __init__(self, value, rows, columns):
        self.value, self.rows, self.columns = value, slice(*rows), slice(*columns)


def call(body, outs, args, cost_us=cost_small, scratch=(), copies=0, vmem=vmem_small, after=(), scalars=()):
    whole = pl.BlockSpec(memory_space=pltpu.VMEM)
    placed = [pl.BlockSpec(memory_space=pltpu.HBM) if copies and len(out.shape) == 3 else whole for out in outs]
    flat, places = [], {}

    def place(item):
        value = item.value if isinstance(item, View) else item
        if id(value) not in places:
            places[id(value)] = len(flat)
            flat.append(value)
        return places[id(value)]

    for item in args:
        for one in item if isinstance(item, tuple) else (item,):
            place(one)

    def run(*refs):
        def found(item):
            if isinstance(item, tuple):
                return tuple(found(one) for one in item)
            ref = refs[place(item)]
            return ref.at[item.rows, item.columns] if isinstance(item, View) else ref

        body(*[found(item) for item in args], *refs[len(flat) + len(after) :])

    return pl.pallas_call(
        run,
        out_shape=outs,
        in_specs=[pl.BlockSpec(memory_space=pltpu.SMEM) if i in scalars else whole for i in range(len(flat))]
        + [pl.BlockSpec(memory_space=pl.ANY)] * len(after),
        out_specs=placed,
        scratch_shapes=[pltpu.VMEM(dims, kind) for dims, kind in scratch]
        + ([pltpu.SemaphoreType.DMA((copies,))] if copies else []),
        compiler_params=pltpu.CompilerParams(vmem_limit_bytes=vmem),
        cost_estimate=pl.CostEstimate(flops=int(cost_us * 1e9), bytes_accessed=int(cost_us * 1e6), transcendentals=0),
    )(*flat, *after)


def shaped(*dims, kind=full_type):
    return jax.ShapeDtypeStruct(dims, kind)


def tail_parts(pre):
    size = jnp.abs(pre)
    base = 1.0 + (0.3275911 * 0.7071067811865476) * size
    guess = pl.reciprocal(base, approx=True)
    guess = guess * (2.0 - base * guess)
    guess = guess * (2.0 - base * guess)
    bell = jnp.exp(-0.5 * (pre * pre))
    series = 0.5 * 1.061405429
    for term in (-1.453152027, 1.421413741, -0.284496736, 0.254829592):
        series = series * guess + 0.5 * term
    return size, bell, series * guess * bell


def smooth(pre):
    size, _, tail = tail_parts(pre)
    return jnp.maximum(pre, 0.0) - size * tail


def smooth_slope(pre):
    _, bell, tail = tail_parts(pre)
    return jnp.where(pre >= 0.0, 1.0 - tail, tail) + 0.3989422804014327 * (pre * bell)


def wide(mask, width):
    return jnp.concatenate([mask] * (width // mask.shape[1]), axis=1)


def fold(value):
    rows, width = value.shape
    return jnp.sum(value.reshape(rows // 8, 8, width), axis=0)


def column_sum(value):
    return jnp.sum(value, axis=0, keepdims=True)


def total(parts):
    result = parts[0][...]
    for part in parts[1:]:
        result = result + part[...]
    return result


def statistics(sums, count):
    center = sums[0:1] / count
    inverse = lax.rsqrt(sums[1:2] / count - center * center + eps_norm)
    return center, inverse


def add_rows(store, row, value):
    store[row * 8 : row * 8 + 8, :] += fold(value)


def finish_rows(store, out_ref, rows):
    for row in range(rows):
        out_ref[row : row + 1, :] = column_sum(store[row * 8 : row * 8 + 8, :])


def times(lhs, rhs):
    return lax.dot_general(lhs, rhs, (((1,), (0,)), ((), ())), preferred_element_type=full_type)


def times_back(lhs, rhs):
    return lax.dot_general(lhs, rhs, (((1,), (1,)), ((), ())), preferred_element_type=full_type)


def times_rows(lhs, rhs):
    return lax.dot_general(lhs, rhs, (((0,), (0,)), ((), ())), preferred_element_type=full_type)


def low(value):
    return value.astype(low_type)


def inside(rows, sides, size_ref, unit):
    images = size_ref.shape[1]
    place = lax.broadcasted_iota(jnp.int32, (rows, 128), 0)
    image = place % images
    bound = jnp.zeros((rows, 128), jnp.int32)
    for index in range(images):
        bound = jnp.where(image == index, size_ref[0, index] // unit, bound)
    pair = place // images
    over = pair % even_width * sides + pair // even_width % sides
    down = pair // (even_width * sides)
    return jnp.where((over < bound) & (down < bound), 1.0, 0.0)


def enter_body(images, x_ref, size_ref, filter_ref, start_ref, out_ref, sums_ref, mask_ref, small_ref, pixel_ref, store):
    height, pairs = x_ref.shape[0], x_ref.shape[1]
    depth = x_ref.shape[4]
    line = even_width * images
    blank = jnp.zeros((even_width - pairs, images, depth), low_type)
    store[...] = jnp.zeros_like(store)
    mask_ref[...] = inside(mask_ref.shape[0], 2, size_ref, 16)
    small_ref[...] = inside(small_ref.shape[0], 1, size_ref, 32)
    for index in range(images):
        bound = (size_ref[0, index] // 32).astype(full_type)
        pixel_ref[index : index + 1, :] = 1.0 / jnp.full((1, 128), bound * bound)

    def step(index, carry):
        rows = pl.ds(pl.multiple_of(index * 4 * line, 4 * line), 4 * line)
        parts = []
        for row in range(2):
            for side in range(2):
                cells = jnp.concatenate([x_ref[index * 2 + row, :, side], blank], axis=0)
                parts.append(cells.reshape(line, depth))
        value = jnp.concatenate(parts, axis=0).astype(full_type) * wide(mask_ref[rows, :], depth)
        value = low(value)
        start_ref[rows, :] = value
        result = times(value, filter_ref[...])
        out_ref[rows, :] = result
        add_rows(store, 0, result)
        add_rows(store, 1, result * result)
        return carry

    lax.fori_loop(0, height // 2, step, 0)
    finish_rows(store, sums_ref, 2)
    sums_ref[2:3, :] = wide(column_sum(fold(mask_ref[...])), sums_ref.shape[1])
    sums_ref[3:4, :] = wide(column_sum(fold(small_ref[...])), sums_ref.shape[1])


def split_store(even_ref, moved_ref, place, value, line):
    even, odd = value[:line], value[line:]
    even_ref[place, 0] = low(even)
    even_ref[place, 1] = low(odd)
    moved_ref[place, 0] = low(pltpu.roll(even, line - line // even_width, 0))
    moved_ref[place, 1] = low(pltpu.roll(odd, line // even_width, 0))


def blank_border(*refs):
    for ref in refs:
        empty = jnp.zeros(ref.shape[1:], ref.dtype)
        ref[0] = empty
        ref[ref.shape[0] - 1] = empty


def tap_sources(even_ref, moved_ref):
    return (
        ((moved_ref, 1), (even_ref, 0), (even_ref, 1)),
        ((even_ref, 0), (even_ref, 1), (moved_ref, 0)),
    )


def block_body(images, parts, u_ref, scale_ref, shift_ref, mask_ref, filter_ref, even_ref, moved_ref, out_ref, sums_ref, count_ref, store):
    depth = filter_ref.shape[1]
    line = even_width * images
    height = even_ref.shape[0] - 2
    sums = total(parts)
    count_ref[...] = sums[2:4, 0:128]
    center, inverse = statistics(sums, sums[2:3, 0:1])
    factor = scale_ref[...] * inverse
    shift = shift_ref[...]
    blank_border(even_ref, moved_ref)
    store[...] = jnp.zeros_like(store)

    def first(index, carry):
        rows = pl.ds(pl.multiple_of(index * 2 * line, 2 * line), 2 * line)
        pre = (u_ref[rows, :] - center) * factor + shift
        value = smooth(pre) * wide(mask_ref[rows, :], depth)
        split_store(even_ref, moved_ref, index + 1, value, line)
        return carry

    lax.fori_loop(0, height, first, 0)
    half = height // 2
    sources = tap_sources(even_ref, moved_ref)
    for side in range(2):
        for part in range(2):
            lhs = jnp.concatenate(
                [
                    ref[half * part + row : half * part + row + half, plane].reshape(half * line, depth)
                    for row in range(3)
                    for ref, plane in sources[side]
                ],
                axis=1,
            )
            result = times(lhs, filter_ref[...])
            for index in range(half):
                begin = (half * part + index) * 2 * line + side * line
                piece = result[index * line : index * line + line]
                out_ref[begin : begin + line, :] = piece
                kept = piece * wide(mask_ref[begin : begin + line, :], piece.shape[1])
                add_rows(store, 0, kept)
                add_rows(store, 1, kept * piece)
    finish_rows(store, sums_ref, 2)


def expand_body(parts, u_ref, count_ref, scale_ref, shift_ref, mask_ref, filter_ref, hidden_ref, out_ref, sums_ref, store, which, rows_step):
    center, inverse = statistics(total(parts), count_ref[which : which + 1, 0:1])
    factor = scale_ref[...] * inverse
    shift = shift_ref[...]
    depth = u_ref.shape[1]
    store[...] = jnp.zeros_like(store)

    def step(index, carry):
        rows = pl.ds(pl.multiple_of(index * rows_step, rows_step), rows_step)
        pre = (u_ref[rows, :] - center) * factor + shift
        value = low(smooth(pre) * wide(mask_ref[rows, :], depth))
        hidden_ref[rows, :] = value
        result = times(value, filter_ref[...])
        out_ref[rows, :] = result
        add_rows(store, 0, result)
        add_rows(store, 1, result * result)
        return carry

    lax.fori_loop(0, u_ref.shape[0] // rows_step, step, 0)
    finish_rows(store, sums_ref, 2)


def join_body(images, parts, u_ref, count_ref, scale_ref, shift_ref, mask_ref, start_ref, reduce_ref, side_ref, block_ref, reduced_ref, picked_ref, sided_ref, sums_ref, side_sums_ref, store, side_store):
    center, inverse = statistics(total(parts), count_ref[0:1, 0:1])
    factor = scale_ref[...] * inverse
    shift = shift_ref[...]
    depth = u_ref.shape[1]
    line = even_width * images
    store[...] = jnp.zeros_like(store)
    side_store[...] = jnp.zeros_like(side_store)

    def step(index, carry):
        rows = pl.ds(pl.multiple_of(index * 4 * line, 4 * line), 4 * line)
        pre = (u_ref[rows, :] - center) * factor + shift + start_ref[rows, :].astype(full_type)
        value = low(smooth(pre) * wide(mask_ref[rows, :], depth))
        block_ref[rows, :] = value
        picked_ref[pl.ds(pl.multiple_of(index * line, line), line), :] = value[:line]
        result = times(value, reduce_ref[...])
        reduced_ref[rows, :] = result
        add_rows(store, 0, result)
        add_rows(store, 1, result * result)
        return carry

    lax.fori_loop(0, u_ref.shape[0] // (4 * line), step, 0)
    finish_rows(store, sums_ref, 2)
    width = 512

    def side(index, carry):
        columns = pl.ds(pl.multiple_of(index * width, width), width)
        result = times(picked_ref[...], side_ref[:, columns])
        sided_ref[:, columns] = result
        side_sums_ref[0:1, columns] = column_sum(fold(result))
        side_sums_ref[1:2, columns] = column_sum(fold(result * result))
        return carry

    lax.fori_loop(0, side_ref.shape[1] // width, side, 0)


def shrink_body(images, parts, u_ref, count_ref, scale_ref, shift_ref, mask_ref, small_ref, filter_ref, even_ref, moved_ref, out_ref, sums_ref):
    depth = u_ref.shape[1]
    line = even_width * images
    height = even_ref.shape[0] - 2
    center, inverse = statistics(total(parts), count_ref[0:1, 0:1])
    factor = scale_ref[...] * inverse
    shift = shift_ref[...]
    blank_border(even_ref, moved_ref)

    def first(index, carry):
        rows = pl.ds(pl.multiple_of(index * 2 * line, 2 * line), 2 * line)
        pre = (u_ref[rows, :] - center) * factor + shift
        value = smooth(pre) * wide(mask_ref[rows, :], depth)
        split_store(even_ref, moved_ref, index + 1, value, line)
        return carry

    lax.fori_loop(0, height, first, 0)
    half = height // 2
    result = None
    for row in range(3):
        lhs = jnp.concatenate(
            [
                jnp.concatenate([ref[2 * index + row, plane] for index in range(half)], axis=0)
                for ref, plane in ((moved_ref, 1), (even_ref, 0), (even_ref, 1))
            ],
            axis=1,
        )
        term = times(lhs, filter_ref[row * 3 * depth : row * 3 * depth + 3 * depth, :])
        result = term if result is None else result + term
    out_ref[...] = result
    kept = result * wide(small_ref[...], result.shape[1])
    sums_ref[0:1, :] = column_sum(fold(kept))
    sums_ref[1:2, :] = column_sum(fold(kept * result))


def leave_body(images, parts, side_parts, u_ref, side_ref, count_ref, scale_ref, shift_ref, side_scale_ref, side_shift_ref, small_ref, pixel_ref, block_ref, joined_ref, pooled_ref, store):
    center, inverse = statistics(total(parts), count_ref[1:2, 0:1])
    factor = scale_ref[...] * inverse
    side_center, side_inverse = statistics(total(side_parts), count_ref[1:2, 0:1])
    side_factor = side_scale_ref[...] * side_inverse
    shift = shift_ref[...] + side_shift_ref[...]
    depth = u_ref.shape[1]
    line = even_width * images
    pairs = block_ref.shape[1]
    store[...] = jnp.zeros_like(store)

    def step(index, carry):
        rows = pl.ds(pl.multiple_of(index * line, line), line)
        pre = (u_ref[rows, :] - center) * factor + (side_ref[rows, :] - side_center) * side_factor + shift
        joined_ref[rows, :] = pre
        value = smooth(pre) * wide(small_ref[rows, :], depth)
        block_ref[index] = low(value).reshape(even_width, images, depth)[:pairs]
        add_rows(store, 0, value)
        return carry

    lax.fori_loop(0, u_ref.shape[0] // line, step, 0)
    summed = store[0:images, :]
    for begin in range(images, 8, images):
        summed = summed + store[begin : begin + images, :]
    pooled_ref[...] = summed * pixel_ref[:, 0:1]


def gather_images(store, row, images):
    summed = store[row * 8 : row * 8 + images, :]
    for begin in range(images, 8, images):
        summed = summed + store[row * 8 + begin : row * 8 + begin + images, :]
    return summed


def slope_sums_body(images, parts, side_parts, joined_ref, u_ref, side_ref, count_ref, small_ref, slope_ref, plain_ref, unit_ref, side_unit_ref, store):
    center, inverse = statistics(total(parts), count_ref[1:2, 0:1])
    side_center, side_inverse = statistics(total(side_parts), count_ref[1:2, 0:1])
    depth = u_ref.shape[1]
    line = even_width * images
    store[...] = jnp.zeros_like(store)

    def step(index, carry):
        rows = pl.ds(pl.multiple_of(index * line, line), line)
        slope = smooth_slope(joined_ref[rows, :]) * wide(small_ref[rows, :], depth)
        slope_ref[rows, :] = slope
        add_rows(store, 0, slope)
        add_rows(store, 1, slope * (u_ref[rows, :] - center))
        add_rows(store, 2, slope * (side_ref[rows, :] - side_center))
        return carry

    lax.fori_loop(0, u_ref.shape[0] // line, step, 0)
    plain_ref[...] = gather_images(store, 0, images)
    unit_ref[...] = gather_images(store, 1, images) * inverse
    side_unit_ref[...] = gather_images(store, 2, images) * side_inverse


def compare_body(pooled_ref, partner_ref, pixel_ref, plain_ref, unit_ref, side_unit_ref, loss_ref, grad_ref, sums_ref):
    pooled, partner = pooled_ref[...], partner_ref[...]
    inverse_own = lax.rsqrt(jnp.sum(pooled * pooled, axis=1, keepdims=True) + eps_cos)
    unit_own = pooled * inverse_own
    unit_other = partner * lax.rsqrt(jnp.sum(partner * partner, axis=1, keepdims=True) + eps_cos)
    cosine = jnp.sum(unit_own * unit_other, axis=1, keepdims=True)
    loss_ref[...] = jnp.broadcast_to(-0.5 * cosine, loss_ref.shape)
    grad = (-0.5 * loss_scale) * inverse_own * (unit_other - cosine * unit_own) * pixel_ref[:, 0:1]
    grad_ref[...] = grad
    sums_ref[0:1, :] = column_sum(grad * plain_ref[...])
    sums_ref[1:2, :] = column_sum(grad * unit_ref[...])
    sums_ref[2:3, :] = column_sum(grad * side_unit_ref[...])


def norm_back(sums, totals, count, scale):
    center, inverse = statistics(sums, count)
    factor = scale * inverse
    return center, inverse, factor, -(factor * inverse * totals[1:2] / count), -(factor * totals[0:1] / count)


def leave_back_body(images, parts, side_parts, grads, slope_ref, grad_ref, u_ref, side_ref, count_ref, scale_ref, side_scale_ref, small_ref, filter_ref, inner_parts, inner_u_ref, inner_slope_ref, low_ref, side_low_ref, out_ref, sums_ref, store):
    totals = total(grads)
    count = count_ref[1:2, 0:1]
    center, _, factor, along, level = norm_back(total(parts), totals, count, scale_ref[...])
    side_totals = jnp.concatenate([totals[0:1], totals[2:3]], axis=0)
    side_center, _, side_factor, side_along, side_level = norm_back(total(side_parts), side_totals, count, side_scale_ref[...])
    depth = u_ref.shape[1]
    line = even_width * images
    grad = jnp.concatenate([grad_ref[...]] * (line // images), axis=0)

    def step(index, carry):
        rows = pl.ds(pl.multiple_of(index * line, line), line)
        mask = wide(small_ref[rows, :], depth)
        joined = slope_ref[rows, :] * grad
        low_ref[rows, :] = low((joined * factor + (u_ref[rows, :] - center) * along + level) * mask)
        side_low_ref[rows, :] = low((joined * side_factor + (side_ref[rows, :] - side_center) * side_along + side_level) * mask)
        return carry

    lax.fori_loop(0, u_ref.shape[0] // line, step, 0)
    inner_center, inner_inverse = statistics(total(inner_parts), count)
    result = times_back(low_ref[...], filter_ref[...]) * inner_slope_ref[...]
    out_ref[...] = result
    sums_ref[0:1, :] = column_sum(fold(result))
    sums_ref[1:2, :] = column_sum(fold(result * (inner_u_ref[...] - inner_center))) * inner_inverse


def shrink_back_body(images, parts, grads, g_ref, u_ref, count_ref, scale_ref, small_ref, filter_ref, inner_parts, inner_u_ref, inner_slope_ref, low_ref, out_ref, sums_ref, store):
    depth = u_ref.shape[1]
    inner = filter_ref.shape[2]
    line = even_width * images
    half = u_ref.shape[0] // line
    center, _, factor, along, level = norm_back(total(parts), total(grads), count_ref[1:2, 0:1], scale_ref[...])
    exact = (g_ref[...] * factor + (u_ref[...] - center) * along + level) * wide(small_ref[...], depth)
    here = low(exact)
    low_ref[...] = here
    right = low(pltpu.roll(exact, exact.shape[0] - images, 0))
    blank = jnp.zeros((line, depth), low_type)
    below = jnp.concatenate([here[line:], blank], axis=0)
    below_right = jnp.concatenate([right[line:], blank], axis=0)
    inner_center, inner_inverse = statistics(total(inner_parts), count_ref[0:1, 0:1])
    store[...] = jnp.zeros_like(store)
    for row in range(2):
        for side in range(2):
            terms = [(here, 1 + row, 1 + side)]
            if side:
                terms.append((right, 1 + row, 0))
            if row:
                terms.append((below, 0, 1 + side))
            if row and side:
                terms.append((below_right, 0, 0))
            lhs = jnp.concatenate([value for value, _, _ in terms], axis=1)
            rhs = jnp.concatenate([filter_ref[down * 3 + over] for _, down, over in terms], axis=1)
            result = times_back(lhs, rhs)
            for index in range(half):
                begin = (index * 4 + row * 2 + side) * line
                rows = slice(begin, begin + line)
                piece = result[index * line : index * line + line] * inner_slope_ref[rows, :]
                out_ref[rows, :] = piece
                add_rows(store, 0, piece)
                add_rows(store, 1, piece * (inner_u_ref[rows, :] - inner_center))
    sums_ref[0:1, :] = column_sum(store[0:8, :])
    sums_ref[1:2, :] = column_sum(store[8:16, :]) * inner_inverse


def join_back_body(images, parts, grads, g_ref, u_ref, count_ref, scale_ref, mask_ref, filter_ref, picked_ref, inner_parts, inner_u_ref, inner_slope_ref, low_ref, out_ref, sums_ref, store):
    depth = u_ref.shape[1]
    line = even_width * images
    center, _, factor, along, level = norm_back(total(parts), total(grads), count_ref[0:1, 0:1], scale_ref[...])
    inner_center, inner_inverse = statistics(total(inner_parts), count_ref[0:1, 0:1])
    store[...] = jnp.zeros_like(store)

    def step(index, carry):
        rows = pl.ds(pl.multiple_of(index * 4 * line, 4 * line), 4 * line)
        value = low((g_ref[rows, :] * factor + (u_ref[rows, :] - center) * along + level) * wide(mask_ref[rows, :], depth))
        low_ref[rows, :] = value
        result = times_back(value, filter_ref[...])
        extra = picked_ref[pl.ds(pl.multiple_of(index * line, line), line), :]
        result = jnp.concatenate([result[:line] + extra, result[line:]], axis=0) * inner_slope_ref[rows, :]
        out_ref[rows, :] = result
        add_rows(store, 0, result)
        add_rows(store, 1, result * (inner_u_ref[rows, :] - inner_center))
        return carry

    lax.fori_loop(0, u_ref.shape[0] // (4 * line), step, 0)
    sums_ref[0:1, :] = column_sum(store[0:8, :])
    sums_ref[1:2, :] = column_sum(store[8:16, :]) * inner_inverse


def expand_back_body(parts, grads, g_ref, u_ref, count_ref, scale_ref, mask_ref, filter_ref, inner_parts, inner_u_ref, inner_slope_ref, low_ref, out_ref, sums_ref, store, rows_step):
    depth = u_ref.shape[1]
    center, _, factor, along, level = norm_back(total(parts), total(grads), count_ref[0:1, 0:1], scale_ref[...])
    inner_center, inner_inverse = statistics(total(inner_parts), count_ref[0:1, 0:1])
    store[...] = jnp.zeros_like(store)

    def step(index, carry):
        rows = pl.ds(pl.multiple_of(index * rows_step, rows_step), rows_step)
        value = low((g_ref[rows, :] * factor + (u_ref[rows, :] - center) * along + level) * wide(mask_ref[rows, :], depth))
        low_ref[rows, :] = value
        result = times_back(value, filter_ref[...]) * inner_slope_ref[rows, :]
        out_ref[rows, :] = result
        add_rows(store, 0, result)
        add_rows(store, 1, result * (inner_u_ref[rows, :] - inner_center))
        return carry

    lax.fori_loop(0, u_ref.shape[0] // rows_step, step, 0)
    sums_ref[0:1, :] = column_sum(store[0:8, :])
    sums_ref[1:2, :] = column_sum(store[8:16, :]) * inner_inverse


def block_back_body(images, parts, grads, g_ref, u_ref, count_ref, scale_ref, mask_ref, filter_ref, inner_parts, inner_u_ref, inner_slope_ref, low_ref, out_ref, sums_ref, even_ref, moved_ref, store):
    depth = u_ref.shape[1]
    line = even_width * images
    height = even_ref.shape[0] - 2
    center, _, factor, along, level = norm_back(total(parts), total(grads), count_ref[0:1, 0:1], scale_ref[...])
    inner_center, inner_inverse = statistics(total(inner_parts), count_ref[0:1, 0:1])
    blank_border(even_ref, moved_ref)
    store[...] = jnp.zeros_like(store)

    def first(index, carry):
        rows = pl.ds(pl.multiple_of(index * 2 * line, 2 * line), 2 * line)
        value = (g_ref[rows, :] * factor + (u_ref[rows, :] - center) * along + level) * wide(mask_ref[rows, :], depth)
        low_ref[rows, :] = low(value)
        split_store(even_ref, moved_ref, index + 1, value, line)
        return carry

    lax.fori_loop(0, height, first, 0)
    half = height // 2
    sources = tap_sources(even_ref, moved_ref)
    rhs = jnp.concatenate([filter_ref[8 - tap] for tap in range(9)], axis=1)
    for side in range(2):
        for part in range(2):
            lhs = jnp.concatenate(
                [
                    ref[half * part + row : half * part + row + half, plane].reshape(half * line, depth)
                    for row in range(3)
                    for ref, plane in sources[side]
                ],
                axis=1,
            )
            result = times_back(lhs, rhs)
            for index in range(half):
                begin = (half * part + index) * 2 * line + side * line
                rows = slice(begin, begin + line)
                piece = result[index * line : index * line + line] * inner_slope_ref[rows, :]
                out_ref[rows, :] = piece
                add_rows(store, 0, piece)
                add_rows(store, 1, piece * (inner_u_ref[rows, :] - inner_center))
    sums_ref[0:1, :] = column_sum(store[0:8, :])
    sums_ref[1:2, :] = column_sum(store[8:16, :]) * inner_inverse


def exit_body(images, parts, grads, g_ref, u_ref, count_ref, scale_ref, mask_ref, filter_ref, joined_ref, low_ref, out_ref):
    depth = u_ref.shape[1]
    pairs = out_ref.shape[1]
    line = even_width * images
    center, _, factor, along, level = norm_back(total(parts), total(grads), count_ref[0:1, 0:1], scale_ref[...])

    def step(index, carry):
        rows = pl.ds(pl.multiple_of(index * 4 * line, 4 * line), 4 * line)
        mask = mask_ref[rows, :]
        value = low((g_ref[rows, :] * factor + (u_ref[rows, :] - center) * along + level) * wide(mask, depth))
        low_ref[rows, :] = value
        result = low((times_back(value, filter_ref[...]) + joined_ref[rows, :]) * wide(mask, joined_ref.shape[1]))
        for row in range(2):
            for side in range(2):
                begin = (row * 2 + side) * line
                cells = result[begin : begin + line].reshape(even_width, images, result.shape[1])
                out_ref[index * 2 + row, :, side] = cells[:pairs]
        return carry

    lax.fori_loop(0, u_ref.shape[0] // (4 * line), step, 0)


def natural_body(images, value_ref, out_ref):
    pairs = out_ref.shape[1]
    line = even_width * images
    depth = value_ref.shape[1]

    def step(index, carry):
        for side in range(2):
            rows = pl.ds(pl.multiple_of(index * 2 * line + side * line, line), line)
            out_ref[index, :, side] = value_ref[rows, :].reshape(even_width, images, depth)[:pairs]
        return carry

    lax.fori_loop(0, out_ref.shape[0], step, 0)


def slope_body(parts, u_ref, count_ref, scale_ref, shift_ref, mask_ref, extras, out_ref, which, rows_step):
    center, inverse = statistics(total(parts), count_ref[which : which + 1, 0:1])
    factor = scale_ref[...] * inverse
    shift = shift_ref[...]
    depth = u_ref.shape[1]

    def step(index, carry):
        rows = pl.ds(pl.multiple_of(index * rows_step, rows_step), rows_step)
        pre = (u_ref[rows, :] - center) * factor + shift
        for extra_ref in extras:
            pre = pre + extra_ref[rows, :].astype(full_type)
        out_ref[rows, :] = low(smooth_slope(pre) * wide(mask_ref[rows, :], depth))
        return carry

    lax.fori_loop(0, u_ref.shape[0] // rows_step, step, 0)


def times_back_body(value_ref, filter_ref, out_ref):
    out_ref[...] = times_back(value_ref[...], filter_ref[...])


def window_start(device, share_size, width):
    return (device * share_size) // (8 * width) * 8


def window_rows(share_size, width):
    return -(-(share_size + 8 * width) // (16 * width)) * 16


def low_rows(rows):
    first = rows // 32 * 8
    return [first, rows // 2 - first] * 2


class AllCopies:
    def __init__(self, source, out, sems, first_device, first_row, share_size):
        self.waiting, self.started = [], []
        owners, rows, width = out.shape
        for owner in range(owners):
            begin = window_start(first_device + owner, share_size, width) - first_row
            copy = pltpu.make_async_copy(source.at[pl.ds(begin, rows)], out.at[owner], sems.at[owner])
            self.waiting.append((begin + rows, copy))

    def start(self, filled):
        for end, copy in self.waiting:
            if end <= filled:
                copy.start()
                self.started.append(copy)
        self.waiting = [item for item in self.waiting if item[0] > filled]

    def finish(self, filled):
        self.start(filled)
        for copy in self.started:
            copy.wait()


class Copies:
    def __init__(self, source, outs, sems, first_device, first_row, share_size, offsets):
        self.waiting, self.started = [], []
        owners, _, width = outs[0].shape
        pieces = len(offsets)
        core = lax.axis_index("dp") % 2
        for owner in range(owners):
            device = first_device + 2 * owner
            end = window_start(device + 1, share_size, width) + window_rows(share_size, width) - first_row
            for piece in range(pieces):
                for which, chosen in enumerate((1 - core, core)):
                    out = outs[which * pieces + piece]
                    begin = window_start(device + chosen, share_size, width) - first_row + offsets[piece]
                    rows = pl.ds(pl.multiple_of(begin, 8), out.shape[1])
                    sem = sems.at[(owner * pieces + piece) * 2 + which]
                    self.waiting.append((end, pltpu.make_async_copy(source.at[rows], out.at[owner], sem)))

    def start(self, filled):
        for end, copy in self.waiting:
            if end <= filled:
                copy.start()
                self.started.append(copy)
        self.waiting = [item for item in self.waiting if item[0] > filled]

    def finish(self, filled):
        self.start(filled)
        for copy in self.started:
            copy.wait()


def put_filter(store, begin, value, grad, copies=None):
    step, across = 256, min(512, grad.shape[1])
    lanes = store.shape[1]
    cuts = grad.shape[1] // lanes
    for row in range(0, value.shape[1], step):
        for column in range(0, grad.shape[1], across):
            result = times_rows(value[:, row : row + step], grad[:, column : column + across])
            for cut in range(across // lanes):
                place = begin + row * cuts + column // lanes + cut
                store[pl.ds(place, step, stride=cuts), :] = result[:, cut * lanes : cut * lanes + lanes]
        if copies is not None:
            copies.start(begin + (row + step) * cuts)
    return begin + value.shape[1] * cuts


def late_filters_body(first_device, first_row, share_size, hidden_ref, picked_ref, low_ref, side_low_ref, out_ref, spill_ref, store, sems):
    copies = AllCopies(store, out_ref, sems, first_device, first_row, share_size)
    filled = hidden_ref.shape[1] * low_ref.shape[1] // 128 + picked_ref.shape[1] * side_low_ref.shape[1] // 128
    store[filled:, :] = jnp.zeros((store.shape[0] - filled, store.shape[1]), full_type)
    filled = put_filter(store, 0, hidden_ref, low_ref, copies)
    spill_ref[...] = store[: spill_ref.shape[0], :]
    put_filter(store, filled, picked_ref, side_low_ref, copies)
    copies.finish(store.shape[0])


def middle_filters_body(share_size, block_ref, low_ref, even_ref, moved_ref, inner_low_ref, spill_ref, *rest):
    *outs, store, sems = rest
    view = lax.axis_index("view")
    first, half = outs[0].shape[1], outs[0].shape[1] + outs[1].shape[1]
    far, near = (1 - view) * half, view * half
    copies = Copies(store, outs, sems, 0, 0, share_size, (far, far + first, near, near + first))
    store[store.shape[0] - spill_ref.shape[0] :, :] = spill_ref[...]
    filled = put_filter(store, 0, block_ref, low_ref, copies)
    half = even_ref.shape[0] // 2 - 1
    for row in range(3):
        for ref, plane in ((moved_ref, 1), (even_ref, 0), (even_ref, 1)):
            lhs = jnp.concatenate([ref[2 * index + row, plane] for index in range(half)], axis=0)
            filled = put_filter(store, filled, lhs, inner_low_ref, copies)
    copies.finish(store.shape[0])


def block_filter_body(even_ref, moved_ref, inner_low_ref, hidden_ref, outer_low_ref, out_ref):
    height, _, line, inner = even_ref.shape
    height = height - 2
    width = inner_low_ref.shape[1]
    grad = inner_low_ref[...].reshape(height, 2, line, width)
    grad = jnp.concatenate([grad[:, side].reshape(height * line, width) for side in range(2)], axis=0)
    sources = tap_sources(even_ref, moved_ref)
    filled = 0
    for row in range(3):
        for over in range(3):
            lhs = jnp.concatenate(
                [
                    sources[side][over][0][row : row + height, sources[side][over][1]].reshape(height * line, inner)
                    for side in range(2)
                ],
                axis=0,
            )
            filled = put_filter(out_ref, filled, lhs, grad)
    put_filter(out_ref, filled, hidden_ref, outer_low_ref)


def early_filters_body(share_size, start_ref, low_ref, later_ref, *rest):
    *outs, store, sems = rest
    copies = Copies(store, outs, sems, 0, 0, share_size, (0,))
    filled = put_filter(store, 0, start_ref, low_ref)
    later = later_ref.shape[0] - spare_rows
    store[filled : filled + later, :] = later_ref[:later, :]
    filled += later
    store[filled:, :] = jnp.zeros((store.shape[0] - filled, store.shape[1]), full_type)
    copies.finish(store.shape[0])


def late_window_body(place, high_ref, high_got_ref, low_ref, low_got_ref, norms_ref, out_ref):
    view = lax.axis_index("view")
    half = low_ref.shape[0]

    @pl.when(view == 0)
    def _():
        out_ref[:half, :] = low_ref[...]
        out_ref[half:, :] = low_got_ref[...]

    @pl.when(view == 1)
    def _():
        out_ref[...] = high_ref[...] + high_got_ref[...]

    rows = pl.ds(place, norms_ref.shape[0])
    out_ref[rows, :] += norms_ref[...]


def early_window_body(place, refs, norms_ref, out_ref):
    out_ref[...] = add_terms(refs)
    rows = pl.ds(place, norms_ref.shape[0])
    out_ref[rows, :] += norms_ref[...]


def exchange(value, axis, bits):
    return lax.ppermute(value, axis, [(i, i ^ bits) for i in range(lax.axis_size(axis))])


def share(sums):
    size = lax.axis_size("dp")
    if size > 1:
        sums = sums + exchange(sums, "dp", 1)
    if size > 2:
        sums = sums + exchange(sums, "dp", 3)
    parts = (sums,)
    bit = 4
    while bit < size:
        if len(parts) > 1:
            parts = (sum(parts[1:], parts[0]),)
        steps = [bit + 1, 2 * bit + 1, 3 * bit + 1] if 2 * bit < size else [bit + 1]
        parts = parts + tuple(exchange(parts[0], "dp", step) for step in steps)
        bit *= 4
    return parts


def add_terms(refs):
    result = refs[0][...]
    for ref in refs[1:]:
        result = result + ref[...]
    return result


def gate(value):
    corner = value[(slice(0, 1),) * (value.ndim - 1) + (slice(0, 128),)]
    return 0.0 * corner.reshape(1, 1, 128)


class Term:
    def __init__(self, value, bits):
        self.value, self.bits, self.chosen = value, list(bits), {}

    def part(self, chosen):
        rows, width = self.value.shape[1:]
        cut = self.value.reshape((2,) * len(self.bits) + (rows, width))
        starts = [chosen.get(item, 0) for item in self.bits] + [0, 0]
        sizes = [1 if item in chosen else 2 for item in self.bits] + [rows, width]
        return lax.dynamic_slice(cut, starts, sizes).reshape(-1, rows, width)


class Windows:
    def __init__(self, terms, bits):
        self.terms, self.bits, self.chosen = [Term(value, bits) for value in terms], list(bits), {}

    def step(self, item, *after):
        axis, bit = item
        own = (lax.axis_index(axis) >> bit) & 1
        chosen = dict(self.chosen)
        chosen[item] = 1 - own
        self.sent = sum([term.part(chosen) for term in self.terms[1:]], self.terms[0].part(chosen))
        if after:
            self.sent = self.sent + sum(gate(value) for value in after)
        self.received = exchange(self.sent, axis, 1 << bit)
        self.chosen[item] = own
        self.bits.remove(item)
        self.terms.append(Term(self.received, self.bits))

    def total(self):
        return (sum([term.part(self.chosen)[0] for term in self.terms[1:]], self.terms[0].part(self.chosen)[0]),)


def per_device(
    inputs,
    resolution,
    reduce_a,
    spatial_a,
    expand_a,
    reduce_b,
    spatial_b,
    expand_b,
    shortcut_b,
    scale_reduce_a,
    shift_reduce_a,
    scale_spatial_a,
    shift_spatial_a,
    scale_expand_a,
    shift_expand_a,
    scale_reduce_b,
    shift_reduce_b,
    scale_spatial_b,
    shift_spatial_b,
    scale_expand_b,
    shift_expand_b,
    scale_shortcut,
    shift_shortcut,
):
    images, height, depth_a = inputs.shape[1], inputs.shape[2], inputs.shape[4]
    pairs = height // 2
    middle_a, middle_b, depth_b = reduce_a.shape[1], reduce_b.shape[1], shortcut_b.shape[1]
    line = even_width * images
    rows_big, rows_small = height * 2 * line, pairs * line
    spatial_a9 = spatial_a.reshape(9, middle_a, middle_a)
    spatial_b9 = spatial_b.reshape(9, middle_b, middle_b)
    cells = inputs[0].transpose(1, 2, 0, 3).reshape(height, pairs, 2, images, depth_a)

    vectors = [
        (scale_reduce_a, shift_reduce_a),
        (scale_spatial_a, shift_spatial_a),
        (scale_expand_a, shift_expand_a),
        (scale_reduce_b, shift_reduce_b),
        (scale_spatial_b, shift_spatial_b),
        (scale_expand_b, shift_expand_b),
        (scale_shortcut, shift_shortcut),
    ]
    packed = jnp.stack([jnp.pad(vector, (0, depth_b - vector.size)) for pair in vectors for vector in pair])

    def affine(index):
        width = vectors[index][0].size
        return tuple(View(packed, (row, row + 1), (0, width)) for row in (2 * index, 2 * index + 1))

    def padded(width):
        return shaped(height + 2, 2, line, width, kind=low_type)

    def with_images(body):
        return functools.partial(body, images)

    start, reduced_a, sums, mask_big, mask_small, pixel = call(
        with_images(enter_body),
        [
            shaped(rows_big, depth_a, kind=low_type),
            shaped(rows_big, middle_a),
            shaped(4, middle_a),
            shaped(rows_big, 128),
            shaped(rows_small, 128),
            shaped(images, 128),
        ],
        [cells, resolution, reduce_a],
        scratch=[((16, middle_a), full_type)],
        scalars=(1,),
    )
    sums_ra = share(sums)
    scale_ra, shift_ra = affine(0)
    even_a, moved_a, mixed_a, sums, counts = call(
        with_images(block_body),
        [padded(middle_a), padded(middle_a), shaped(rows_big, middle_a), shaped(2, middle_a), shaped(2, 128)],
        [sums_ra, reduced_a, scale_ra, shift_ra, mask_big, spatial_a.reshape(9 * middle_a, middle_a)],
        scratch=[((16, middle_a), full_type)],
    )
    def slope(parts, value, scale, shift, mask, extras, which, rows_step):
        return call(
            functools.partial(slope_body, which=which, rows_step=rows_step),
            [shaped(*value.shape, kind=low_type)],
            [parts, value, counts, scale, shift, mask, extras],
        )[0]

    slope_ra = slope(sums_ra, reduced_a, scale_ra, shift_ra, mask_big, (), 0, 2 * line)
    sums_sa = share(sums)
    scale_sa, shift_sa = affine(1)
    hidden_two_a, expanded_a, sums = call(
        functools.partial(expand_body, which=0, rows_step=4 * line),
        [shaped(rows_big, middle_a, kind=low_type), shaped(rows_big, depth_a), shaped(2, depth_a)],
        [sums_sa, mixed_a, counts, scale_sa, shift_sa, mask_big, expand_a],
        scratch=[((16, depth_a), full_type)],
        after=(slope_ra,),
    )
    slope_sa = slope(sums_sa, mixed_a, scale_sa, shift_sa, mask_big, (), 0, 2 * line)
    sums_ea = share(sums)
    scale_ea, shift_ea = affine(2)
    block_a, reduced_b, picked, side_b, sums, side_sums = call(
        with_images(join_body),
        [
            shaped(rows_big, depth_a, kind=low_type),
            shaped(rows_big, middle_b),
            shaped(rows_small, depth_a, kind=low_type),
            shaped(rows_small, depth_b),
            shaped(2, middle_b),
            shaped(2, depth_b),
        ],
        [sums_ea, expanded_a, counts, scale_ea, shift_ea, mask_big, start, reduce_b, shortcut_b],
        scratch=[((16, middle_b), full_type), ((16, 128), full_type)],
        after=(slope_sa,),
    )
    slope_ea = slope(sums_ea, expanded_a, scale_ea, shift_ea, mask_big, (start,), 0, 2 * line)
    shared = share(jnp.concatenate([sums, side_sums], axis=1))
    sums_rb = tuple(View(part, (0, 2), (0, middle_b)) for part in shared)
    sums_sc = tuple(View(part, (0, 2), (middle_b, middle_b + depth_b)) for part in shared)
    scale_rb, shift_rb = affine(3)
    scale_sc, shift_sc = affine(6)
    even_b, moved_b, mixed_b, sums = call(
        with_images(shrink_body),
        [padded(middle_b), padded(middle_b), shaped(rows_small, middle_b), shaped(2, middle_b)],
        [sums_rb, reduced_b, counts, scale_rb, shift_rb, mask_big, mask_small, spatial_b.reshape(9 * middle_b, middle_b)],
        after=(slope_ea,),
    )
    block_out = call(
        with_images(natural_body), [shaped(height, pairs, 2, images, depth_a, kind=low_type)], [block_a]
    )[0]
    slope_rb = slope(sums_rb, reduced_b, scale_rb, shift_rb, mask_big, (), 0, 2 * line)
    sums_sb = share(sums)
    scale_sb, shift_sb = affine(4)
    hidden_two_b, expanded_b, sums = call(
        functools.partial(expand_body, which=1, rows_step=line),
        [shaped(rows_small, middle_b, kind=low_type), shaped(rows_small, depth_b), shaped(2, depth_b)],
        [sums_sb, mixed_b, counts, scale_sb, shift_sb, mask_small, expand_b],
        scratch=[((16, depth_b), full_type)],
        after=(slope_rb, block_out),
    )
    slope_sb = slope(sums_sb, mixed_b, scale_sb, shift_sb, mask_small, (), 1, line)
    sums_eb = share(sums)
    scale_eb, shift_eb = affine(5)
    block_b, joined_b, pooled = call(
        with_images(leave_body),
        [shaped(pairs, pairs, images, depth_b, kind=low_type), shaped(rows_small, depth_b), shaped(images, depth_b)],
        [sums_eb, sums_sc, expanded_b, side_b, counts, scale_eb, shift_eb, scale_sc, shift_sc, mask_small, pixel],
        scratch=[((8, depth_b), full_type)],
        after=(slope_sb,),
    )
    partner = exchange(pooled, "view", 1)
    slope_b, plain, unit, side_unit = call(
        with_images(slope_sums_body),
        [shaped(rows_small, depth_b)] + [shaped(images, depth_b)] * 3,
        [sums_eb, sums_sc, joined_b, expanded_b, side_b, counts, mask_small],
        scratch=[((24, depth_b), full_type)],
    )
    loss, grad_out, sums = call(
        compare_body,
        [shaped(images, 128), shaped(images, depth_b), shaped(3, depth_b)],
        [pooled, partner, pixel, plain, unit, side_unit],
    )
    grads_eb = share(sums)

    size = lax.axis_size("dp")
    half = size // 2
    bits = [("dp", bit) for bit in range(size.bit_length() - 2, 0, -1)]
    low_first = sorted(bits, key=lambda item: item[1])
    high_first = low_first[1:] + low_first[:1]
    lanes = 128
    first_rows = (depth_a + 9 * middle_b) * middle_b // lanes
    norm_rows_b = (4 * middle_b + 4 * depth_b) // lanes
    total_b = first_rows + (middle_b + depth_a) * depth_b // lanes + norm_rows_b
    share_b = total_b * lanes // (2 * size)
    window_b = window_rows(share_b, lanes)
    end_low = window_start(size - 1, share_b, lanes) + window_b
    end_high = window_start(2 * size - 1, share_b, lanes) + window_b

    def windows(count, pieces):
        return [pltpu.HBM((count, piece, lanes), full_type) for piece in pieces] * 2

    def pairs_of(outs):
        count = len(outs) // 2
        return [(kept, exchange(send, "dp", 1)) for send, kept in zip(outs[:count], outs[count:])]

    low_eb, low_sc, grad_sb, sums = call(
        with_images(leave_back_body),
        [
            shaped(rows_small, depth_b, kind=low_type),
            shaped(rows_small, depth_b, kind=low_type),
            shaped(rows_small, middle_b),
            shaped(2, middle_b),
        ],
        [
            sums_eb,
            sums_sc,
            grads_eb,
            slope_b,
            grad_out,
            expanded_b,
            side_b,
            counts,
            scale_eb,
            scale_sc,
            mask_small,
            expand_b,
            sums_sb,
            mixed_b,
            slope_sb,
        ],
        scratch=[((8, 128), full_type)],
    )
    grads_sb = share(sums)
    late_windows, spill = call(
        functools.partial(late_filters_body, size, first_rows, share_b),
        [pltpu.HBM((size, window_b, lanes), full_type), shaped(end_low - first_rows, lanes)],
        [hidden_two_b, picked, low_eb, low_sc],
        scratch=[((end_high - first_rows, lanes), full_type)],
        copies=size,
        vmem=vmem_large,
        after=(grads_sb[0],),
    )
    grad_picked = call(times_back_body, [shaped(rows_small, depth_a)], [low_sc, shortcut_b])[0]
    high_sum = lax.psum_scatter(late_windows, "dp", scatter_dimension=0, tiled=False)
    low_sb, grad_rb, sums = call(
        with_images(shrink_back_body),
        [shaped(rows_small, middle_b, kind=low_type), shaped(rows_big, middle_b), shaped(2, middle_b)],
        [sums_sb, grads_sb, grad_sb, mixed_b, counts, scale_sb, mask_small, spatial_b9, sums_rb, reduced_b, slope_rb],
        scratch=[((16, middle_b), full_type)],
        after=(spill, grad_picked),
    )
    grads_rb = share(sums)
    low_rb, joined_grad, sums = call(
        with_images(join_back_body),
        [shaped(rows_big, middle_b, kind=low_type), shaped(rows_big, depth_a), shaped(2, depth_a)],
        [sums_rb, grads_rb, grad_rb, reduced_b, counts, scale_rb, mask_big, reduce_b, grad_picked, sums_ea, expanded_a, slope_ea],
        scratch=[((16, depth_a), full_type)],
    )
    grads_ea = share(sums)
    outs_low = call(
        functools.partial(middle_filters_body, share_b),
        windows(half, low_rows(window_b)),
        [block_a, low_rb, even_b, moved_b, low_sb, spill],
        scratch=[((end_low, lanes), full_type)],
        copies=8 * half,
        vmem=vmem_large,
        after=(grads_ea[0],),
    )
    low_ea, grad_sa, sums = call(
        functools.partial(expand_back_body, rows_step=4 * line),
        [shaped(rows_big, depth_a, kind=low_type), shaped(rows_big, middle_a), shaped(2, middle_a)],
        [sums_ea, grads_ea, joined_grad, expanded_a, counts, scale_ea, mask_big, expand_a, sums_sa, mixed_a, slope_sa],
        scratch=[((16, middle_a), full_type)],
        after=(outs_low[0],),
    )
    grads_sa = share(sums)
    far_one, far_two, near_one, near_two = pairs_of(outs_low)
    far_sum_one = far_one[0] + far_one[1]
    far_sum_two = far_two[0] + far_two[1]
    got_one, got_two = exchange(far_sum_one, "view", 1), exchange(far_sum_two, "view", 1)
    low_one = Windows(near_one + (got_one,), bits)
    low_two = Windows(near_two + (got_two,), bits)
    low_sa, grad_ra, sums = call(
        with_images(block_back_body),
        [shaped(rows_big, middle_a, kind=low_type), shaped(rows_big, middle_a), shaped(2, middle_a)],
        [sums_sa, grads_sa, grad_sa, mixed_a, counts, scale_sa, mask_big, spatial_a9, sums_ra, reduced_a, slope_ra],
        scratch=[
            ((height + 2, 2, line, middle_a), low_type),
            ((height + 2, 2, line, middle_a), low_type),
            ((16, middle_a), full_type),
        ],
        after=(far_sum_one, far_sum_two),
    )
    grads_ra = share(sums)
    ready, x_bit, z_bits = [], low_first[:1], low_first[1:]
    if bits:
        x_bit = x_bit[0]
        low_one.step(x_bit, *grads_ra[1:])
        ready = [low_one.sent]
    low_ra, input_grad = call(
        with_images(exit_body),
        [shaped(rows_big, middle_a, kind=low_type), shaped(height, pairs, 2, images, depth_a, kind=low_type)],
        [sums_ra, grads_ra, grad_ra, reduced_a, counts, scale_ra, mask_big, reduce_a, joined_grad],
        after=ready,
    )
    norm_rows_a = (4 * middle_a + 2 * depth_a) // lanes
    total_a = (depth_a * 2 + 9 * middle_a) * middle_a // lanes + norm_rows_a
    share_a = total_a * lanes // (2 * size)
    window_a = window_rows(share_a, lanes)
    end_a = window_start(2 * size - 1, share_a, lanes) + window_a
    later = call(
        block_filter_body,
        [shaped(total_a - norm_rows_a - depth_a * middle_a // lanes + spare_rows, lanes)],
        [even_a, moved_a, low_sa, hidden_two_a, low_ea],
        after=(low_ra,),
    )[0]
    outs = call(
        functools.partial(early_filters_body, share_a),
        windows(size, [window_a]),
        [start, low_ra, later],
        scratch=[((end_a, lanes), full_type)],
        copies=2 * size,
        vmem=2 * vmem_small,
        after=(got_two,) + ((low_one.received,) if bits else ()),
    )
    early = Windows(pairs_of(outs)[0], [("view", 0)] + bits)
    early.step(("view", 0))
    early_got = early.received
    if bits:
        for item in z_bits[:1]:
            low_one.step(item)
        low_two.step(x_bit, early.sent)
        for item in z_bits[1:]:
            low_one.step(item)
        early.step(x_bit)
        for item in z_bits:
            low_two.step(item)
        for item in z_bits:
            early.step(item)
    all_grads = [sum(parts[1:], parts[0]) for parts in (grads_rb, grads_sb, grads_eb, grads_ra, grads_sa, grads_ea)]
    norms = jnp.concatenate([value.reshape(-1, lanes) for value in all_grads], axis=0)
    norms = norms + exchange(norms + 0.0 * early_got[0, :1], "view", 1)
    packed_last = jnp.concatenate([low_one.total()[0], low_two.total()[0]], axis=0)
    high_got = lax.ppermute(high_sum, "view", [(0, 1)])
    low_last = lax.ppermute(packed_last, "view", [(1, 0)])
    cut = []
    for value in all_grads:
        rows = value.size // lanes
        cut.append(norms[:rows].reshape(value.shape))
        norms = norms[rows:]
    norms_b = [cut[0], cut[1], cut[2][:2], cut[2][0], cut[2][2]]
    norms_a = cut[3:]
    device = lax.axis_index("view") * size + lax.axis_index("dp")

    def norm_block(norms):
        values = jnp.concatenate([value.reshape(-1, lanes) for value in norms], axis=0)
        return jnp.where(device == 2 * size - 1, values, 0.0)

    def cut_out(window, share_size):
        begin = device * share_size - window_start(device, share_size, lanes) * lanes
        return lax.dynamic_slice(window.reshape(-1), (begin,), (share_size,))

    late_place = total_b - norm_rows_b - window_start(2 * size - 1, share_b, lanes)
    late_window = call(
        functools.partial(late_window_body, late_place),
        [shaped(window_b, lanes)],
        [high_sum, high_got, packed_last, low_last, norm_block(norms_b)],
        cost_us=0,
    )[0]
    early_place = total_a - norm_rows_a - window_start(2 * size - 1, share_a, lanes)
    early_window = call(
        functools.partial(early_window_body, early_place),
        [shaped(window_a, lanes)],
        [early.total(), norm_block(norms_a)],
        cost_us=0,
    )[0]
    late_done, early_done = cut_out(late_window, share_b), cut_out(early_window, share_a)

    def natural(value):
        return value.reshape(height, height, images, depth_a).transpose(2, 0, 1, 3)[None]

    return (
        loss[:, 0][None],
        natural(block_out),
        block_b.transpose(2, 0, 1, 3)[None],
        natural(input_grad),
        early_done,
        late_done,
    )


def solution(mesh):
    copied = (P(),) * 21
    images = P("view", "dp", None, None, None)
    packed = P(("view", "dp"))
    return jax.shard_map(
        per_device,
        mesh=mesh,
        in_specs=(images, P("view", "dp")) + copied,
        out_specs=(P("view", "dp"), images, images, images, packed, packed),
        check_vma=False,
    )
```
